32 devices in a mesh: member: 2 (over x), lon: 16 (over z, y, core).
Axes of the slice: x: 2, y: 2, z: 4, core: 2. Of those that a mesh axis runs over, the one named last changes fastest.
Arguments:
- surface_old: float32 [1024, 256], P(('member', 'lon')), parts along dimension 0, may hold values from -6 to 6
- surface_forcing: float32 [1024, 256], P(('member', 'lon')), parts along dimension 0, may hold values from -13 to 13
- surface_coeff: float32 [512, 256], P('lon'), may hold values from 0.1 to 1
- ocean_mask: int32 [512, 256], P('lon'), may hold values from 0 to 1, as said below
- column_depth: int32 [256, 512], P('lon'), may hold values from 0 to 16, as said below
- east_depth: int32 [256, 512], P('lon'), may hold values from 0 to 16, as said below
- tracers: float32 [16, 16, 256, 512], P('member', None, 'lon'), parts along dimension 0, may hold values from 0.05 to 2
- u_clinic: float32 [32, 256, 512], P('member', 'lon'), parts along dimension 0, may hold values from -0.9 to 0.9
- v_clinic: float32 [32, 256, 512], P('member', 'lon'), parts along dimension 0, may hold values from -0.9 to 0.9
Outputs:
- surface: float32 [1024, 256], P(('member', 'lon')), parts along dimension 0
- tracers_new: float32 [16, 16, 256, 512], P('member', None, 'lon'), parts along dimension 0
The draws below stay inside these ranges and needn't reach their ends.
There are 2 independent parts, one for each index of `member`. The reference program is written for one: setup_inputs(seed, part) draws one part's arguments, and reference() takes and returns one part's arrays. A program takes and returns all parts, laid end to end along the dimension named above; an argument that names none is the same for every part. Nothing has to cross between parts.
Inputs may be any that keep to these rules, and one draw needn't show every extreme that they name: ocean_mask[j, i] is 1 exactly where column_depth[i, j] is positive, else 0. `column_depth`: 0 marks land. east_depth[i, j] is the smaller of column_depth[i, j] and column_depth[i + 1, j], longitudes periodic.
All inputs are finite; a program needn't handle non-finite values.
Results may differ from the reference program's by a relative error of at most 0.0003.
Values sent between devices are 32-bit elements; how exact they have to be, the bound alone decides.
No kernel may reach another device: no remote copies, remote signals or barrier semaphores. Data moves between devices by JAX's collectives and lax.ppermute only.
A program may use at most 64 MiB of HBM per device.

```python
import math
import jax
import jax.numpy as jnp
from jax import lax

TRACERS = 8
LEVELS = 16
LATITUDES = 512
SOLVER_ITERS = 4
LONGITUDES = 256


def depth_table(key):
    land_key, level_key = jax.random.split(jax.random.fold_in(key, 7))
    is_land = jax.random.randint(land_key, (LONGITUDES, LATITUDES), 0, 4) == 0
    levels_drawn = jax.random.randint(level_key, (LONGITUDES, LATITUDES), 1, LEVELS + 1)
    depths_all = jnp.where(is_land, 0, levels_drawn).astype(jnp.int32)
    depths_all = depths_all.at[0, 0].set(LEVELS).at[1, 0].set(LEVELS).at[2, 0].set(0)
    return depths_all


def draw_column_depth(key, part):
    return depth_table(key)


def draw_east_depth(key, part):
    depths_all = depth_table(key)
    return jnp.minimum(depths_all, jnp.roll(depths_all, -1, axis=0)).astype(jnp.int32)


def draw_ocean_mask(key, part):
    return (depth_table(key) > 0).astype(jnp.int32).T


def draw_surface_forcing(key, part):
    rows_frac = jnp.arange(LATITUDES, dtype=jnp.float32)[:, None] / (LATITUDES - 1)
    normal_part = jnp.clip(jax.random.normal(key, (LATITUDES, LONGITUDES), jnp.float32), -4.0, 4.0)
    return ((1.0 + 2.0 * rows_frac) * normal_part).astype(jnp.float32)


def steps_of(stream_key, shape, cuts, least, high):
    level = 1.0
    for dim, parts in cuts:
        draws = jax.random.uniform(jax.random.fold_in(jax.random.fold_in(stream_key, 6), dim), (parts,), jnp.float32, least / len(cuts), high / len(cuts))
        level = level * jnp.repeat(jnp.exp(draws), shape[dim] // parts).reshape((-1,) + (1,) * (len(shape) - 1 - dim))
    return level


def scatter_about(own_key, shape, deviation, bound, cuts=(), kind=jnp.bfloat16):
    array = deviation * jax.random.normal(own_key, shape, jnp.float32)
    if cuts:
        array = array * steps_of(own_key, shape, cuts, -0.22, 0.18)
    return jnp.clip(array, -bound, bound).astype(kind)


def setup_inputs(seed: int = 0, part: int = 0) -> dict:
    seeds = jax.random.split(jax.random.key(seed), 10)
    own_keys = jax.random.split(jax.random.fold_in(seeds[9], part), 10)
    return {
        "surface_old": scatter_about(own_keys[0], (LATITUDES, LONGITUDES), 1.0, 6.0, ((0, 16),), jnp.float32),
        "surface_forcing": draw_surface_forcing(jax.random.fold_in(jax.random.fold_in(seeds[9], part), 71), part),
        "surface_coeff": jnp.clip(jnp.exp(math.log(1.0) - 2.3025851 * jax.random.uniform(seeds[2], (LATITUDES, LONGITUDES), jnp.float32) ** steps_of(seeds[2], (LATITUDES, LONGITUDES), ((0, 16),), -0.2, 0.2)), 0.1, 1.0),
        "ocean_mask": draw_ocean_mask(jax.random.fold_in(seeds[9], 71), part),
        "column_depth": draw_column_depth(jax.random.fold_in(seeds[9], 71), part),
        "east_depth": draw_east_depth(jax.random.fold_in(seeds[9], 71), part),
        "tracers": jnp.clip(0.05 + 1.95 * jax.random.uniform(own_keys[6], (TRACERS, LEVELS, LONGITUDES, LATITUDES), jnp.float32) ** steps_of(own_keys[6], (TRACERS, LEVELS, LONGITUDES, LATITUDES), ((2, 16),), -0.2, 0.2), 0.05, 2.0),
        "u_clinic": scatter_about(own_keys[7], (LEVELS, LONGITUDES, LATITUDES), 0.3, 0.9, ((1, 16),), jnp.float32),
        "v_clinic": scatter_about(own_keys[8], (LEVELS, LONGITUDES, LATITUDES), 0.3, 0.9, ((1, 16),), jnp.float32),
    }


BARO_GAIN = 0.1
HORIZ_DIFF = 0.1
VERT_DIFF = 0.15
RATE_CARBON = 0.3
RATE_AMMONIUM = 0.2
RATE_NITRITE = 0.2
RATE_SULFIDE = 0.3
RATE_NITROUS = 0.2
HALF_OXYGEN = 0.3
HALF_NITRATE = 0.3
HALF_NITRITE = 0.3
YIELD_NITROUS = 0.3


def apply_operator(values_in, mask_float, coeff):
    masked = mask_float * values_in
    northern = jnp.concatenate([masked[1:], masked[-1:, ::-1]], axis=0)
    southern = jnp.concatenate([jnp.zeros_like(masked[:1]), masked[:-1]], axis=0)
    eastern = jnp.roll(masked, -1, axis=1)
    western = jnp.roll(masked, 1, axis=1)
    return (coeff + 4.0 * mask_float) * values_in - mask_float * (((northern + southern) + eastern) + western)


def solve_surface(right_side, mask_float, coeff):
    solution = jnp.zeros_like(right_side)
    residual = right_side
    direction = right_side
    norm_now = jnp.sum(residual * residual)
    for sweep in range(SOLVER_ITERS):
        applied = apply_operator(direction, mask_float, coeff)
        step_size = norm_now / jnp.sum(direction * applied)
        solution = solution + step_size * direction
        residual = residual - step_size * applied
        norm_next = jnp.sum(residual * residual)
        direction = residual + (norm_next / norm_now) * direction
        norm_now = norm_next
    return solution


def open_faces(column_depth, east_depth, east_baro, north_baro, u_clinic, v_clinic):
    level_index = lax.broadcasted_iota(jnp.int32, u_clinic.shape, 0)
    wet = (level_index < column_depth[None]).astype(jnp.float32)
    east_open = (level_index < east_depth[None]).astype(jnp.float32)
    north_open = wet * jnp.concatenate([wet[:, :, 1:], jnp.zeros_like(wet[:, :, :1])], axis=2)
    below_open = wet * jnp.concatenate([wet[1:], jnp.zeros_like(wet[:1])], axis=0)
    east_flow = (u_clinic + east_baro[None]) * east_open
    north_flow = (v_clinic + north_baro[None]) * north_open
    return wet, east_open, north_open, below_open, east_flow, north_flow


def meridional_vertical(masked, north_flow, north_open, below_open):
    count_rows = masked.shape[-1]
    pad_widths = [(0, 0)] * (masked.ndim - 1) + [(2, 2)]
    padded = jnp.pad(masked, pad_widths)
    south_one = padded[..., 1:count_rows + 1]
    north_one = padded[..., 3:count_rows + 3]
    north_two = padded[..., 4:count_rows + 4]
    face_north = (7.0 * (masked + north_one) - (south_one + north_two)) / 12.0
    flux_north = north_flow * face_north - HORIZ_DIFF * (north_one - masked) * north_open
    flux_south = jnp.concatenate([jnp.zeros_like(flux_north[..., :1]), flux_north[..., :-1]], axis=-1)
    below = jnp.concatenate([masked[..., 1:, :, :], jnp.zeros_like(masked[..., :1, :, :])], axis=-3)
    flux_down = VERT_DIFF * (below - masked) * below_open
    flux_up = jnp.concatenate([jnp.zeros_like(flux_down[..., :1, :, :]), flux_down[..., :-1, :, :]], axis=-3)
    return (flux_south - flux_north) + (flux_down - flux_up)


def redox_sources(masked):
    oxygen = masked[0]
    nitrate = masked[1]
    nitrite = masked[2]
    ammonium = masked[3]
    carbon = masked[5]
    sulfide = masked[6]
    nitrous = masked[7]
    breakdown = RATE_CARBON * carbon
    with_oxygen = oxygen / (oxygen + HALF_OXYGEN)
    with_nitrate = (1.0 - with_oxygen) * nitrate / (nitrate + HALF_NITRATE)
    with_nitrite = (1.0 - with_oxygen - with_nitrate) * nitrite / (nitrite + HALF_NITRITE)
    with_sulfate = 1.0 - with_oxygen - with_nitrate - with_nitrite
    first_nitr = RATE_AMMONIUM * ammonium * with_oxygen
    second_nitr = RATE_NITRITE * nitrite * with_oxygen
    sulfide_ox = RATE_SULFIDE * sulfide * with_oxygen
    return jnp.stack([
        -1.3 * breakdown * with_oxygen - 1.5 * first_nitr - 0.5 * second_nitr - 2.0 * sulfide_ox,
        -0.9 * breakdown * with_nitrate + second_nitr,
        0.9 * breakdown * with_nitrate - 0.6 * breakdown * with_nitrite + (1.0 - YIELD_NITROUS) * first_nitr - second_nitr,
        0.15 * breakdown - first_nitr,
        0.1 * breakdown,
        -breakdown,
        0.5 * breakdown * with_sulfate - sulfide_ox,
        YIELD_NITROUS * first_nitr - RATE_NITROUS * nitrous * (1.0 - with_oxygen),
    ])


def zonal_terms(masked, east_flow, east_open):
    east_one = jnp.roll(masked, -1, axis=-2)
    east_two = jnp.roll(masked, -2, axis=-2)
    west_one = jnp.roll(masked, 1, axis=-2)
    face_east = (7.0 * (masked + east_one) - (west_one + east_two)) / 12.0
    flux_east = east_flow * face_east - HORIZ_DIFF * (east_one - masked) * east_open
    return jnp.roll(flux_east, 1, axis=-2) - flux_east


def reference(surface_old, surface_forcing, surface_coeff, ocean_mask, column_depth, east_depth, tracers, u_clinic, v_clinic):
    mask_float = ocean_mask.astype(jnp.float32)
    right_side = surface_coeff * surface_old + surface_forcing
    surface = solve_surface(right_side, mask_float, surface_coeff)
    band_flow = -BARO_GAIN * (jnp.roll(surface, -1, axis=1) - surface)
    strip_surface = surface.T
    above_surface = jnp.concatenate([strip_surface[:, 1:], strip_surface[:, -1:]], axis=1)
    north_baro = -BARO_GAIN * (above_surface - strip_surface)
    wet, east_open, north_open, below_open, east_flow, north_flow = open_faces(
        column_depth, east_depth, band_flow.T, north_baro, u_clinic, v_clinic)
    masked = tracers * wet[None]

    def per_tracer(single):
        return zonal_terms(single, east_flow, east_open) + meridional_vertical(single, north_flow, north_open, below_open)

    transport = lax.map(per_tracer, masked)
    tendency = transport + redox_sources(masked)
    tracers_new = tracers + wet[None] * tendency
    return surface, tracers_new
```

```python
import jax
import jax.numpy as jnp
from jax import lax
from jax.experimental import pallas as pl
from jax.experimental.pallas import tpu as pltpu
from jax.sharding import PartitionSpec as P

BARO_GAIN = 0.1
HORIZ_DIFF = 0.1
VERT_DIFF = 0.15
RATE_CARBON = 0.3
RATE_AMMONIUM = 0.2
RATE_NITRITE = 0.2
RATE_SULFIDE = 0.3
RATE_NITROUS = 0.2
HALF_OXYGEN = 0.3
HALF_NITRATE = 0.3
HALF_NITRITE = 0.3
YIELD_NITROUS = 0.3


def padded_2(block, sides, width, periodic):
    for axis, dim in sides:
        count = lax.axis_size(axis)
        forward = [(i, i + 1) for i in range(count - 1)]
        if periodic:
            forward.append((count - 1, 0))
        backward = [(target, source) for source, target in forward]
        low = lax.ppermute(
            lax.slice_in_dim(block, block.shape[dim] - width, None, axis=dim), axis, forward
        )
        high = lax.ppermute(lax.slice_in_dim(block, 0, width, axis=dim), axis, backward)
        block = jnp.concatenate([low, block, high], axis=dim)
    return block


LANES = 128
HALO = 8
SLAB_ROWS = 24
BASIS = 4
CENTRE = 4.55
SPREAD = 4.45
PIVOT_FLOOR = 3e-7


def pack_kernel(old_ref, force_ref, coeff_ref, mask_ref, low_ref, high_ref):
    rows = old_ref.shape[0]
    coeff = coeff_ref[...]
    fields = (
        coeff * old_ref[...] + force_ref[...],
        coeff,
        mask_ref[...].astype(jnp.float32),
    )
    for place, field in enumerate(fields):
        low_ref[HALO * place : HALO * (place + 1)] = field[:HALO]
        high_ref[HALO * place : HALO * (place + 1)] = field[rows - HALO :]


def basis_kernel(
    old_ref, force_ref, coeff_ref, mask_ref, below_ref, above_ref, folded_ref, slabs_ref, basis_ref
):
    rows, width = old_ref.shape
    count = slabs_ref.shape[0]
    columns = width // count
    top_device = lax.axis_index("lon") == count - 1
    above = jnp.where(top_device, folded_ref[...], above_ref[...])

    def extended(place, own):
        part = slice(HALO * place, HALO * (place + 1))
        return jnp.concatenate([below_ref[part], own, above[part]], axis=0)

    coeff_own = coeff_ref[...]
    first = extended(0, coeff_own * old_ref[...] + force_ref[...])
    coeff = extended(1, coeff_own)
    mask = extended(2, mask_ref[...].astype(jnp.float32))
    diagonal = (coeff + 4.0 * mask - CENTRE) * (1.0 / SPREAD)
    beside = mask * (1.0 / SPREAD)
    total = rows + 2 * HALO

    def scaled(values):
        masked = mask * values
        around = (
            pltpu.roll(masked, total - 1, 0)
            + pltpu.roll(masked, 1, 0)
            + pltpu.roll(masked, width - 1, 1)
            + pltpu.roll(masked, 1, 1)
        )
        return diagonal * values - beside * around

    vectors = [first, scaled(first)]
    while len(vectors) < BASIS + 1:
        vectors.append(2.0 * scaled(vectors[-1]) - vectors[-2])
    own = [vector[HALO : HALO + rows] for vector in vectors]
    sums = []
    for order in range(2 * BASIS):
        product = own[order // 2] * own[(order + 1) // 2]
        sums.append(jnp.sum(product, axis=0, keepdims=True))
    partial = jnp.sum(jnp.concatenate(sums, axis=0), axis=1, keepdims=True)
    lane = lax.broadcasted_iota(jnp.int32, (2 * BASIS, LANES), 1)
    place = lax.broadcasted_iota(jnp.int32, (2 * BASIS, LANES), 0)
    moments = jnp.sum(jnp.where(lane == place, partial, 0.0), axis=0, keepdims=True)
    stacked = jnp.concatenate(own[:BASIS], axis=0)
    basis_ref[...] = stacked
    if BASIS * rows < LANES:
        stacked = jnp.concatenate(
            [stacked, jnp.zeros((LANES - BASIS * rows, width), jnp.float32)], axis=0
        )
    turned = stacked.T
    for target in range(count):
        start = target * columns
        east = (start + columns) % width
        west = (start - 1) % width
        slabs_ref[target, :columns] = turned[start : start + columns]
        slabs_ref[target, columns : columns + 1] = turned[east : east + 1]
        slabs_ref[target, columns + 1 : columns + 2] = turned[west : west + 1]
        slabs_ref[target, columns + 2 : columns + 3] = moments


def basis_weights(moments):
    gram = {}

    def inner(i, j):
        key = (i + j, abs(i - j))
        if key not in gram:
            gram[key] = 0.5 * (moments[i + j] + moments[abs(i - j)])
        return gram[key]

    matrix = [[None] * BASIS for _ in range(BASIS)]
    for i in range(BASIS):
        for j in range(i + 1):
            if i == 0:
                image = moments[1]
            elif j == 0:
                image = inner(1, i)
            else:
                image = 0.5 * (inner(i, j + 1) + inner(i, j - 1))
            matrix[i][j] = CENTRE * inner(i, j) + SPREAD * image
    right = [inner(i, 0) for i in range(BASIS)]
    start = [matrix[i][i] for i in range(BASIS)]
    inverse = []
    factors = [[None] * BASIS for _ in range(BASIS)]
    for n in range(BASIS):
        pivot = matrix[n][n]
        inverse.append(jnp.where(pivot > PIVOT_FLOOR * start[n], 1.0 / pivot, 0.0))
        for i in range(n + 1, BASIS):
            factors[i][n] = matrix[i][n] * inverse[n]
        for i in range(n + 1, BASIS):
            for j in range(n + 1, i + 1):
                matrix[i][j] = matrix[i][j] - factors[i][n] * matrix[j][n]
            right[i] = right[i] - factors[i][n] * right[n]
    weights = [None] * BASIS
    for n in reversed(range(BASIS)):
        value = right[n] * inverse[n]
        for i in range(n + 1, BASIS):
            value = value - factors[i][n] * weights[i]
        weights[n] = value
    return weights


def combine_kernel(slabs_ref, basis_ref, strip_ref, surface_ref):
    count, slab_rows, _ = slabs_ref.shape
    rows, width = surface_ref.shape
    columns = width // count
    moment_row = slabs_ref[0, columns + 2 : columns + 3]
    for source in range(1, count):
        moment_row = moment_row + slabs_ref[source, columns + 2 : columns + 3]
    dots = [moment_row[:, m : m + 1] for m in range(2 * BASIS)]
    weights = basis_weights(
        dots[:2] + [2.0 * dots[m] - dots[m % 2] for m in range(2, 2 * BASIS)]
    )
    group = lax.broadcasted_iota(jnp.int32, (1, LANES), 1) // rows
    lane_weight = jnp.zeros((1, LANES), jnp.float32)
    for k in range(BASIS):
        lane_weight = jnp.where(group == k, weights[k], lane_weight)
    surface = weights[0] * basis_ref[:rows]
    for k in range(1, BASIS):
        surface = surface + weights[k] * basis_ref[k * rows : (k + 1) * rows]
    surface_ref[...] = surface
    groups = LANES // rows
    group_full = lax.broadcasted_iota(jnp.int32, (slab_rows, LANES), 1) // rows
    for tile in range(count // groups):
        joined = None
        for p in range(groups):
            part = slabs_ref[tile * groups + p] * lane_weight
            shift = LANES // 2
            while shift >= rows:
                part = part + pltpu.roll(part, shift, 1)
                shift //= 2
            joined = part if joined is None else jnp.where(group_full == p, part, joined)
        strip_ref[:, tile * LANES : (tile + 1) * LANES] = joined


def solve_surface(surface_old, surface_forcing, surface_coeff, ocean_mask):
    rows, width = surface_old.shape
    count = lax.axis_size("lon")
    f32 = jnp.float32
    packed = jax.ShapeDtypeStruct((3 * HALO, width), f32)
    fields = (surface_old, surface_forcing, surface_coeff, ocean_mask)
    low, high = pl.pallas_call(pack_kernel, out_shape=(packed, packed), name="pack_edges")(*fields)
    forward = [(i, i + 1) for i in range(count - 1)]
    backward = [(target, source) for source, target in forward]
    below = lax.ppermute(high, "lon", forward)
    above = lax.ppermute(low, "lon", backward)
    folded = jnp.flip(high.reshape(3, HALO, width), axis=(1, 2)).reshape(3 * HALO, width)
    slabs, basis = pl.pallas_call(
        basis_kernel,
        out_shape=(
            jax.ShapeDtypeStruct((count, SLAB_ROWS, LANES), f32),
            jax.ShapeDtypeStruct((BASIS * rows, width), f32),
        ),
        name="solver_basis",
    )(*fields, below, above, folded)
    moved = lax.all_to_all(slabs, "lon", split_axis=0, concat_axis=0, tiled=True)
    strip, surface = pl.pallas_call(
        combine_kernel,
        out_shape=(
            jax.ShapeDtypeStruct((SLAB_ROWS, count * rows), f32),
            jax.ShapeDtypeStruct((rows, width), f32),
        ),
        name="solver_combine",
    )(moved, basis)
    return strip, surface


def open_faces(column_depth, east_depth, east_baro, north_baro, u_clinic, v_clinic):
    level_index = lax.broadcasted_iota(jnp.int32, u_clinic.shape, 0)
    wet = (level_index < column_depth[None]).astype(jnp.float32)
    east_open = (level_index < east_depth[None]).astype(jnp.float32)
    north_open = wet * jnp.concatenate([wet[:, :, 1:], jnp.zeros_like(wet[:, :, :1])], axis=2)
    below_open = wet * jnp.concatenate([wet[1:], jnp.zeros_like(wet[:1])], axis=0)
    east_flow = (u_clinic + east_baro[None]) * east_open
    north_flow = (v_clinic + north_baro[None]) * north_open
    return (wet, east_open, north_open, below_open, east_flow, north_flow)


def meridional_vertical(masked, north_flow, north_open, below_open):
    count_rows = masked.shape[-1]
    pad_widths = [(0, 0)] * (masked.ndim - 1) + [(2, 2)]
    padded = jnp.pad(masked, pad_widths)
    south_one = padded[..., 1 : count_rows + 1]
    north_one = padded[..., 3 : count_rows + 3]
    north_two = padded[..., 4 : count_rows + 4]
    face_north = (7.0 * (masked + north_one) - (south_one + north_two)) / 12.0
    flux_north = north_flow * face_north - HORIZ_DIFF * (north_one - masked) * north_open
    flux_south = jnp.concatenate(
        [jnp.zeros_like(flux_north[..., :1]), flux_north[..., :-1]], axis=-1
    )
    below = jnp.concatenate([masked[..., 1:, :, :], jnp.zeros_like(masked[..., :1, :, :])], axis=-3)
    flux_down = VERT_DIFF * (below - masked) * below_open
    flux_up = jnp.concatenate(
        [jnp.zeros_like(flux_down[..., :1, :, :]), flux_down[..., :-1, :, :]], axis=-3
    )
    return flux_south - flux_north + (flux_down - flux_up)


def redox_sources(masked):
    oxygen = masked[0]
    nitrate = masked[1]
    nitrite = masked[2]
    ammonium = masked[3]
    carbon = masked[5]
    sulfide = masked[6]
    nitrous = masked[7]
    breakdown = RATE_CARBON * carbon
    with_oxygen = oxygen / (oxygen + HALF_OXYGEN)
    with_nitrate = (1.0 - with_oxygen) * nitrate / (nitrate + HALF_NITRATE)
    with_nitrite = (1.0 - with_oxygen - with_nitrate) * nitrite / (nitrite + HALF_NITRITE)
    with_sulfate = 1.0 - with_oxygen - with_nitrate - with_nitrite
    first_nitr = RATE_AMMONIUM * ammonium * with_oxygen
    second_nitr = RATE_NITRITE * nitrite * with_oxygen
    sulfide_ox = RATE_SULFIDE * sulfide * with_oxygen
    return jnp.stack(
        [
            -1.3 * breakdown * with_oxygen
            - 1.5 * first_nitr
            - 0.5 * second_nitr
            - 2.0 * sulfide_ox,
            -0.9 * breakdown * with_nitrate + second_nitr,
            0.9 * breakdown * with_nitrate
            - 0.6 * breakdown * with_nitrite
            + (1.0 - YIELD_NITROUS) * first_nitr
            - second_nitr,
            0.15 * breakdown - first_nitr,
            0.1 * breakdown,
            -breakdown,
            0.5 * breakdown * with_sulfate - sulfide_ox,
            YIELD_NITROUS * first_nitr - RATE_NITROUS * nitrous * (1.0 - with_oxygen),
        ]
    )


def body(
    surface_old,
    surface_forcing,
    surface_coeff,
    ocean_mask,
    column_depth,
    east_depth,
    tracers,
    u_clinic,
    v_clinic,
):
    strip, surface = solve_surface(surface_old, surface_forcing, surface_coeff, ocean_mask)
    columns = tracers.shape[2]
    strip_surface = strip[:columns]
    east_baro = -BARO_GAIN * (strip[1 : columns + 1] - strip_surface)
    above_surface = jnp.concatenate([strip_surface[:, 1:], strip_surface[:, -1:]], axis=1)
    north_baro = -BARO_GAIN * (above_surface - strip_surface)
    wet, east_open, north_open, below_open, east_flow, north_flow = open_faces(
        column_depth, east_depth, east_baro, north_baro, u_clinic, v_clinic
    )
    masked = tracers * wet[None]
    tracer_count = masked.shape[0]
    columns_here = masked.shape[2]
    stacked = jnp.concatenate([masked, east_flow[None], east_open[None]], axis=0)
    padded = padded_2(stacked, (("lon", 2),), 2, True)
    tracer_pad = padded[:tracer_count]
    west_flow = padded[tracer_count, :, 1:2]
    west_open = padded[tracer_count + 1, :, 1:2]
    flow_all = jnp.concatenate([west_flow, east_flow], axis=1)
    open_all = jnp.concatenate([west_open, east_open], axis=1)
    center = tracer_pad[:, :, 1 : columns_here + 2]
    east_one = tracer_pad[:, :, 2 : columns_here + 3]
    west_one = tracer_pad[:, :, 0 : columns_here + 1]
    east_two = tracer_pad[:, :, 3 : columns_here + 4]
    face_east = (7.0 * (center + east_one) - (west_one + east_two)) / 12.0
    flux_all = flow_all[None] * face_east - HORIZ_DIFF * (east_one - center) * open_all[None]
    conv_east = flux_all[:, :, :-1] - flux_all[:, :, 1:]
    transport = conv_east + meridional_vertical(
        masked, north_flow[None], north_open[None], below_open[None]
    )
    tendency = transport + redox_sources(masked)
    tracers_new = tracers + wet[None] * tendency
    return (surface, tracers_new)


def solution(mesh):
    in_specs = (
        P(("member", "lon"), None),
        P(("member", "lon"), None),
        P("lon", None),
        P("lon", None),
        P("lon", None),
        P("lon", None),
        P("member", None, "lon", None),
        P("member", "lon", None),
        P("member", "lon", None),
    )
    out_specs = (P(("member", "lon"), None), P("member", None, "lon", None))
    return jax.shard_map(body, mesh=mesh, in_specs=in_specs, out_specs=out_specs, check_vma=False)
```

```python
import functools

import jax
import jax.numpy as jnp
from jax import lax
from jax.experimental import pallas as pl
from jax.experimental.pallas import tpu as pltpu
from jax.sharding import PartitionSpec as P

BARO_GAIN = 0.1
HORIZ_DIFF = 0.1
VERT_DIFF = 0.15
RATE_CARBON = 0.3
RATE_AMMONIUM = 0.2
RATE_NITRITE = 0.2
RATE_SULFIDE = 0.3
RATE_NITROUS = 0.2
HALF_OXYGEN = 0.3
HALF_NITRATE = 0.3
HALF_NITRITE = 0.3
YIELD_NITROUS = 0.3


SUBLANES = 8
LANES = 128
SMALL_VMEM = 8 * 2**20
RESULT_VMEM = 14 * 2**20
HALO = 8
SLAB_ROWS = 24
BASIS = 4
CENTRE = 4.55
SPREAD = 4.45
PIVOT_FLOOR = 3e-7


def pack_kernel(old_ref, force_ref, coeff_ref, mask_ref, low_ref, high_ref):
    rows = old_ref.shape[0]
    coeff = coeff_ref[...]
    fields = (
        coeff * old_ref[...] + force_ref[...],
        coeff,
        mask_ref[...].astype(jnp.float32),
    )
    for place, field in enumerate(fields):
        low_ref[HALO * place : HALO * (place + 1)] = field[:HALO]
        high_ref[HALO * place : HALO * (place + 1)] = field[rows - HALO :]


def basis_kernel(
    old_ref,
    force_ref,
    coeff_ref,
    mask_ref,
    below_ref,
    above_ref,
    folded_ref,
    _,
    keep_ref,
    send_ref,
    basis_ref,
):
    rows, width = old_ref.shape
    count = 2 * keep_ref.shape[0]
    columns = width // count
    top_device = lax.axis_index("lon") == count - 1
    above = jnp.where(top_device, folded_ref[...], above_ref[...])

    def extended(place, own):
        part = slice(HALO * place, HALO * (place + 1))
        return jnp.concatenate([below_ref[part], own, above[part]], axis=0)

    coeff_own = coeff_ref[...]
    first = extended(0, coeff_own * old_ref[...] + force_ref[...])
    coeff = extended(1, coeff_own)
    mask = extended(2, mask_ref[...].astype(jnp.float32))
    diagonal = (coeff + 4.0 * mask - CENTRE) * (1.0 / SPREAD)
    beside = mask * (1.0 / SPREAD)
    total = rows + 2 * HALO

    def scaled(values):
        masked = mask * values
        around = (
            pltpu.roll(masked, total - 1, 0)
            + pltpu.roll(masked, 1, 0)
            + pltpu.roll(masked, width - 1, 1)
            + pltpu.roll(masked, 1, 1)
        )
        return diagonal * values - beside * around

    vectors = [first, scaled(first)]
    while len(vectors) < BASIS + 1:
        vectors.append(2.0 * scaled(vectors[-1]) - vectors[-2])
    own = [vector[HALO : HALO + rows] for vector in vectors]
    sums = []
    for order in range(2 * BASIS):
        product = own[order // 2] * own[(order + 1) // 2]
        sums.append(jnp.sum(product, axis=0, keepdims=True))
    partial = jnp.sum(jnp.concatenate(sums, axis=0), axis=1, keepdims=True)
    lane = lax.broadcasted_iota(jnp.int32, (2 * BASIS, LANES), 1)
    place = lax.broadcasted_iota(jnp.int32, (2 * BASIS, LANES), 0)
    moments = jnp.sum(jnp.where(lane == place, partial, 0.0), axis=0, keepdims=True)
    stacked = jnp.concatenate(own[:BASIS], axis=0)
    basis_ref[...] = stacked
    if BASIS * rows < LANES:
        stacked = jnp.concatenate(
            [stacked, jnp.zeros((LANES - BASIS * rows, width), jnp.float32)], axis=0
        )
    turned = stacked.T
    core = lax.rem(lax.axis_index("lon"), 2)
    slabs = []
    for target in range(count):
        start = target * columns
        east = (start + columns) % width
        west = (start - 1) % width
        pieces = [
            turned[start : start + columns],
            turned[east : east + 1],
            turned[west : west + 1],
            moments,
            jnp.zeros((SLAB_ROWS - columns - 3, LANES), jnp.float32),
        ]
        slabs.append(jnp.concatenate(pieces, axis=0))
    for pair in range(count // 2):
        even, odd = slabs[2 * pair], slabs[2 * pair + 1]
        keep_ref[pair] = jnp.where(core == 0, even, odd)
        send_ref[pair] = jnp.where(core == 0, odd, even)


def split_kernel(kept_ref, came_ref, keep_ref, send_ref):
    here = lax.axis_index("lon")
    core, half = lax.rem(here, 2), lax.rem(here // 2, 2)
    for group in range(keep_ref.shape[0]):
        for y in range(2):
            mine, other = kept_ref[2 * group + y], came_ref[2 * group + y]
            first = jnp.where(core == 0, mine, other)
            second = jnp.where(core == 0, other, mine)

            @pl.when(half == y)
            def _():
                keep_ref[group, 0] = first
                keep_ref[group, 1] = second

            @pl.when(half != y)
            def _():
                send_ref[group, 0] = first
                send_ref[group, 1] = second


def spread_kernel(kept_ref, came_ref, *out_refs):
    here = lax.axis_index("lon")
    half, group = lax.rem(here // 2, 2), here // 4
    groups = len(out_refs)
    for step in range(groups):
        target = lax.rem(group + step, groups)
        for core in range(2):
            mine, other = kept_ref[target, core], came_ref[target, core]
            out_refs[step][core] = jnp.where(half == 0, mine, other)
            out_refs[step][2 + core] = jnp.where(half == 0, other, mine)


def basis_weights(moments):
    gram = {}

    def inner(i, j):
        key = (i + j, abs(i - j))
        if key not in gram:
            gram[key] = 0.5 * (moments[i + j] + moments[abs(i - j)])
        return gram[key]

    matrix = [[None] * BASIS for _ in range(BASIS)]
    for i in range(BASIS):
        for j in range(i + 1):
            if i == 0:
                image = moments[1]
            elif j == 0:
                image = inner(1, i)
            else:
                image = 0.5 * (inner(i, j + 1) + inner(i, j - 1))
            matrix[i][j] = CENTRE * inner(i, j) + SPREAD * image
    right = [inner(i, 0) for i in range(BASIS)]
    start = [matrix[i][i] for i in range(BASIS)]
    inverse = []
    factors = [[None] * BASIS for _ in range(BASIS)]
    for n in range(BASIS):
        pivot = matrix[n][n]
        inverse.append(jnp.where(pivot > PIVOT_FLOOR * start[n], 1.0 / pivot, 0.0))
        for i in range(n + 1, BASIS):
            factors[i][n] = matrix[i][n] * inverse[n]
        for i in range(n + 1, BASIS):
            for j in range(n + 1, i + 1):
                matrix[i][j] = matrix[i][j] - factors[i][n] * matrix[j][n]
            right[i] = right[i] - factors[i][n] * right[n]
    weights = [None] * BASIS
    for n in reversed(range(BASIS)):
        value = right[n] * inverse[n]
        for i in range(n + 1, BASIS):
            value = value - factors[i][n] * weights[i]
        weights[n] = value
    return weights


def reverse_tile(tile):
    for axis, size in ((0, SUBLANES), (1, LANES)):
        place = lax.broadcasted_iota(jnp.int32, (SUBLANES, LANES), axis)
        step = size // 2
        while step:
            tile = jnp.where(
                (place & step) != 0,
                pltpu.roll(tile, step, axis),
                pltpu.roll(tile, size - step, axis),
            )
            step //= 2
    return tile


def edge_kernel(
    high_ref,
    tracers_ref,
    depth_ref,
    east_depth_ref,
    u_ref,
    folded_ref,
    east_going_ref,
    west_going_ref,
):
    tiles = high_ref.shape[1] // LANES
    for place in range(3):
        rows = slice(HALO * place, HALO * (place + 1))
        for tile in range(tiles):
            other = tiles - 1 - tile
            folded_ref[rows, tile * LANES : (tile + 1) * LANES] = reverse_tile(
                high_ref[rows, other * LANES : (other + 1) * LANES]
            )
    kinds, levels, columns, rows = tracers_ref.shape
    for z in range(levels):
        for side in range(2):
            column = columns - 2 + side
            west_wet = (z < depth_ref[side : side + 1]).astype(jnp.float32)
            east_wet = (z < depth_ref[column : column + 1]).astype(jnp.float32)
            for kind in range(kinds):
                west_going_ref[2 * z + side, kind : kind + 1] = (
                    tracers_ref[kind, z, side : side + 1] * west_wet
                )
                east_going_ref[2 * z + side, kind : kind + 1] = (
                    tracers_ref[kind, z, column : column + 1] * east_wet
                )
        place = 2 * levels + z // SUBLANES
        row = z % SUBLANES
        east_going_ref[place, row : row + 1] = u_ref[z, columns - 1 : columns]
    place = 2 * levels + levels // SUBLANES
    east_going_ref[place] = jnp.broadcast_to(
        east_depth_ref[columns - 1 : columns].astype(jnp.float32), (SUBLANES, rows)
    )


def grid_tiles(columns, rows):
    return [
        (block, tile)
        for block in range(columns // SUBLANES)
        for tile in range(rows // LANES)
    ]


def tile_index(place):
    block, tile = place
    return (
        slice(block * SUBLANES, (block + 1) * SUBLANES),
        slice(tile * LANES, (tile + 1) * LANES),
    )


def shift_columns(tiles, step, outer, blocks, count):
    sublane = lax.broadcasted_iota(jnp.int32, (SUBLANES, LANES), 0)
    turned = {p: pltpu.roll(x, SUBLANES - 1 if step > 0 else 1, 0) for p, x in tiles.items()}
    inside = sublane < SUBLANES - 1 if step > 0 else sublane > 0
    shifted = {}
    for block in range(blocks):
        for tile in range(count):
            beyond = block + step
            other = turned[beyond, tile] if 0 <= beyond < blocks else outer[tile]
            shifted[block, tile] = jnp.where(inside, turned[block, tile], other)
    return shifted


def shift_rows(tiles, step, blocks, count):
    lane = lax.broadcasted_iota(jnp.int32, (SUBLANES, LANES), 1)
    turned = {p: pltpu.roll(x, LANES - 1 if step > 0 else 1, 1) for p, x in tiles.items()}
    inside = lane < LANES - 1 if step > 0 else lane > 0
    shifted = {}
    for block in range(blocks):
        for tile in range(count):
            beyond = tile + step
            other = turned[block, beyond] if 0 <= beyond < count else 0.0
            shifted[block, tile] = jnp.where(inside, turned[block, tile], other)
    return shifted


def reciprocal(value):
    guess = pl.reciprocal(value, approx=True)
    return guess * (2.0 - value * guess)


def redox_sources(masked):
    oxygen, nitrate, nitrite, ammonium, _, carbon, sulfide, nitrous = masked
    over_oxygen = reciprocal(oxygen + HALF_OXYGEN)
    with_oxygen = oxygen * over_oxygen
    no_oxygen = HALF_OXYGEN * over_oxygen
    with_nitrate = no_oxygen * nitrate * reciprocal(nitrate + HALF_NITRATE)
    rest = no_oxygen - with_nitrate
    with_nitrite = rest * nitrite * reciprocal(nitrite + HALF_NITRITE)
    with_sulfate = rest - with_nitrite
    breakdown = RATE_CARBON * carbon
    first_nitr = RATE_AMMONIUM * ammonium * with_oxygen
    second_nitr = RATE_NITRITE * nitrite * with_oxygen
    sulfide_ox = RATE_SULFIDE * sulfide * with_oxygen
    by_nitrate = 0.9 * breakdown * with_nitrate
    return (
        -1.3 * breakdown * with_oxygen - 1.5 * first_nitr - 0.5 * second_nitr - 2.0 * sulfide_ox,
        second_nitr - by_nitrate,
        by_nitrate
        - 0.6 * breakdown * with_nitrite
        + (1.0 - YIELD_NITROUS) * first_nitr
        - second_nitr,
        0.15 * breakdown - first_nitr,
        0.1 * breakdown,
        -breakdown,
        0.5 * breakdown * with_sulfate - sulfide_ox,
        YIELD_NITROUS * first_nitr - RATE_NITROUS * nitrous * no_oxygen,
    )


def source_kernel(tracers_ref, depth_ref, base_ref):
    kinds, levels, columns, rows = tracers_ref.shape
    places = grid_tiles(columns, rows)

    @pl.loop(0, levels)
    def _(level):
        above = jnp.maximum(level - 1, 0)
        below = jnp.minimum(level + 1, levels - 1)
        mix_up_level = jnp.where(level > 0, VERT_DIFF, 0.0)
        for p in places:
            at = tile_index(p)
            depth_here = depth_ref[at]
            wet = jnp.where(level < depth_here, 1.0, 0.0)
            mix_up = wet * mix_up_level
            mix_down = jnp.where(level + 1 < depth_here, VERT_DIFF, 0.0)
            values = [tracers_ref[(kind, level) + at] for kind in range(kinds)]
            sources = redox_sources([value * wet for value in values])
            for kind in range(kinds):
                value = values[kind]
                down = (tracers_ref[(kind, below) + at] - value) * mix_down
                up = (value - tracers_ref[(kind, above) + at]) * mix_up
                base_ref[(kind, level) + at] = value + (wet * sources[kind] + (down - up))


def north_kernel(tracers_ref, depth_ref, v_ref, before_ref, _, base_ref, face_north_ref, north_ref):
    kinds, levels, columns, rows = tracers_ref.shape
    blocks, count = columns // SUBLANES, rows // LANES
    places = grid_tiles(columns, rows)
    depth = {p: depth_ref[tile_index(p)].astype(jnp.float32) for p in places}
    north_depth = shift_rows(depth, 1, blocks, count)
    for p in places:
        north_ref[tile_index(p)] = jnp.minimum(depth[p], north_depth[p]).astype(jnp.int32)

    @pl.loop(0, levels)
    def _(level):
        wet, scale, mix = {}, {}, {}
        for p in places:
            at = tile_index(p)
            wet[p] = jnp.where(level < depth_ref[at], 1.0, 0.0)
            is_open = level < north_ref[at]
            scale[p] = jnp.where(is_open, 1.0 / 12.0, 0.0)
            mix[p] = jnp.where(is_open, HORIZ_DIFF, 0.0)
        for kind in range(kinds):
            masked = {p: tracers_ref[(kind, level) + tile_index(p)] * wet[p] for p in places}
            one = shift_rows(masked, 1, blocks, count)
            two = shift_rows(one, 1, blocks, count)
            south = shift_rows(masked, -1, blocks, count)
            flux = {}
            for p in places:
                at = (kind, level) + tile_index(p)
                face = (7.0 * (masked[p] + one[p]) - (south[p] + two[p])) * scale[p]
                face_north_ref[at] = face
                flux[p] = v_ref[(level,) + tile_index(p)] * face - mix[p] * (one[p] - masked[p])
            incoming = shift_rows(flux, -1, blocks, count)
            for p in places:
                at = (kind, level) + tile_index(p)
                base_ref[at] = before_ref[at] + (incoming[p] - flux[p])


def east_kernel(
    tracers_ref,
    depth_ref,
    east_depth_ref,
    u_ref,
    from_west_ref,
    from_east_ref,
    own_west_ref,
    before_ref,
    _,
    base_ref,
    face_east_ref,
    face_west_ref,
    flux_west_ref,
):
    kinds, levels, columns, rows = tracers_ref.shape
    blocks, count = columns // SUBLANES, rows // LANES
    places = grid_tiles(columns, rows)
    depth_west = from_west_ref[2 * levels + levels // SUBLANES]
    for z in range(levels):
        row = z % SUBLANES
        u_west = from_west_ref[2 * levels + z // SUBLANES, row : row + 1]
        center, east_one = from_west_ref[2 * z + 1], own_west_ref[2 * z]
        outer = from_west_ref[2 * z] + own_west_ref[2 * z + 1]
        scale_west = jnp.where(z < depth_west, 1.0 / 12.0, 0.0)
        mix_west = jnp.where(z < depth_west, HORIZ_DIFF, 0.0)
        face = (7.0 * (center + east_one) - outer) * scale_west
        face_west_ref[z] = face
        flux_west_ref[z] = u_west * face - mix_west * (east_one - center)

    @pl.loop(0, levels)
    def _(level):
        wet, scale, mix = {}, {}, {}
        for p in places:
            at = tile_index(p)
            wet[p] = jnp.where(level < depth_ref[at], 1.0, 0.0)
            is_open = level < east_depth_ref[at]
            scale[p] = jnp.where(is_open, 1.0 / 12.0, 0.0)
            mix[p] = jnp.where(is_open, HORIZ_DIFF, 0.0)
        for kind in range(kinds):
            def halo(ref, index):
                return [
                    jnp.broadcast_to(
                        ref[index, kind : kind + 1, tile * LANES : (tile + 1) * LANES],
                        (SUBLANES, LANES),
                    )
                    for tile in range(count)
                ]

            masked = {p: tracers_ref[(kind, level) + tile_index(p)] * wet[p] for p in places}
            one = shift_columns(masked, 1, halo(from_east_ref, 2 * level), blocks, count)
            two = shift_columns(one, 1, halo(from_east_ref, 2 * level + 1), blocks, count)
            west = shift_columns(masked, -1, halo(from_west_ref, 2 * level + 1), blocks, count)
            flux = {}
            for p in places:
                at = (kind, level) + tile_index(p)
                face = (7.0 * (masked[p] + one[p]) - (west[p] + two[p])) * scale[p]
                face_east_ref[at] = face
                flux[p] = u_ref[(level,) + tile_index(p)] * face - mix[p] * (one[p] - masked[p])
            incoming = shift_columns(flux, -1, halo(flux_west_ref, level), blocks, count)
            for p in places:
                at = (kind, level) + tile_index(p)
                base_ref[at] = before_ref[at] + (incoming[p] - flux[p])


def update_kernel(groups, *refs):
    came_refs, refs = refs[:groups], refs[groups:]
    basis_ref, base_ref, face_east_ref, face_north_ref, face_west_ref = refs[:5]
    surface_ref, out_ref, slabs_ref, result_ref, sems = refs[5:]
    group = lax.axis_index("lon") // 4
    for step in range(groups):
        source = lax.rem(group + groups - step, groups)
        for place in range(4):
            slabs_ref[4 * source + place] = came_refs[step][place]
    kinds, levels, columns, rows = base_ref.shape
    blocks, count = columns // SUBLANES, rows // LANES
    places = grid_tiles(columns, rows)
    sources, slab_rows, _ = slabs_ref.shape
    band, width = surface_ref.shape
    moment_row = slabs_ref[0, columns + 2 : columns + 3]
    for source in range(1, sources):
        moment_row = moment_row + slabs_ref[source, columns + 2 : columns + 3]
    dots = [moment_row[:, m : m + 1] for m in range(2 * BASIS)]
    weights = basis_weights(
        dots[:2] + [2.0 * dots[m] - dots[m % 2] for m in range(2, 2 * BASIS)]
    )
    lane_group = lax.broadcasted_iota(jnp.int32, (1, LANES), 1) // band
    lane_weight = jnp.zeros((1, LANES), jnp.float32)
    for k in range(BASIS):
        lane_weight = jnp.where(lane_group == k, weights[k], lane_weight)
    surface = weights[0] * basis_ref[:band]
    for k in range(1, BASIS):
        surface = surface + weights[k] * basis_ref[k * band : (k + 1) * band]
    surface_ref[...] = surface

    fill = LANES // band
    group_full = lax.broadcasted_iota(jnp.int32, (slab_rows, LANES), 1) // band
    height, east_edge, west_edge = {}, [], []
    for tile in range(count):
        joined = None
        for p in range(fill):
            part = slabs_ref[tile * fill + p] * lane_weight
            shift = LANES // 2
            while shift >= band:
                part = part + pltpu.roll(part, shift, 1)
                shift //= 2
            joined = part if joined is None else jnp.where(group_full == p, part, joined)
        for block in range(blocks):
            height[block, tile] = joined[block * SUBLANES : (block + 1) * SUBLANES]
        east_edge.append(jnp.broadcast_to(joined[columns : columns + 1], (SUBLANES, LANES)))
        west_edge.append(
            jnp.broadcast_to(joined[columns + 1 : columns + 2], (SUBLANES, LANES))
        )
    height_east = shift_columns(height, 1, east_edge, blocks, count)
    height_north = shift_rows(height, 1, blocks, count)
    flow_east = {p: -BARO_GAIN * (height_east[p] - height[p]) for p in places}
    flow_north = {p: -BARO_GAIN * (height_north[p] - height[p]) for p in places}
    flow_west = [
        -BARO_GAIN * (jnp.broadcast_to(height[0, tile][:1], (SUBLANES, LANES)) - west_edge[tile])
        for tile in range(count)
    ]

    def copy(kind):
        return pltpu.make_async_copy(result_ref.at[kind], out_ref.at[kind], sems.at[kind])

    for kind in range(kinds):
        @pl.loop(0, levels, unroll=4)
        def _(level):
            flux_east, flux_north = {}, {}
            for p in places:
                at = (kind, level) + tile_index(p)
                flux_east[p] = flow_east[p] * face_east_ref[at]
                flux_north[p] = flow_north[p] * face_north_ref[at]
            edge = [
                flow_west[tile]
                * jnp.broadcast_to(
                    face_west_ref[level, kind : kind + 1, tile * LANES : (tile + 1) * LANES],
                    (SUBLANES, LANES),
                )
                for tile in range(count)
            ]
            from_west = shift_columns(flux_east, -1, edge, blocks, count)
            from_south = shift_rows(flux_north, -1, blocks, count)
            for p in places:
                at = (kind, level) + tile_index(p)
                result_ref[at] = base_ref[at] + (
                    (from_west[p] - flux_east[p]) + (from_south[p] - flux_north[p])
                )

        copy(kind).start()
    for kind in range(kinds):
        copy(kind).wait()


def body(
    surface_old,
    surface_forcing,
    surface_coeff,
    ocean_mask,
    column_depth,
    east_depth,
    tracers,
    u_clinic,
    v_clinic,
):
    band, width = surface_old.shape
    kinds, levels, columns, rows = tracers.shape
    count = lax.axis_size("lon")
    f32 = jnp.float32
    sds = jax.ShapeDtypeStruct
    vmem = pl.BlockSpec(memory_space=pltpu.VMEM)
    fields = (surface_old, surface_forcing, surface_coeff, ocean_mask)
    forward = [(i, i + 1) for i in range(count - 1)]
    backward = [(target, source) for source, target in forward]
    ring = [(i, (i + 1) % count) for i in range(count)]
    ring_back = [(target, source) for source, target in ring]

    def call(kernel, out_shape, name, operands, scratch=(), limit=SMALL_VMEM, cost=0):
        return pl.pallas_call(
            kernel,
            out_shape=out_shape,
            in_specs=[vmem] * len(operands),
            out_specs=[pl.BlockSpec(memory_space=pl.ANY) if x is result else vmem for x in out_shape],
            scratch_shapes=list(scratch),
            compiler_params=pltpu.CompilerParams(vmem_limit_bytes=limit),
            cost_estimate=pl.CostEstimate(
                flops=cost * tracers.size, bytes_accessed=8 * tracers.size, transcendentals=0
            )
            if cost
            else None,
            name=name,
        )(*operands)

    result = sds(tracers.shape, f32)
    packed = sds((3 * HALO, width), f32)
    held = pltpu.VMEM(tracers.shape, f32)

    low, high = call(pack_kernel, (packed, packed), "pack_edges", fields)
    below = lax.ppermute(high, "lon", forward)
    above = lax.ppermute(low, "lon", backward)

    folded, east_going, own_west = call(
        edge_kernel,
        (
            packed,
            sds((2 * levels + levels // SUBLANES + 1, kinds, rows), f32),
            sds((2 * levels, kinds, rows), f32),
        ),
        "pack_tracer_edges",
        (high, tracers, column_depth, east_depth, u_clinic),
    )
    from_west = lax.ppermute(east_going, "lon", ring)
    from_east = lax.ppermute(own_west, "lon", ring_back)
    (base,) = call(source_kernel, (held,), "sources", (tracers, column_depth), cost=70)

    groups = count // 4
    half_slabs = sds((count // 2, SLAB_ROWS, LANES), f32)
    keep, send, basis = call(
        basis_kernel,
        (half_slabs, half_slabs, sds((BASIS * band, width), f32)),
        "solver_basis",
        fields + (below, above, folded, base),
    )
    came = lax.ppermute(send, "lon", [(i, i ^ 1) for i in range(count)])
    quarter = sds((groups, 2, SLAB_ROWS, LANES), f32)
    keep, send = call(split_kernel, (quarter, quarter), "split_slabs", (keep, came))
    came = lax.ppermute(send, "lon", [(i, i ^ 2) for i in range(count)])
    base, face_north = call(
        north_kernel,
        (held, held),
        "north_fluxes",
        (tracers, column_depth, v_clinic, base, keep),
        scratch=[pltpu.VMEM((columns, rows), jnp.int32)],
        cost=70,
    )
    sends = call(
        spread_kernel,
        (sds((4, SLAB_ROWS, LANES), f32),) * groups,
        "spread_slabs",
        (keep, came),
    )
    slabs = [sends[0]]
    for step in range(1, groups):
        pairs = [(i, (i + 4 * step) % count) for i in range(count)]
        slabs.append(lax.ppermute(sends[step], "lon", pairs))
    base, face_east, face_west = call(
        east_kernel,
        (held, held, pltpu.VMEM((levels, kinds, rows), f32)),
        "east_fluxes",
        (
            tracers,
            column_depth,
            east_depth,
            u_clinic,
            from_west,
            from_east,
            own_west,
            base,
            sends[0],
        ),
        scratch=[pltpu.VMEM((levels, kinds, rows), f32)],
        cost=70,
    )
    return tuple(
        call(
            functools.partial(update_kernel, groups),
            (sds((band, width), f32), result),
            "surface_update",
            (*slabs, basis, base, face_east, face_north, face_west),
            scratch=[
                pltpu.VMEM((count, SLAB_ROWS, LANES), f32),
                pltpu.VMEM(tracers.shape, f32),
                pltpu.SemaphoreType.DMA((kinds,)),
            ],
            limit=RESULT_VMEM,
        )
    )


def solution(mesh):
    in_specs = (
        P(("member", "lon"), None),
        P(("member", "lon"), None),
        P("lon", None),
        P("lon", None),
        P("lon", None),
        P("lon", None),
        P("member", None, "lon", None),
        P("member", "lon", None),
        P("member", "lon", None),
    )
    out_specs = (P(("member", "lon"), None), P("member", None, "lon", None))
    return jax.shard_map(body, mesh=mesh, in_specs=in_specs, out_specs=out_specs, check_vma=False)
```

```python
import jax
import jax.numpy as jnp
from jax import lax
from jax.experimental import pallas as pl
from jax.experimental.pallas import tpu as pltpu
from jax.sharding import PartitionSpec as P

BARO_GAIN = 0.1
HORIZ_DIFF = 0.1
VERT_DIFF = 0.15
RATE_CARBON = 0.3
RATE_AMMONIUM = 0.2
RATE_NITRITE = 0.2
RATE_SULFIDE = 0.3
RATE_NITROUS = 0.2
HALF_OXYGEN = 0.3
HALF_NITRATE = 0.3
HALF_NITRITE = 0.3
YIELD_NITROUS = 0.3


SUBLANES = 8
LANES = 128
SMALL_VMEM = 4 * 2**20
RESULT_VMEM = 14 * 2**20
HALO = 8
SLAB_ROWS = 24
BASIS = 4
CENTRE = 4.55
SPREAD = 4.45
PIVOT_FLOOR = 3e-7


def pack_kernel(old_in, force_in, coeff_in, mask_in, low_ref, high_ref, own_ref, *scratch):
    old_ref, force_ref, coeff_ref, mask_ref, sems = scratch
    copies = [
        pltpu.make_async_copy(source, target, sems.at[place])
        for place, (source, target) in enumerate(
            zip((old_in, force_in, coeff_in, mask_in), (old_ref, force_ref, coeff_ref, mask_ref))
        )
    ]
    for copy in copies:
        copy.start()
    for copy in copies:
        copy.wait()
    rows = old_ref.shape[0]
    coeff = coeff_ref[...]
    fields = (
        coeff * old_ref[...] + force_ref[...],
        coeff,
        mask_ref[...].astype(jnp.float32),
    )
    for place, field in enumerate(fields):
        low_ref[HALO * place : HALO * (place + 1)] = field[:HALO]
        high_ref[HALO * place : HALO * (place + 1)] = field[rows - HALO :]
        own_ref[rows * place : rows * (place + 1)] = field


def basis_kernel(
    own_ref,
    below_ref,
    above_ref,
    folded_ref,
    basis_ref,
    *refs,
):
    send_refs, slabs_ref = refs[:-1], refs[-1]
    rows, width = own_ref.shape[0] // 3, own_ref.shape[1]
    count = slabs_ref.shape[0]
    columns = width // count
    top_device = lax.axis_index("lon") == count - 1
    above = jnp.where(top_device, folded_ref[...], above_ref[...])

    def extended(place):
        part = slice(HALO * place, HALO * (place + 1))
        own = own_ref[rows * place : rows * (place + 1)]
        return jnp.concatenate([below_ref[part], own, above[part]], axis=0)

    first, coeff, mask = extended(0), extended(1), extended(2)
    diagonal = (coeff + 4.0 * mask - CENTRE) * (1.0 / SPREAD)
    beside = mask * (1.0 / SPREAD)
    total = rows + 2 * HALO

    def scaled(values):
        masked = mask * values
        around = (
            pltpu.roll(masked, total - 1, 0)
            + pltpu.roll(masked, 1, 0)
            + pltpu.roll(masked, width - 1, 1)
            + pltpu.roll(masked, 1, 1)
        )
        return diagonal * values - beside * around

    vectors = [first, scaled(first)]
    while len(vectors) < BASIS + 1:
        vectors.append(2.0 * scaled(vectors[-1]) - vectors[-2])
    own = [vector[HALO : HALO + rows] for vector in vectors]
    sums = []
    for order in range(2 * BASIS):
        product = own[order // 2] * own[(order + 1) // 2]
        sums.append(jnp.sum(product, axis=0, keepdims=True))
    partial = jnp.sum(jnp.concatenate(sums, axis=0), axis=1, keepdims=True)
    lane = lax.broadcasted_iota(jnp.int32, (2 * BASIS, LANES), 1)
    place = lax.broadcasted_iota(jnp.int32, (2 * BASIS, LANES), 0)
    moments = jnp.sum(jnp.where(lane == place, partial, 0.0), axis=0, keepdims=True)
    stacked = jnp.concatenate(own[:BASIS], axis=0)
    basis_ref[...] = stacked
    if BASIS * rows < LANES:
        stacked = jnp.concatenate(
            [stacked, jnp.zeros((LANES - BASIS * rows, width), jnp.float32)], axis=0
        )
    turned = stacked.T
    for target in range(count):
        start = target * columns
        east = (start + columns) % width
        west = (start - 1) % width
        pieces = [
            turned[start : start + columns],
            turned[east : east + 1],
            turned[west : west + 1],
            moments,
            jnp.zeros((SLAB_ROWS - columns - 3, LANES), jnp.float32),
        ]
        slabs_ref[target] = jnp.concatenate(pieces, axis=0)
    groups = len(send_refs)
    group = lax.axis_index("lon") // 4
    for step in range(groups):
        target = lax.rem(group + step, groups)
        for place in range(4):
            send_refs[step][place] = slabs_ref[4 * target + place]


def core_kernel(*refs):
    came_refs, (_, keep_ref, send_ref) = refs[:-3], refs[-3:]
    here = lax.axis_index("lon")
    core, group = lax.rem(here, 2), here // 4
    groups = len(came_refs)
    for step in range(groups):
        source = lax.rem(group + groups - step, groups)
        for y in range(2):
            keep_ref[y, source] = came_refs[step][2 * y + core]
            send_ref[y, source] = came_refs[step][2 * y + 1 - core]


def half_kernel(kept_ref, came_ref, keep_ref, send_ref):
    here = lax.axis_index("lon")
    core, half = lax.rem(here, 2), lax.rem(here // 2, 2)
    keep_ref[core] = kept_ref[half]
    keep_ref[1 - core] = came_ref[half]
    send_ref[core] = kept_ref[1 - half]
    send_ref[1 - core] = came_ref[1 - half]


def basis_weights(moments):
    gram = {}

    def inner(i, j):
        key = (i + j, abs(i - j))
        if key not in gram:
            gram[key] = 0.5 * (moments[i + j] + moments[abs(i - j)])
        return gram[key]

    matrix = [[None] * BASIS for _ in range(BASIS)]
    for i in range(BASIS):
        for j in range(i + 1):
            if i == 0:
                image = moments[1]
            elif j == 0:
                image = inner(1, i)
            else:
                image = 0.5 * (inner(i, j + 1) + inner(i, j - 1))
            matrix[i][j] = CENTRE * inner(i, j) + SPREAD * image
    right = [inner(i, 0) for i in range(BASIS)]
    start = [matrix[i][i] for i in range(BASIS)]
    inverse = []
    factors = [[None] * BASIS for _ in range(BASIS)]
    for n in range(BASIS):
        pivot = matrix[n][n]
        inverse.append(jnp.where(pivot > PIVOT_FLOOR * start[n], 1.0 / pivot, 0.0))
        for i in range(n + 1, BASIS):
            factors[i][n] = matrix[i][n] * inverse[n]
        for i in range(n + 1, BASIS):
            for j in range(n + 1, i + 1):
                matrix[i][j] = matrix[i][j] - factors[i][n] * matrix[j][n]
            right[i] = right[i] - factors[i][n] * right[n]
    weights = [None] * BASIS
    for n in reversed(range(BASIS)):
        value = right[n] * inverse[n]
        for i in range(n + 1, BASIS):
            value = value - factors[i][n] * weights[i]
        weights[n] = value
    return weights


def reverse_tile(tile):
    for axis, size in ((0, SUBLANES), (1, LANES)):
        place = lax.broadcasted_iota(jnp.int32, (SUBLANES, LANES), axis)
        step = size // 2
        while step:
            tile = jnp.where(
                (place & step) != 0,
                pltpu.roll(tile, step, axis),
                pltpu.roll(tile, size - step, axis),
            )
            step //= 2
    return tile


def load_kernel(
    high_ref,
    tracers_in,
    depth_in,
    east_depth_in,
    u_in,
    v_in,
    folded_ref,
    tracers_ref,
    depth_ref,
    east_depth_ref,
    u_ref,
    v_ref,
    sems,
):
    kinds = tracers_ref.shape[0]
    copies = [
        pltpu.make_async_copy(source, target, sems.at[place])
        for place, (source, target) in enumerate(
            [
                (depth_in, depth_ref),
                (east_depth_in, east_depth_ref),
                (u_in, u_ref),
                (v_in, v_ref),
            ]
            + [(tracers_in.at[kind], tracers_ref.at[kind]) for kind in range(kinds)]
        )
    ]
    for copy in copies:
        copy.start()
    tiles = high_ref.shape[1] // LANES
    for place in range(3):
        part = slice(HALO * place, HALO * (place + 1))
        for tile in range(tiles):
            other = tiles - 1 - tile
            folded_ref[part, tile * LANES : (tile + 1) * LANES] = reverse_tile(
                high_ref[part, other * LANES : (other + 1) * LANES]
            )
    for copy in copies:
        copy.wait()


def edge_kernel(
    tracers_ref, depth_ref, east_depth_ref, u_ref, _, east_going_ref, west_going_ref
):
    kinds, levels, columns, rows = tracers_ref.shape
    for z in range(levels):
        place = 2 * levels + z // SUBLANES
        row = z % SUBLANES
        east_going_ref[place, row : row + 1] = u_ref[z, columns - 1 : columns]
    place = 2 * levels + levels // SUBLANES
    east_going_ref[place] = jnp.broadcast_to(
        east_depth_ref[columns - 1 : columns].astype(jnp.float32), (SUBLANES, rows)
    )
    for kind in range(kinds):
        for z in range(levels):
            for side in range(2):
                column = columns - 2 + side
                west_wet = (z < depth_ref[side : side + 1]).astype(jnp.float32)
                east_wet = (z < depth_ref[column : column + 1]).astype(jnp.float32)
                west_going_ref[2 * z + side, kind : kind + 1] = (
                    tracers_ref[kind, z, side : side + 1] * west_wet
                )
                east_going_ref[2 * z + side, kind : kind + 1] = (
                    tracers_ref[kind, z, column : column + 1] * east_wet
                )


def grid_tiles(columns, rows):
    return [
        (block, tile)
        for block in range(columns // SUBLANES)
        for tile in range(rows // LANES)
    ]


def tile_index(place):
    block, tile = place
    return (
        slice(block * SUBLANES, (block + 1) * SUBLANES),
        slice(tile * LANES, (tile + 1) * LANES),
    )


def shift_columns(tiles, step, outer, blocks, count):
    sublane = lax.broadcasted_iota(jnp.int32, (SUBLANES, LANES), 0)
    turned = {p: pltpu.roll(x, SUBLANES - 1 if step > 0 else 1, 0) for p, x in tiles.items()}
    inside = sublane < SUBLANES - 1 if step > 0 else sublane > 0
    shifted = {}
    for block in range(blocks):
        for tile in range(count):
            beyond = block + step
            other = turned[beyond, tile] if 0 <= beyond < blocks else outer[tile]
            shifted[block, tile] = jnp.where(inside, turned[block, tile], other)
    return shifted


def shift_rows(tiles, step, blocks, count):
    lane = lax.broadcasted_iota(jnp.int32, (SUBLANES, LANES), 1)
    turned = {p: pltpu.roll(x, LANES - 1 if step > 0 else 1, 1) for p, x in tiles.items()}
    inside = lane < LANES - 1 if step > 0 else lane > 0
    shifted = {}
    for block in range(blocks):
        for tile in range(count):
            beyond = tile + step
            other = turned[block, beyond] if 0 <= beyond < count else 0.0
            shifted[block, tile] = jnp.where(inside, turned[block, tile], other)
    return shifted


def reciprocal(value):
    guess = pl.reciprocal(value, approx=True)
    return guess * (2.0 - value * guess)


def redox_sources(masked):
    oxygen, nitrate, nitrite, ammonium, _, carbon, sulfide, nitrous = masked
    over_oxygen = reciprocal(oxygen + HALF_OXYGEN)
    with_oxygen = oxygen * over_oxygen
    no_oxygen = HALF_OXYGEN * over_oxygen
    with_nitrate = no_oxygen * nitrate * reciprocal(nitrate + HALF_NITRATE)
    rest = no_oxygen - with_nitrate
    with_nitrite = rest * nitrite * reciprocal(nitrite + HALF_NITRITE)
    with_sulfate = rest - with_nitrite
    breakdown = RATE_CARBON * carbon
    first_nitr = RATE_AMMONIUM * ammonium * with_oxygen
    second_nitr = RATE_NITRITE * nitrite * with_oxygen
    sulfide_ox = RATE_SULFIDE * sulfide * with_oxygen
    by_nitrate = 0.9 * breakdown * with_nitrate
    return (
        -1.3 * breakdown * with_oxygen - 1.5 * first_nitr - 0.5 * second_nitr - 2.0 * sulfide_ox,
        second_nitr - by_nitrate,
        by_nitrate
        - 0.6 * breakdown * with_nitrite
        + (1.0 - YIELD_NITROUS) * first_nitr
        - second_nitr,
        0.15 * breakdown - first_nitr,
        0.1 * breakdown,
        -breakdown,
        0.5 * breakdown * with_sulfate - sulfide_ox,
        YIELD_NITROUS * first_nitr - RATE_NITROUS * nitrous * no_oxygen,
    )


def source_kernel(tracers_ref, depth_ref, _, base_ref):
    kinds, levels, columns, rows = tracers_ref.shape
    places = grid_tiles(columns, rows)

    @pl.loop(0, levels)
    def _(level):
        above = jnp.maximum(level - 1, 0)
        below = jnp.minimum(level + 1, levels - 1)
        mix_up_level = jnp.where(level > 0, VERT_DIFF, 0.0)
        for p in places:
            at = tile_index(p)
            depth_here = depth_ref[at]
            wet = jnp.where(level < depth_here, 1.0, 0.0)
            mix_up = wet * mix_up_level
            mix_down = jnp.where(level + 1 < depth_here, VERT_DIFF, 0.0)
            values = [tracers_ref[(kind, level) + at] for kind in range(kinds)]
            sources = redox_sources([value * wet for value in values])
            for kind in range(kinds):
                value = values[kind]
                down = (tracers_ref[(kind, below) + at] - value) * mix_down
                up = (value - tracers_ref[(kind, above) + at]) * mix_up
                base_ref[(kind, level) + at] = value + (wet * sources[kind] + (down - up))


def north_kernel(
    tracers_ref,
    depth_ref,
    v_ref,
    before_ref,
    base_ref,
    face_ref,
    face_south_ref,
    band_ref,
    north_ref,
    south_ref,
):
    kinds, levels, columns, rows = tracers_ref.shape
    blocks, count = columns // SUBLANES, rows // LANES
    places = grid_tiles(columns, rows)
    source = lax.broadcasted_iota(jnp.int32, (rows, rows), 0)
    target = lax.broadcasted_iota(jnp.int32, (rows, rows), 1)
    for place, moved in enumerate((0, 1)):
        offset = source - target + moved
        near = (offset == 0) | (offset == 1)
        far = (offset == -1) | (offset == 2)
        band = jnp.where(near, 7.0, jnp.where(far, -1.0, 0.0))
        band_ref[:, place * rows : (place + 1) * rows] = band.astype(jnp.bfloat16)
    depth = {p: depth_ref[tile_index(p)].astype(jnp.float32) for p in places}
    depth_north = shift_rows(depth, 1, blocks, count)
    depth_south = shift_rows(depth, -1, blocks, count)
    for p in places:
        at = tile_index(p)
        north_ref[at] = jnp.minimum(depth[p], depth_north[p]).astype(jnp.int32)
        south_ref[at] = jnp.minimum(depth[p], depth_south[p]).astype(jnp.int32)

    @pl.loop(0, levels)
    def _(level):
        wet, scale, mix, scale_s, mix_s, flow = {}, {}, {}, {}, {}, {}
        for p in places:
            at = tile_index(p)
            wet[p] = jnp.where(level < depth_ref[at], 1.0, 0.0)
            is_open = level < north_ref[at]
            scale[p] = jnp.where(is_open, 1.0 / 12.0, 0.0)
            mix[p] = jnp.where(is_open, HORIZ_DIFF, 0.0)
            is_open = level < south_ref[at]
            scale_s[p] = jnp.where(is_open, 1.0 / 12.0, 0.0)
            mix_s[p] = jnp.where(is_open, HORIZ_DIFF, 0.0)
            flow[p] = v_ref[(level,) + at]
        flow_s = shift_rows(flow, -1, blocks, count)
        wet_full = jnp.where(level < depth_ref[...], 1.0, 0.0)
        masked_full = [tracers_ref[kind, level] * wet_full for kind in range(kinds)]
        whole = jnp.concatenate(masked_full, axis=0)
        first = whole.astype(jnp.bfloat16)
        second = (whole - first.astype(jnp.float32)).astype(jnp.bfloat16)
        weights = band_ref[...]
        faces = jnp.dot(first, weights, preferred_element_type=jnp.float32) + jnp.dot(
            second, weights, preferred_element_type=jnp.float32
        )
        for kind in range(kinds):
            masked = {p: masked_full[kind][tile_index(p)] for p in places}
            north = shift_rows(masked, 1, blocks, count)
            south = shift_rows(masked, -1, blocks, count)
            for p in places:
                rows_at, lanes_at = tile_index(p)
                at = (kind, level, rows_at, lanes_at)
                row = kind * columns + rows_at.start
                picked = faces[row : row + SUBLANES]
                face = picked[:, lanes_at] * scale[p]
                face_south = (
                    picked[:, rows + lanes_at.start : rows + lanes_at.stop] * scale_s[p]
                )
                face_ref[at] = face
                face_south_ref[at] = face_south
                flux = flow[p] * face - mix[p] * (north[p] - masked[p])
                flux_south = flow_s[p] * face_south - mix_s[p] * (masked[p] - south[p])
                base_ref[at] = before_ref[at] + (flux_south - flux)


def east_kernel(
    tracers_ref,
    depth_ref,
    east_depth_ref,
    u_ref,
    from_west_ref,
    from_east_ref,
    own_west_ref,
    before_ref,
    _,
    base_ref,
    face_east_ref,
    face_west_ref,
    flux_west_ref,
):
    kinds, levels, columns, rows = tracers_ref.shape
    blocks, count = columns // SUBLANES, rows // LANES
    places = grid_tiles(columns, rows)
    depth_west = from_west_ref[2 * levels + levels // SUBLANES]
    for z in range(levels):
        row = z % SUBLANES
        u_west = from_west_ref[2 * levels + z // SUBLANES, row : row + 1]
        center, east_one = from_west_ref[2 * z + 1], own_west_ref[2 * z]
        outer = from_west_ref[2 * z] + own_west_ref[2 * z + 1]
        scale_west = jnp.where(z < depth_west, 1.0 / 12.0, 0.0)
        mix_west = jnp.where(z < depth_west, HORIZ_DIFF, 0.0)
        face = (7.0 * (center + east_one) - outer) * scale_west
        face_west_ref[z] = face
        flux_west_ref[z] = u_west * face - mix_west * (east_one - center)

    @pl.loop(0, levels)
    def _(level):
        wet, scale, mix = {}, {}, {}
        for p in places:
            at = tile_index(p)
            wet[p] = jnp.where(level < depth_ref[at], 1.0, 0.0)
            is_open = level < east_depth_ref[at]
            scale[p] = jnp.where(is_open, 1.0 / 12.0, 0.0)
            mix[p] = jnp.where(is_open, HORIZ_DIFF, 0.0)
        for kind in range(kinds):
            def halo(ref, index):
                return [
                    jnp.broadcast_to(
                        ref[index, kind : kind + 1, tile * LANES : (tile + 1) * LANES],
                        (SUBLANES, LANES),
                    )
                    for tile in range(count)
                ]

            masked = {p: tracers_ref[(kind, level) + tile_index(p)] * wet[p] for p in places}
            one = shift_columns(masked, 1, halo(from_east_ref, 2 * level), blocks, count)
            two = shift_columns(one, 1, halo(from_east_ref, 2 * level + 1), blocks, count)
            west = shift_columns(masked, -1, halo(from_west_ref, 2 * level + 1), blocks, count)
            flux = {}
            for p in places:
                at = (kind, level) + tile_index(p)
                face = (7.0 * (masked[p] + one[p]) - (west[p] + two[p])) * scale[p]
                face_east_ref[at] = face
                flux[p] = u_ref[(level,) + tile_index(p)] * face - mix[p] * (one[p] - masked[p])
            incoming = shift_columns(flux, -1, halo(flux_west_ref, level), blocks, count)
            for p in places:
                at = (kind, level) + tile_index(p)
                base_ref[at] = before_ref[at] + (incoming[p] - flux[p])


def update_kernel(
    kept_ref,
    came_ref,
    basis_ref,
    base_ref,
    face_east_ref,
    face_north_ref,
    face_south_ref,
    face_west_ref,
    surface_ref,
    out_ref,
    slabs_ref,
    result_ref,
    sems,
):
    half = lax.rem(lax.axis_index("lon") // 2, 2)
    for source in range(kept_ref.shape[1]):
        for core in range(2):
            slabs_ref[4 * source + 2 * half + core] = kept_ref[core, source]
            slabs_ref[4 * source + 2 * (1 - half) + core] = came_ref[core, source]
    kinds, levels, columns, rows = base_ref.shape
    blocks, count = columns // SUBLANES, rows // LANES
    places = grid_tiles(columns, rows)
    sources, slab_rows, _ = slabs_ref.shape
    band, width = surface_ref.shape
    moment_row = slabs_ref[0, columns + 2 : columns + 3]
    for source in range(1, sources):
        moment_row = moment_row + slabs_ref[source, columns + 2 : columns + 3]
    dots = [moment_row[:, m : m + 1] for m in range(2 * BASIS)]
    weights = basis_weights(
        dots[:2] + [2.0 * dots[m] - dots[m % 2] for m in range(2, 2 * BASIS)]
    )
    lane_group = lax.broadcasted_iota(jnp.int32, (1, LANES), 1) // band
    lane_weight = jnp.zeros((1, LANES), jnp.float32)
    for k in range(BASIS):
        lane_weight = jnp.where(lane_group == k, weights[k], lane_weight)
    surface = weights[0] * basis_ref[:band]
    for k in range(1, BASIS):
        surface = surface + weights[k] * basis_ref[k * band : (k + 1) * band]
    surface_ref[...] = surface

    fill = LANES // band
    group_full = lax.broadcasted_iota(jnp.int32, (slab_rows, LANES), 1) // band
    height, east_edge, west_edge = {}, [], []
    for tile in range(count):
        joined = None
        for p in range(fill):
            part = slabs_ref[tile * fill + p] * lane_weight
            shift = LANES // 2
            while shift >= band:
                part = part + pltpu.roll(part, shift, 1)
                shift //= 2
            joined = part if joined is None else jnp.where(group_full == p, part, joined)
        for block in range(blocks):
            height[block, tile] = joined[block * SUBLANES : (block + 1) * SUBLANES]
        east_edge.append(jnp.broadcast_to(joined[columns : columns + 1], (SUBLANES, LANES)))
        west_edge.append(
            jnp.broadcast_to(joined[columns + 1 : columns + 2], (SUBLANES, LANES))
        )
    height_east = shift_columns(height, 1, east_edge, blocks, count)
    height_north = shift_rows(height, 1, blocks, count)
    flow_east = {p: -BARO_GAIN * (height_east[p] - height[p]) for p in places}
    flow_north = {p: -BARO_GAIN * (height_north[p] - height[p]) for p in places}
    flow_south = shift_rows(flow_north, -1, blocks, count)
    flow_west = [
        -BARO_GAIN * (jnp.broadcast_to(height[0, tile][:1], (SUBLANES, LANES)) - west_edge[tile])
        for tile in range(count)
    ]

    def copy(kind):
        return pltpu.make_async_copy(result_ref.at[kind], out_ref.at[kind], sems.at[kind])

    for kind in range(kinds):
        @pl.loop(0, levels, unroll=4)
        def _(level):
            flux_east = {
                p: flow_east[p] * face_east_ref[(kind, level) + tile_index(p)] for p in places
            }
            edge = [
                flow_west[tile]
                * jnp.broadcast_to(
                    face_west_ref[level, kind : kind + 1, tile * LANES : (tile + 1) * LANES],
                    (SUBLANES, LANES),
                )
                for tile in range(count)
            ]
            from_west = shift_columns(flux_east, -1, edge, blocks, count)
            for p in places:
                at = (kind, level) + tile_index(p)
                result_ref[at] = base_ref[at] + (
                    (from_west[p] - flux_east[p])
                    + (flow_south[p] * face_south_ref[at] - flow_north[p] * face_north_ref[at])
                )

        copy(kind).start()
    for kind in range(kinds):
        copy(kind).wait()


def body(
    surface_old,
    surface_forcing,
    surface_coeff,
    ocean_mask,
    column_depth,
    east_depth,
    tracers,
    u_clinic,
    v_clinic,
):
    band, width = surface_old.shape
    kinds, levels, columns, rows = tracers.shape
    count = lax.axis_size("lon")
    f32 = jnp.float32
    sds = jax.ShapeDtypeStruct
    vmem = pl.BlockSpec(memory_space=pltpu.VMEM)
    hbm = pl.BlockSpec(memory_space=pltpu.HBM)
    fields = (surface_old, surface_forcing, surface_coeff, ocean_mask)
    forward = [(i, i + 1) for i in range(count - 1)]
    backward = [(target, source) for source, target in forward]
    ring = [(i, (i + 1) % count) for i in range(count)]
    ring_back = [(target, source) for source, target in ring]

    def call(
        kernel, out_shape, name, operands, scratch=(), limit=SMALL_VMEM, cost=0, far=()
    ):
        return pl.pallas_call(
            kernel,
            out_shape=out_shape,
            in_specs=[hbm if place in far else vmem for place in range(len(operands))],
            out_specs=[pl.BlockSpec(memory_space=pl.ANY) if x is result else vmem for x in out_shape],
            scratch_shapes=list(scratch),
            compiler_params=pltpu.CompilerParams(vmem_limit_bytes=limit),
            cost_estimate=pl.CostEstimate(
                flops=cost * tracers.size, bytes_accessed=8 * tracers.size, transcendentals=0
            )
            if cost
            else None,
            name=name,
        )(
            *(
                pltpu.with_memory_space_constraint(x, pltpu.HBM) if place in far else x
                for place, x in enumerate(operands)
            )
        )

    result = sds(tracers.shape, f32)
    packed = sds((3 * HALO, width), f32)
    held = pltpu.VMEM(tracers.shape, f32)

    low, high, own = call(
        pack_kernel,
        (packed, packed, sds((3 * band, width), f32)),
        "pack_edges",
        fields,
        scratch=[pltpu.VMEM(x.shape, x.dtype) for x in fields] + [pltpu.SemaphoreType.DMA((4,))],
        far=range(4),
    )
    below = lax.ppermute(high, "lon", forward)
    above = lax.ppermute(low, "lon", backward)

    def fetched(x):
        return pltpu.VMEM(x.shape, x.dtype)

    inputs = (tracers, column_depth, east_depth, u_clinic, v_clinic)
    folded, tracers, column_depth, east_depth, u_clinic, v_clinic = call(
        load_kernel,
        (
            packed,
            *(fetched(x) for x in inputs),
        ),
        "load",
        (high, *inputs),
        scratch=[pltpu.SemaphoreType.DMA((4 + kinds,))],
        far=range(1, 6),
    )
    groups = count // 4
    basis, *sends = call(
        basis_kernel,
        (sds((BASIS * band, width), f32),) + (sds((4, SLAB_ROWS, LANES), f32),) * groups,
        "solver_basis",
        (own, below, above, folded),
        scratch=[pltpu.VMEM((count, SLAB_ROWS, LANES), f32)],
    )
    slabs = [sends[0]]
    for step in range(1, groups):
        pairs = [(i, (i + 4 * step) % count) for i in range(count)]
        slabs.append(lax.ppermute(sends[step], "lon", pairs))
    east_going, own_west = call(
        edge_kernel,
        (
            sds((2 * levels + levels // SUBLANES + 1, kinds, rows), f32),
            sds((2 * levels, kinds, rows), f32),
        ),
        "pack_tracer_edges",
        (tracers, column_depth, east_depth, u_clinic, basis),
    )
    from_west = lax.ppermute(east_going, "lon", ring)
    from_east = lax.ppermute(own_west, "lon", ring_back)
    (base,) = call(source_kernel, (held,), "sources", (tracers, column_depth, own_west), cost=70)
    base, face_north, face_south = call(
        north_kernel,
        (held, held, held),
        "north_fluxes",
        (tracers, column_depth, v_clinic, base),
        scratch=[
            pltpu.VMEM((rows, 2 * rows), jnp.bfloat16),
            pltpu.VMEM((columns, rows), jnp.int32),
            pltpu.VMEM((columns, rows), jnp.int32),
        ],
        cost=70,
    )
    quarter = sds((2, groups, SLAB_ROWS, LANES), f32)
    keep, send = call(core_kernel, (quarter, quarter), "split_cores", (*slabs, base))
    came = lax.ppermute(send, "lon", [(i, i ^ 1) for i in range(count)])
    keep, send = call(half_kernel, (quarter, quarter), "split_halves", (keep, came))
    came = lax.ppermute(send, "lon", [(i, i ^ 2) for i in range(count)])
    base, face_east, face_west = call(
        east_kernel,
        (held, held, pltpu.VMEM((levels, kinds, rows), f32)),
        "east_fluxes",
        (
            tracers,
            column_depth,
            east_depth,
            u_clinic,
            from_west,
            from_east,
            own_west,
            base,
            keep,
        ),
        scratch=[pltpu.VMEM((levels, kinds, rows), f32)],
        cost=70,
    )
    return tuple(
        call(
            update_kernel,
            (sds((band, width), f32), result),
            "surface_update",
            (keep, came, basis, base, face_east, face_north, face_south, face_west),
            scratch=[
                pltpu.VMEM((count, SLAB_ROWS, LANES), f32),
                pltpu.VMEM(tracers.shape, f32),
                pltpu.SemaphoreType.DMA((kinds,)),
            ],
            limit=RESULT_VMEM,
        )
    )


def solution(mesh):
    in_specs = (
        P(("member", "lon"), None),
        P(("member", "lon"), None),
        P("lon", None),
        P("lon", None),
        P("lon", None),
        P("lon", None),
        P("member", None, "lon", None),
        P("member", "lon", None),
        P("member", "lon", None),
    )
    out_specs = (P(("member", "lon"), None), P("member", None, "lon", None))
    return jax.shard_map(body, mesh=mesh, in_specs=in_specs, out_specs=out_specs, check_vma=False)
```

```python
import jax
import jax.numpy as jnp
from jax import lax
from jax.experimental import pallas as pl
from jax.experimental.pallas import tpu as pltpu
from jax.sharding import PartitionSpec as P

BARO_GAIN = 0.1
HORIZ_DIFF = 0.1
VERT_DIFF = 0.15
RATE_CARBON = 0.3
RATE_AMMONIUM = 0.2
RATE_NITRITE = 0.2
RATE_SULFIDE = 0.3
RATE_NITROUS = 0.2
HALF_OXYGEN = 0.3
HALF_NITRATE = 0.3
HALF_NITRITE = 0.3
YIELD_NITROUS = 0.3


SUBLANES = 8
LANES = 128
SMALL_VMEM = 4 * 2**20
RESULT_VMEM = 14 * 2**20
HALO = 8
SLAB_ROWS = 24
BASIS = 4
CENTRE = 4.55
SPREAD = 4.45
PIVOT_FLOOR = 3e-7


def pack_kernel(old_in, force_in, coeff_in, mask_in, low_ref, high_ref, own_ref, *scratch):
    old_ref, force_ref, coeff_ref, mask_ref, sems = scratch
    copies = [
        pltpu.make_async_copy(source, target, sems.at[place])
        for place, (source, target) in enumerate(
            zip((old_in, force_in, coeff_in, mask_in), (old_ref, force_ref, coeff_ref, mask_ref))
        )
    ]
    for copy in copies:
        copy.start()
    for copy in copies:
        copy.wait()
    rows = old_ref.shape[0]
    coeff = coeff_ref[...]
    fields = (
        coeff * old_ref[...] + force_ref[...],
        coeff,
        mask_ref[...].astype(jnp.float32),
    )
    for place, field in enumerate(fields):
        low_ref[HALO * place : HALO * (place + 1)] = field[:HALO]
        high_ref[HALO * place : HALO * (place + 1)] = field[rows - HALO :]
        own_ref[rows * place : rows * (place + 1)] = field


def basis_kernel(
    own_ref,
    below_ref,
    above_ref,
    folded_ref,
    basis_ref,
    *refs,
):
    send_refs, slabs_ref = refs[:-1], refs[-1]
    rows, width = own_ref.shape[0] // 3, own_ref.shape[1]
    count = slabs_ref.shape[0]
    columns = width // count
    top_device = lax.axis_index("lon") == count - 1
    above = jnp.where(top_device, folded_ref[...], above_ref[...])

    def extended(place):
        part = slice(HALO * place, HALO * (place + 1))
        own = own_ref[rows * place : rows * (place + 1)]
        return jnp.concatenate([below_ref[part], own, above[part]], axis=0)

    first, coeff, mask = extended(0), extended(1), extended(2)
    diagonal = (coeff + 4.0 * mask - CENTRE) * (1.0 / SPREAD)
    beside = mask * (1.0 / SPREAD)
    total = rows + 2 * HALO

    def scaled(values):
        masked = mask * values
        around = (
            pltpu.roll(masked, total - 1, 0)
            + pltpu.roll(masked, 1, 0)
            + pltpu.roll(masked, width - 1, 1)
            + pltpu.roll(masked, 1, 1)
        )
        return diagonal * values - beside * around

    vectors = [first, scaled(first)]
    while len(vectors) < BASIS + 1:
        vectors.append(2.0 * scaled(vectors[-1]) - vectors[-2])
    own = [vector[HALO : HALO + rows] for vector in vectors]
    sums = []
    for order in range(2 * BASIS):
        product = own[order // 2] * own[(order + 1) // 2]
        sums.append(jnp.sum(product, axis=0, keepdims=True))
    partial = jnp.sum(jnp.concatenate(sums, axis=0), axis=1, keepdims=True)
    lane = lax.broadcasted_iota(jnp.int32, (2 * BASIS, LANES), 1)
    place = lax.broadcasted_iota(jnp.int32, (2 * BASIS, LANES), 0)
    moments = jnp.sum(jnp.where(lane == place, partial, 0.0), axis=0, keepdims=True)
    stacked = jnp.concatenate(own[:BASIS], axis=0)
    basis_ref[...] = stacked
    if BASIS * rows < LANES:
        stacked = jnp.concatenate(
            [stacked, jnp.zeros((LANES - BASIS * rows, width), jnp.float32)], axis=0
        )
    turned = stacked.T
    for target in range(count):
        start = target * columns
        east = (start + columns) % width
        west = (start - 1) % width
        pieces = [
            turned[start : start + columns],
            turned[east : east + 1],
            turned[west : west + 1],
            moments,
            jnp.zeros((SLAB_ROWS - columns - 3, LANES), jnp.float32),
        ]
        slabs_ref[target] = jnp.concatenate(pieces, axis=0)
    groups = len(send_refs)
    group = lax.axis_index("lon") // 4
    for step in range(groups):
        target = lax.rem(group + step, groups)
        for place in range(4):
            send_refs[step][place] = slabs_ref[4 * target + place]


def core_kernel(*refs):
    came_refs, (_, keep_ref, send_ref) = refs[:-3], refs[-3:]
    here = lax.axis_index("lon")
    core, group = lax.rem(here, 2), here // 4
    groups = len(came_refs)
    for step in range(groups):
        source = lax.rem(group + groups - step, groups)
        for y in range(2):
            keep_ref[y, source] = came_refs[step][2 * y + core]
            send_ref[y, source] = came_refs[step][2 * y + 1 - core]


def half_kernel(kept_ref, came_ref, keep_ref, send_ref):
    here = lax.axis_index("lon")
    core, half = lax.rem(here, 2), lax.rem(here // 2, 2)
    keep_ref[core] = kept_ref[half]
    keep_ref[1 - core] = came_ref[half]
    send_ref[core] = kept_ref[1 - half]
    send_ref[1 - core] = came_ref[1 - half]


def basis_weights(moments):
    gram = {}

    def inner(i, j):
        key = (i + j, abs(i - j))
        if key not in gram:
            gram[key] = 0.5 * (moments[i + j] + moments[abs(i - j)])
        return gram[key]

    matrix = [[None] * BASIS for _ in range(BASIS)]
    for i in range(BASIS):
        for j in range(i + 1):
            if i == 0:
                image = moments[1]
            elif j == 0:
                image = inner(1, i)
            else:
                image = 0.5 * (inner(i, j + 1) + inner(i, j - 1))
            matrix[i][j] = CENTRE * inner(i, j) + SPREAD * image
    right = [inner(i, 0) for i in range(BASIS)]
    start = [matrix[i][i] for i in range(BASIS)]
    inverse = []
    factors = [[None] * BASIS for _ in range(BASIS)]
    for n in range(BASIS):
        pivot = matrix[n][n]
        inverse.append(jnp.where(pivot > PIVOT_FLOOR * start[n], 1.0 / pivot, 0.0))
        for i in range(n + 1, BASIS):
            factors[i][n] = matrix[i][n] * inverse[n]
        for i in range(n + 1, BASIS):
            for j in range(n + 1, i + 1):
                matrix[i][j] = matrix[i][j] - factors[i][n] * matrix[j][n]
            right[i] = right[i] - factors[i][n] * right[n]
    weights = [None] * BASIS
    for n in reversed(range(BASIS)):
        value = right[n] * inverse[n]
        for i in range(n + 1, BASIS):
            value = value - factors[i][n] * weights[i]
        weights[n] = value
    return weights


def reverse_tile(tile):
    for axis, size in ((0, SUBLANES), (1, LANES)):
        place = lax.broadcasted_iota(jnp.int32, (SUBLANES, LANES), axis)
        step = size // 2
        while step:
            tile = jnp.where(
                (place & step) != 0,
                pltpu.roll(tile, step, axis),
                pltpu.roll(tile, size - step, axis),
            )
            step //= 2
    return tile


def load_kernel(
    high_ref,
    tracers_in,
    depth_in,
    east_depth_in,
    u_in,
    v_in,
    folded_ref,
    tracers_ref,
    depth_ref,
    east_depth_ref,
    u_ref,
    v_ref,
    sems,
):
    kinds = tracers_ref.shape[0]
    copies = [
        pltpu.make_async_copy(source, target, sems.at[place])
        for place, (source, target) in enumerate(
            [
                (depth_in, depth_ref),
                (east_depth_in, east_depth_ref),
                (u_in, u_ref),
                (v_in, v_ref),
            ]
            + [(tracers_in.at[kind], tracers_ref.at[kind]) for kind in range(kinds)]
        )
    ]
    for copy in copies:
        copy.start()
    tiles = high_ref.shape[1] // LANES
    for place in range(3):
        part = slice(HALO * place, HALO * (place + 1))
        for tile in range(tiles):
            other = tiles - 1 - tile
            folded_ref[part, tile * LANES : (tile + 1) * LANES] = reverse_tile(
                high_ref[part, other * LANES : (other + 1) * LANES]
            )
    for copy in copies:
        copy.wait()


def edge_kernel(
    tracers_ref, depth_ref, east_depth_ref, u_ref, _, east_going_ref, west_going_ref
):
    kinds, levels, columns, rows = tracers_ref.shape
    for z in range(levels):
        place = 2 * levels + z // SUBLANES
        row = z % SUBLANES
        east_going_ref[place, row : row + 1] = u_ref[z, columns - 1 : columns]
    place = 2 * levels + levels // SUBLANES
    east_going_ref[place] = jnp.broadcast_to(
        east_depth_ref[columns - 1 : columns].astype(jnp.float32), (SUBLANES, rows)
    )
    for kind in range(kinds):
        for z in range(levels):
            for side in range(2):
                column = columns - 2 + side
                west_wet = (z < depth_ref[side : side + 1]).astype(jnp.float32)
                east_wet = (z < depth_ref[column : column + 1]).astype(jnp.float32)
                west_going_ref[2 * z + side, kind : kind + 1] = (
                    tracers_ref[kind, z, side : side + 1] * west_wet
                )
                east_going_ref[2 * z + side, kind : kind + 1] = (
                    tracers_ref[kind, z, column : column + 1] * east_wet
                )


def grid_tiles(columns, rows):
    return [
        (block, tile)
        for block in range(columns // SUBLANES)
        for tile in range(rows // LANES)
    ]


def tile_index(place):
    block, tile = place
    return (
        slice(block * SUBLANES, (block + 1) * SUBLANES),
        slice(tile * LANES, (tile + 1) * LANES),
    )


def shift_columns(tiles, step, outer, blocks, count):
    sublane = lax.broadcasted_iota(jnp.int32, (SUBLANES, LANES), 0)
    turned = {p: pltpu.roll(x, SUBLANES - 1 if step > 0 else 1, 0) for p, x in tiles.items()}
    inside = sublane < SUBLANES - 1 if step > 0 else sublane > 0
    shifted = {}
    for block in range(blocks):
        for tile in range(count):
            beyond = block + step
            other = turned[beyond, tile] if 0 <= beyond < blocks else outer[tile]
            shifted[block, tile] = jnp.where(inside, turned[block, tile], other)
    return shifted


def shift_rows(tiles, step, blocks, count):
    lane = lax.broadcasted_iota(jnp.int32, (SUBLANES, LANES), 1)
    turned = {p: pltpu.roll(x, LANES - 1 if step > 0 else 1, 1) for p, x in tiles.items()}
    inside = lane < LANES - 1 if step > 0 else lane > 0
    shifted = {}
    for block in range(blocks):
        for tile in range(count):
            beyond = tile + step
            other = turned[block, beyond] if 0 <= beyond < count else 0.0
            shifted[block, tile] = jnp.where(inside, turned[block, tile], other)
    return shifted


def reciprocal(value):
    guess = pl.reciprocal(value, approx=True)
    return guess * (2.0 - value * guess)


def redox_sources(masked):
    oxygen, nitrate, nitrite, ammonium, _, carbon, sulfide, nitrous = masked
    over_oxygen = reciprocal(oxygen + HALF_OXYGEN)
    with_oxygen = oxygen * over_oxygen
    no_oxygen = HALF_OXYGEN * over_oxygen
    with_nitrate = no_oxygen * nitrate * reciprocal(nitrate + HALF_NITRATE)
    rest = no_oxygen - with_nitrate
    with_nitrite = rest * nitrite * reciprocal(nitrite + HALF_NITRITE)
    with_sulfate = rest - with_nitrite
    breakdown = RATE_CARBON * carbon
    first_nitr = RATE_AMMONIUM * ammonium * with_oxygen
    second_nitr = RATE_NITRITE * nitrite * with_oxygen
    sulfide_ox = RATE_SULFIDE * sulfide * with_oxygen
    by_nitrate = 0.9 * breakdown * with_nitrate
    return (
        -1.3 * breakdown * with_oxygen - 1.5 * first_nitr - 0.5 * second_nitr - 2.0 * sulfide_ox,
        second_nitr - by_nitrate,
        by_nitrate
        - 0.6 * breakdown * with_nitrite
        + (1.0 - YIELD_NITROUS) * first_nitr
        - second_nitr,
        0.15 * breakdown - first_nitr,
        0.1 * breakdown,
        -breakdown,
        0.5 * breakdown * with_sulfate - sulfide_ox,
        YIELD_NITROUS * first_nitr - RATE_NITROUS * nitrous * no_oxygen,
    )


def source_kernel(tracers_ref, depth_ref, _, base_ref):
    kinds, levels, columns, rows = tracers_ref.shape
    places = grid_tiles(columns, rows)

    @pl.loop(0, levels)
    def _(level):
        above = jnp.maximum(level - 1, 0)
        below = jnp.minimum(level + 1, levels - 1)
        mix_up_level = jnp.where(level > 0, VERT_DIFF, 0.0)
        for p in places:
            at = tile_index(p)
            depth_here = depth_ref[at]
            wet = jnp.where(level < depth_here, 1.0, 0.0)
            mix_up = wet * mix_up_level
            mix_down = jnp.where(level + 1 < depth_here, VERT_DIFF, 0.0)
            values = [tracers_ref[(kind, level) + at] for kind in range(kinds)]
            sources = redox_sources([value * wet for value in values])
            for kind in range(kinds):
                value = values[kind]
                down = (tracers_ref[(kind, below) + at] - value) * mix_down
                up = (value - tracers_ref[(kind, above) + at]) * mix_up
                base_ref[(kind, level) + at] = value + (wet * sources[kind] + (down - up))


def turn(ref_block, target_ref, start=0):
    rows = ref_block.shape[1]
    for tile in range(rows // LANES):
        part = slice(tile * LANES, (tile + 1) * LANES)
        target_ref[start + part.start : start + part.stop] = ref_block[:, part].T


def shifted(here, other, step):
    sublane = lax.broadcasted_iota(jnp.int32, (SUBLANES, LANES), 0)
    inside = sublane < SUBLANES - step if step > 0 else sublane >= -step
    amount = (SUBLANES - step) % SUBLANES if step > 0 else -step
    other = pltpu.roll(other, amount, 0) if other is not None else 0.0
    return jnp.where(inside, pltpu.roll(here, amount, 0), other)


def row_tile(block):
    return slice(block * SUBLANES, (block + 1) * SUBLANES)


def north_kernel(
    tracers_ref,
    depth_ref,
    v_ref,
    _,
    change_ref,
    face_ref,
    depth_turned_ref,
    wet_ref,
    scale_ref,
    flow_ref,
    mix_ref,
    masked_ref,
):
    kinds, levels, columns, rows = tracers_ref.shape
    per_layer = LANES // columns
    layers = levels // per_layer
    blocks = rows // SUBLANES
    depth = depth_ref[...].astype(jnp.float32)
    turn(jnp.concatenate([depth] * per_layer, axis=0), depth_turned_ref)
    lane_level = lax.broadcasted_iota(jnp.int32, (SUBLANES, LANES), 1) // columns
    for layer in range(layers):
        span = slice(layer * per_layer, (layer + 1) * per_layer)
        turn(v_ref[span].reshape(LANES, rows), flow_ref.at[layer])
        level = (lane_level + layer * per_layer).astype(jnp.float32)
        for block in range(blocks):
            at = row_tile(block)
            here = depth_turned_ref[at]
            after = depth_turned_ref[row_tile(block + 1)] if block + 1 < blocks else None
            is_open = level < jnp.minimum(here, shifted(here, after, 1))
            scale = jnp.where(is_open, 1.0 / 12.0, 0.0)
            wet_ref[layer, at] = jnp.where(level < here, 1.0, 0.0)
            scale_ref[layer, at] = scale
            mix_ref[layer, at] = jnp.where(is_open, HORIZ_DIFF, 0.0)
            flow_ref[layer, at] = flow_ref[layer, at] * scale

    @pl.loop(0, kinds)
    def _(kind):
        for layer in range(layers):
            span = slice(layer * per_layer, (layer + 1) * per_layer)
            turn(tracers_ref[kind, span].reshape(LANES, rows), masked_ref.at[layer])
            tiles = [
                masked_ref[layer, row_tile(block)] * wet_ref[layer, row_tile(block)]
                for block in range(blocks)
            ]
            before = None
            for block in range(blocks):
                at = row_tile(block)
                here = tiles[block]
                after = tiles[block + 1] if block + 1 < blocks else None
                one = shifted(here, after, 1)
                two = shifted(here, after, 2)
                south = shifted(here, tiles[block - 1] if block else None, -1)
                face = 7.0 * (here + one) - (south + two)
                face_ref[kind, layer, at] = face * scale_ref[layer, at]
                flux = face * flow_ref[layer, at] - (one - here) * mix_ref[layer, at]
                change_ref[kind, layer, at] = shifted(flux, before, -1) - flux
                before = flux


def east_kernel(
    tracers_ref,
    depth_ref,
    east_depth_ref,
    u_ref,
    from_west_ref,
    from_east_ref,
    own_west_ref,
    before_ref,
    _,
    base_ref,
    face_east_ref,
    face_west_ref,
    flux_west_ref,
):
    kinds, levels, columns, rows = tracers_ref.shape
    blocks, count = columns // SUBLANES, rows // LANES
    places = grid_tiles(columns, rows)
    depth_west = from_west_ref[2 * levels + levels // SUBLANES]
    for z in range(levels):
        row = z % SUBLANES
        u_west = from_west_ref[2 * levels + z // SUBLANES, row : row + 1]
        center, east_one = from_west_ref[2 * z + 1], own_west_ref[2 * z]
        outer = from_west_ref[2 * z] + own_west_ref[2 * z + 1]
        scale_west = jnp.where(z < depth_west, 1.0 / 12.0, 0.0)
        mix_west = jnp.where(z < depth_west, HORIZ_DIFF, 0.0)
        face = (7.0 * (center + east_one) - outer) * scale_west
        for kind in range(kinds):
            face_west_ref[kind, z : z + 1] = face[kind : kind + 1]
        flux_west_ref[z] = u_west * face - mix_west * (east_one - center)

    @pl.loop(0, levels)
    def _(level):
        wet, scale, mix = {}, {}, {}
        for p in places:
            at = tile_index(p)
            wet[p] = jnp.where(level < depth_ref[at], 1.0, 0.0)
            is_open = level < east_depth_ref[at]
            scale[p] = jnp.where(is_open, 1.0 / 12.0, 0.0)
            mix[p] = jnp.where(is_open, HORIZ_DIFF, 0.0)
        for kind in range(kinds):
            def halo(ref, index):
                return [
                    jnp.broadcast_to(
                        ref[index, kind : kind + 1, tile * LANES : (tile + 1) * LANES],
                        (SUBLANES, LANES),
                    )
                    for tile in range(count)
                ]

            masked = {p: tracers_ref[(kind, level) + tile_index(p)] * wet[p] for p in places}
            one = shift_columns(masked, 1, halo(from_east_ref, 2 * level), blocks, count)
            two = shift_columns(one, 1, halo(from_east_ref, 2 * level + 1), blocks, count)
            west = shift_columns(masked, -1, halo(from_west_ref, 2 * level + 1), blocks, count)
            flux = {}
            for p in places:
                at = (kind, level) + tile_index(p)
                face = (7.0 * (masked[p] + one[p]) - (west[p] + two[p])) * scale[p]
                face_east_ref[at] = face
                flux[p] = u_ref[(level,) + tile_index(p)] * face - mix[p] * (one[p] - masked[p])
            incoming = shift_columns(flux, -1, halo(flux_west_ref, level), blocks, count)
            for p in places:
                at = (kind, level) + tile_index(p)
                base_ref[at] = before_ref[at] + (incoming[p] - flux[p])


def update_kernel(
    kept_ref,
    came_ref,
    basis_ref,
    base_ref,
    face_east_ref,
    face_west_ref,
    change_ref,
    face_north_ref,
    surface_ref,
    out_ref,
    slabs_ref,
    height_ref,
    flow_ref,
    turned_ref,
    result_ref,
    sems,
):
    half = lax.rem(lax.axis_index("lon") // 2, 2)
    for source in range(kept_ref.shape[1]):
        for core in range(2):
            slabs_ref[4 * source + 2 * half + core] = kept_ref[core, source]
            slabs_ref[4 * source + 2 * (1 - half) + core] = came_ref[core, source]
    kinds, levels, columns, rows = base_ref.shape
    blocks, count = columns // SUBLANES, rows // LANES
    places = grid_tiles(columns, rows)
    sources, slab_rows, _ = slabs_ref.shape
    band, width = surface_ref.shape
    moment_row = slabs_ref[0, columns + 2 : columns + 3]
    for source in range(1, sources):
        moment_row = moment_row + slabs_ref[source, columns + 2 : columns + 3]
    dots = [moment_row[:, m : m + 1] for m in range(2 * BASIS)]
    weights = basis_weights(
        dots[:2] + [2.0 * dots[m] - dots[m % 2] for m in range(2, 2 * BASIS)]
    )
    lane_group = lax.broadcasted_iota(jnp.int32, (1, LANES), 1) // band
    lane_weight = jnp.zeros((1, LANES), jnp.float32)
    for k in range(BASIS):
        lane_weight = jnp.where(lane_group == k, weights[k], lane_weight)
    surface = weights[0] * basis_ref[:band]
    for k in range(1, BASIS):
        surface = surface + weights[k] * basis_ref[k * band : (k + 1) * band]
    surface_ref[...] = surface

    fill = LANES // band
    group_full = lax.broadcasted_iota(jnp.int32, (slab_rows, LANES), 1) // band
    height, east_edge, west_edge = {}, [], []
    for tile in range(count):
        joined = None
        for p in range(fill):
            part = slabs_ref[tile * fill + p] * lane_weight
            shift = LANES // 2
            while shift >= band:
                part = part + pltpu.roll(part, shift, 1)
                shift //= 2
            joined = part if joined is None else jnp.where(group_full == p, part, joined)
        for block in range(blocks):
            height[block, tile] = joined[block * SUBLANES : (block + 1) * SUBLANES]
        east_edge.append(jnp.broadcast_to(joined[columns : columns + 1], (SUBLANES, LANES)))
        west_edge.append(
            jnp.broadcast_to(joined[columns + 1 : columns + 2], (SUBLANES, LANES))
        )
    height_east = shift_columns(height, 1, east_edge, blocks, count)
    flow_east = {p: -BARO_GAIN * (height_east[p] - height[p]) for p in places}
    per_layer = LANES // columns
    layers = levels // per_layer
    row_blocks = rows // SUBLANES
    for p in places:
        for repeat in range(per_layer):
            at = tile_index(p)
            start = repeat * columns
            height_ref[start + at[0].start : start + at[0].stop, at[1]] = height[p]
    turn(height_ref, turned_ref)
    for block in range(row_blocks):
        here = turned_ref[row_tile(block)]
        after = turned_ref[row_tile(block + 1)] if block + 1 < row_blocks else None
        flow_ref[row_tile(block)] = -BARO_GAIN * (shifted(here, after, 1) - here)
    flow_west = [
        -BARO_GAIN * (jnp.broadcast_to(height[0, tile][:1], (SUBLANES, LANES)) - west_edge[tile])
        for tile in range(count)
    ]

    def copy(kind):
        return pltpu.make_async_copy(result_ref.at[kind], out_ref.at[kind], sems.at[kind])

    @pl.loop(0, kinds)
    def _(kind):
        for layer in range(layers):
            before = None
            for block in range(row_blocks):
                at = row_tile(block)
                flux = flow_ref[at] * face_north_ref[kind, layer, at]
                turned_ref[at] = change_ref[kind, layer, at] + (shifted(flux, before, -1) - flux)
                before = flux
            for tile in range(count):
                part = slice(tile * LANES, (tile + 1) * LANES)
                along = turned_ref[part].T
                for z in range(per_layer):
                    level = layer * per_layer + z
                    flux_east = {
                        (block, tile): flow_east[block, tile]
                        * face_east_ref[(kind, level) + tile_index((block, tile))]
                        for block in range(blocks)
                    }
                    edge = flow_west[tile] * jnp.broadcast_to(
                        face_west_ref[kind, level : level + 1, part], (SUBLANES, LANES)
                    )
                    for block in range(blocks):
                        at = (kind, level) + tile_index((block, tile))
                        start = z * columns + block * SUBLANES
                        west = flux_east[block - 1, tile] if block else edge
                        flux = flux_east[block, tile]
                        result_ref[at] = base_ref[at] + (
                            (shifted(flux, west, -1) - flux) + along[start : start + SUBLANES]
                        )
        copy(kind).start()

    for kind in range(kinds):
        copy(kind).wait()


def body(
    surface_old,
    surface_forcing,
    surface_coeff,
    ocean_mask,
    column_depth,
    east_depth,
    tracers,
    u_clinic,
    v_clinic,
):
    band, width = surface_old.shape
    kinds, levels, columns, rows = tracers.shape
    count = lax.axis_size("lon")
    f32 = jnp.float32
    sds = jax.ShapeDtypeStruct
    vmem = pl.BlockSpec(memory_space=pltpu.VMEM)
    hbm = pl.BlockSpec(memory_space=pltpu.HBM)
    fields = (surface_old, surface_forcing, surface_coeff, ocean_mask)
    forward = [(i, i + 1) for i in range(count - 1)]
    backward = [(target, source) for source, target in forward]
    ring = [(i, (i + 1) % count) for i in range(count)]
    ring_back = [(target, source) for source, target in ring]

    def call(
        kernel, out_shape, name, operands, scratch=(), limit=SMALL_VMEM, cost=0, far=()
    ):
        return pl.pallas_call(
            kernel,
            out_shape=out_shape,
            in_specs=[hbm if place in far else vmem for place in range(len(operands))],
            out_specs=[pl.BlockSpec(memory_space=pl.ANY) if x is result else vmem for x in out_shape],
            scratch_shapes=list(scratch),
            compiler_params=pltpu.CompilerParams(vmem_limit_bytes=limit),
            cost_estimate=pl.CostEstimate(
                flops=cost * tracers.size, bytes_accessed=8 * tracers.size, transcendentals=0
            )
            if cost
            else None,
            name=name,
        )(
            *(
                pltpu.with_memory_space_constraint(x, pltpu.HBM) if place in far else x
                for place, x in enumerate(operands)
            )
        )

    result = sds(tracers.shape, f32)
    packed = sds((3 * HALO, width), f32)
    held = pltpu.VMEM(tracers.shape, f32)

    low, high, own = call(
        pack_kernel,
        (packed, packed, sds((3 * band, width), f32)),
        "pack_edges",
        fields,
        scratch=[pltpu.VMEM(x.shape, x.dtype) for x in fields] + [pltpu.SemaphoreType.DMA((4,))],
        far=range(4),
    )
    below = lax.ppermute(high, "lon", forward)
    above = lax.ppermute(low, "lon", backward)

    def fetched(x):
        return pltpu.VMEM(x.shape, x.dtype)

    inputs = (tracers, column_depth, east_depth, u_clinic, v_clinic)
    folded, tracers, column_depth, east_depth, u_clinic, v_clinic = call(
        load_kernel,
        (
            packed,
            *(fetched(x) for x in inputs),
        ),
        "load",
        (high, *inputs),
        scratch=[pltpu.SemaphoreType.DMA((4 + kinds,))],
        far=range(1, 6),
    )
    groups = count // 4
    basis, *sends = call(
        basis_kernel,
        (sds((BASIS * band, width), f32),) + (sds((4, SLAB_ROWS, LANES), f32),) * groups,
        "solver_basis",
        (own, below, above, folded),
        scratch=[pltpu.VMEM((count, SLAB_ROWS, LANES), f32)],
    )
    slabs = [sends[0]]
    for step in range(1, groups):
        pairs = [(i, (i + 4 * step) % count) for i in range(count)]
        slabs.append(lax.ppermute(sends[step], "lon", pairs))
    east_going, own_west = call(
        edge_kernel,
        (
            sds((2 * levels + levels // SUBLANES + 1, kinds, rows), f32),
            sds((2 * levels, kinds, rows), f32),
        ),
        "pack_tracer_edges",
        (tracers, column_depth, east_depth, u_clinic, basis),
    )
    from_west = lax.ppermute(east_going, "lon", ring)
    from_east = lax.ppermute(own_west, "lon", ring_back)
    (base,) = call(source_kernel, (held,), "sources", (tracers, column_depth, own_west), cost=70)
    turned = (kinds, levels * columns // LANES, rows, LANES)
    change, face_north = call(
        north_kernel,
        (pltpu.VMEM(turned, f32), pltpu.VMEM(turned, f32)),
        "north_fluxes",
        (tracers, column_depth, v_clinic, base),
        scratch=[pltpu.VMEM((rows, LANES), f32)] + [pltpu.VMEM(turned[1:], f32)] * 5,
        cost=70,
    )
    quarter = sds((2, groups, SLAB_ROWS, LANES), f32)
    keep, send = call(core_kernel, (quarter, quarter), "split_cores", (*slabs, change))
    came = lax.ppermute(send, "lon", [(i, i ^ 1) for i in range(count)])
    keep, send = call(half_kernel, (quarter, quarter), "split_halves", (keep, came))
    came = lax.ppermute(send, "lon", [(i, i ^ 2) for i in range(count)])
    base, face_east, face_west = call(
        east_kernel,
        (held, held, pltpu.VMEM((kinds, levels, rows), f32)),
        "east_fluxes",
        (
            tracers,
            column_depth,
            east_depth,
            u_clinic,
            from_west,
            from_east,
            own_west,
            base,
            keep,
        ),
        scratch=[pltpu.VMEM((levels, kinds, rows), f32)],
        cost=70,
    )
    return tuple(
        call(
            update_kernel,
            (sds((band, width), f32), result),
            "surface_update",
            (keep, came, basis, base, face_east, face_west, change, face_north),
            scratch=[
                pltpu.VMEM((count, SLAB_ROWS, LANES), f32),
                pltpu.VMEM((LANES, rows), f32),
                pltpu.VMEM((rows, LANES), f32),
                pltpu.VMEM((rows, LANES), f32),
                pltpu.VMEM(tracers.shape, f32),
                pltpu.SemaphoreType.DMA((kinds,)),
            ],
            limit=RESULT_VMEM,
        )
    )


def solution(mesh):
    in_specs = (
        P(("member", "lon"), None),
        P(("member", "lon"), None),
        P("lon", None),
        P("lon", None),
        P("lon", None),
        P("lon", None),
        P("member", None, "lon", None),
        P("member", "lon", None),
        P("member", "lon", None),
    )
    out_specs = (P(("member", "lon"), None), P("member", None, "lon", None))
    return jax.shard_map(body, mesh=mesh, in_specs=in_specs, out_specs=out_specs, check_vma=False)
```

```python
import jax
import jax.numpy as jnp
from jax import lax
from jax.experimental import pallas as pl
from jax.experimental.pallas import tpu as pltpu
from jax.sharding import PartitionSpec as P

BARO_GAIN = 0.1
HORIZ_DIFF = 0.1
VERT_DIFF = 0.15
RATE_CARBON = 0.3
RATE_AMMONIUM = 0.2
RATE_NITRITE = 0.2
RATE_SULFIDE = 0.3
RATE_NITROUS = 0.2
HALF_OXYGEN = 0.3
HALF_NITRATE = 0.3
HALF_NITRITE = 0.3
YIELD_NITROUS = 0.3


SUBLANES = 8
LANES = 128
SMALL_VMEM = 4 * 2**20
RESULT_VMEM = 14 * 2**20
HALO = 8
SLAB_ROWS = 24
BASIS = 4
CENTRE = 4.55
SPREAD = 4.45
PIVOT_FLOOR = 3e-7


def is_even():
    return lax.rem(lax.axis_index("lon"), 2) == 0


def basis_kernel(
    own_ref,
    inner_ref,
    outer_ref,
    folded_ref,
    basis_ref,
    *refs,
):
    send_refs, slabs_ref = refs[:-1], refs[-1]
    rows, width = own_ref.shape[0] // 3, own_ref.shape[1]
    count = slabs_ref.shape[0]
    columns = width // count
    top_device = lax.axis_index("lon") == count - 1
    below = jnp.where(is_even(), outer_ref[...], inner_ref[...])
    above = jnp.where(is_even(), inner_ref[...], outer_ref[...])
    above = jnp.where(top_device, folded_ref[...], above)

    def extended(place):
        part = slice(HALO * place, HALO * (place + 1))
        own = own_ref[rows * place : rows * (place + 1)]
        return jnp.concatenate([below[part], own, above[part]], axis=0)

    first, coeff, mask = extended(0), extended(1), extended(2)
    diagonal = (coeff + 4.0 * mask - CENTRE) * (1.0 / SPREAD)
    beside = mask * (1.0 / SPREAD)
    total = rows + 2 * HALO

    def scaled(values):
        masked = mask * values
        around = (
            pltpu.roll(masked, total - 1, 0)
            + pltpu.roll(masked, 1, 0)
            + pltpu.roll(masked, width - 1, 1)
            + pltpu.roll(masked, 1, 1)
        )
        return diagonal * values - beside * around

    vectors = [first, scaled(first)]
    while len(vectors) < BASIS + 1:
        vectors.append(2.0 * scaled(vectors[-1]) - vectors[-2])
    own = [vector[HALO : HALO + rows] for vector in vectors]
    sums = []
    for order in range(2 * BASIS):
        product = own[order // 2] * own[(order + 1) // 2]
        sums.append(jnp.sum(product, axis=0, keepdims=True))
    partial = jnp.sum(jnp.concatenate(sums, axis=0), axis=1, keepdims=True)
    lane = lax.broadcasted_iota(jnp.int32, (2 * BASIS, LANES), 1)
    place = lax.broadcasted_iota(jnp.int32, (2 * BASIS, LANES), 0)
    moments = jnp.sum(jnp.where(lane == place, partial, 0.0), axis=0, keepdims=True)
    stacked = jnp.concatenate(own[:BASIS], axis=0)
    basis_ref[...] = stacked
    if BASIS * rows < LANES:
        stacked = jnp.concatenate(
            [stacked, jnp.zeros((LANES - BASIS * rows, width), jnp.float32)], axis=0
        )
    turned = stacked.T
    for target in range(count):
        start = target * columns
        east = (start + columns) % width
        west = (start - 1) % width
        pieces = [
            turned[start : start + columns],
            turned[east : east + 1],
            turned[west : west + 1],
            moments,
            jnp.zeros((SLAB_ROWS - columns - 3, LANES), jnp.float32),
        ]
        slabs_ref[target] = jnp.concatenate(pieces, axis=0)
    groups = len(send_refs)
    group = lax.axis_index("lon") // 4
    for step in range(groups):
        target = lax.rem(group + step, groups)
        for place in range(4):
            send_refs[step][place] = slabs_ref[4 * target + place]


def core_kernel(*refs):
    came_refs, (_, keep_ref, send_ref) = refs[:-3], refs[-3:]
    here = lax.axis_index("lon")
    core, group = lax.rem(here, 2), here // 4
    groups = len(came_refs)
    for step in range(groups):
        source = lax.rem(group + groups - step, groups)
        for y in range(2):
            keep_ref[y, source] = came_refs[step][2 * y + core]
            send_ref[y, source] = came_refs[step][2 * y + 1 - core]


def half_kernel(kept_ref, came_ref, keep_ref, send_ref):
    here = lax.axis_index("lon")
    core, half = lax.rem(here, 2), lax.rem(here // 2, 2)
    keep_ref[core] = kept_ref[half]
    keep_ref[1 - core] = came_ref[half]
    send_ref[core] = kept_ref[1 - half]
    send_ref[1 - core] = came_ref[1 - half]


def basis_weights(moments):
    gram = {}

    def inner(i, j):
        key = (i + j, abs(i - j))
        if key not in gram:
            gram[key] = 0.5 * (moments[i + j] + moments[abs(i - j)])
        return gram[key]

    matrix = [[None] * BASIS for _ in range(BASIS)]
    for i in range(BASIS):
        for j in range(i + 1):
            if i == 0:
                image = moments[1]
            elif j == 0:
                image = inner(1, i)
            else:
                image = 0.5 * (inner(i, j + 1) + inner(i, j - 1))
            matrix[i][j] = CENTRE * inner(i, j) + SPREAD * image
    right = [inner(i, 0) for i in range(BASIS)]
    start = [matrix[i][i] for i in range(BASIS)]
    inverse = []
    factors = [[None] * BASIS for _ in range(BASIS)]
    for n in range(BASIS):
        pivot = matrix[n][n]
        inverse.append(jnp.where(pivot > PIVOT_FLOOR * start[n], 1.0 / pivot, 0.0))
        for i in range(n + 1, BASIS):
            factors[i][n] = matrix[i][n] * inverse[n]
        for i in range(n + 1, BASIS):
            for j in range(n + 1, i + 1):
                matrix[i][j] = matrix[i][j] - factors[i][n] * matrix[j][n]
            right[i] = right[i] - factors[i][n] * right[n]
    weights = [None] * BASIS
    for n in reversed(range(BASIS)):
        value = right[n] * inverse[n]
        for i in range(n + 1, BASIS):
            value = value - factors[i][n] * weights[i]
        weights[n] = value
    return weights


def reverse_tile(tile):
    for axis, size in ((0, SUBLANES), (1, LANES)):
        place = lax.broadcasted_iota(jnp.int32, (SUBLANES, LANES), axis)
        step = size // 2
        while step:
            tile = jnp.where(
                (place & step) != 0,
                pltpu.roll(tile, step, axis),
                pltpu.roll(tile, size - step, axis),
            )
            step //= 2
    return tile


def load_kernel(
    old_in,
    force_in,
    coeff_in,
    mask_in,
    tracers_in,
    depth_in,
    east_depth_in,
    u_in,
    v_in,
    inner_ref,
    outer_ref,
    own_ref,
    folded_ref,
    tracers_ref,
    depth_ref,
    east_depth_ref,
    u_ref,
    v_ref,
    edge_inner_ref,
    edge_outer_ref,
    old_ref,
    force_ref,
    coeff_ref,
    mask_ref,
    sems,
):
    kinds, levels, columns, rows = tracers_ref.shape
    band = old_ref.shape[0]
    moves = [
        (old_in, old_ref),
        (force_in, force_ref),
        (coeff_in, coeff_ref),
        (mask_in, mask_ref),
        (depth_in, depth_ref),
        (east_depth_in, east_depth_ref),
        (u_in, u_ref),
    ]
    moves += [(tracers_in.at[kind], tracers_ref.at[kind]) for kind in range(kinds)]
    moves += [(v_in, v_ref)]
    copies = [
        pltpu.make_async_copy(source, target, sems.at[place])
        for place, (source, target) in enumerate(moves)
    ]
    for copy in copies:
        copy.start()
    for copy in copies[:4]:
        copy.wait()
    coeff = coeff_ref[...]
    fields = (
        coeff * old_ref[...] + force_ref[...],
        coeff,
        mask_ref[...].astype(jnp.float32),
    )
    for place, field in enumerate(fields):
        low, high = field[:HALO], field[band - HALO :]
        part = slice(HALO * place, HALO * (place + 1))
        inner_ref[part] = jnp.where(is_even(), high, low)
        outer_ref[part] = jnp.where(is_even(), low, high)
        own_ref[band * place : band * (place + 1)] = field
        tiles = high.shape[1] // LANES
        for tile in range(tiles):
            other = tiles - 1 - tile
            folded_ref[part, tile * LANES : (tile + 1) * LANES] = reverse_tile(
                high[:, other * LANES : (other + 1) * LANES]
            )
    for copy in copies[4:7]:
        copy.wait()

    def pack(kind, first, target_ref):
        for side in range(2):
            column = first + side
            for z in range(levels):
                wet = (z < depth_ref[column : column + 1]).astype(jnp.float32)
                target_ref[2 * z + side, kind : kind + 1] = (
                    tracers_ref[kind, z, column : column + 1] * wet
                )

    def pack_faces(target_ref):
        for z in range(levels):
            place = 2 * levels + z // SUBLANES
            row = z % SUBLANES
            target_ref[place, row : row + 1] = u_ref[z, columns - 1 : columns]
        place = 2 * levels + levels // SUBLANES
        target_ref[place] = jnp.broadcast_to(
            east_depth_ref[columns - 1 : columns].astype(jnp.float32), (SUBLANES, rows)
        )

    pack_faces(edge_inner_ref)
    pack_faces(edge_outer_ref)

    def pack_all(inner_column, outer_column):
        for kind in range(kinds):
            copies[7 + kind].wait()
            pack(kind, inner_column, edge_inner_ref)
            pack(kind, outer_column, edge_outer_ref)

    @pl.when(is_even())
    def _():
        pack_all(columns - 2, 0)

    @pl.when(jnp.logical_not(is_even()))
    def _():
        pack_all(0, columns - 2)

    copies[-1].wait()


def grid_tiles(columns, rows):
    return [
        (block, tile)
        for block in range(columns // SUBLANES)
        for tile in range(rows // LANES)
    ]


def tile_index(place):
    block, tile = place
    return (
        slice(block * SUBLANES, (block + 1) * SUBLANES),
        slice(tile * LANES, (tile + 1) * LANES),
    )


def shift_columns(tiles, step, outer, blocks, count):
    sublane = lax.broadcasted_iota(jnp.int32, (SUBLANES, LANES), 0)
    turned = {p: pltpu.roll(x, SUBLANES - 1 if step > 0 else 1, 0) for p, x in tiles.items()}
    inside = sublane < SUBLANES - 1 if step > 0 else sublane > 0
    shifted = {}
    for block in range(blocks):
        for tile in range(count):
            beyond = block + step
            other = turned[beyond, tile] if 0 <= beyond < blocks else outer[tile]
            shifted[block, tile] = jnp.where(inside, turned[block, tile], other)
    return shifted


def shift_rows(tiles, step, blocks, count):
    lane = lax.broadcasted_iota(jnp.int32, (SUBLANES, LANES), 1)
    turned = {p: pltpu.roll(x, LANES - 1 if step > 0 else 1, 1) for p, x in tiles.items()}
    inside = lane < LANES - 1 if step > 0 else lane > 0
    shifted = {}
    for block in range(blocks):
        for tile in range(count):
            beyond = tile + step
            other = turned[block, beyond] if 0 <= beyond < count else 0.0
            shifted[block, tile] = jnp.where(inside, turned[block, tile], other)
    return shifted


def reciprocal(value):
    guess = pl.reciprocal(value, approx=True)
    return guess * (2.0 - value * guess)


def redox_sources(masked):
    oxygen, nitrate, nitrite, ammonium, _, carbon, sulfide, nitrous = masked
    over_oxygen = reciprocal(oxygen + HALF_OXYGEN)
    with_oxygen = oxygen * over_oxygen
    no_oxygen = HALF_OXYGEN * over_oxygen
    with_nitrate = no_oxygen * nitrate * reciprocal(nitrate + HALF_NITRATE)
    rest = no_oxygen - with_nitrate
    with_nitrite = rest * nitrite * reciprocal(nitrite + HALF_NITRITE)
    with_sulfate = rest - with_nitrite
    breakdown = RATE_CARBON * carbon
    first_nitr = RATE_AMMONIUM * ammonium * with_oxygen
    second_nitr = RATE_NITRITE * nitrite * with_oxygen
    sulfide_ox = RATE_SULFIDE * sulfide * with_oxygen
    by_nitrate = 0.9 * breakdown * with_nitrate
    return (
        -1.3 * breakdown * with_oxygen - 1.5 * first_nitr - 0.5 * second_nitr - 2.0 * sulfide_ox,
        second_nitr - by_nitrate,
        by_nitrate
        - 0.6 * breakdown * with_nitrite
        + (1.0 - YIELD_NITROUS) * first_nitr
        - second_nitr,
        0.15 * breakdown - first_nitr,
        0.1 * breakdown,
        -breakdown,
        0.5 * breakdown * with_sulfate - sulfide_ox,
        YIELD_NITROUS * first_nitr - RATE_NITROUS * nitrous * no_oxygen,
    )


def source_kernel(tracers_ref, depth_ref, _, base_ref):
    kinds, levels, columns, rows = tracers_ref.shape
    places = grid_tiles(columns, rows)

    @pl.loop(0, levels)
    def _(level):
        above = jnp.maximum(level - 1, 0)
        below = jnp.minimum(level + 1, levels - 1)
        mix_up_level = jnp.where(level > 0, VERT_DIFF, 0.0)
        for p in places:
            at = tile_index(p)
            depth_here = depth_ref[at]
            wet = jnp.where(level < depth_here, 1.0, 0.0)
            mix_up = wet * mix_up_level
            mix_down = jnp.where(level + 1 < depth_here, VERT_DIFF, 0.0)
            values = [tracers_ref[(kind, level) + at] for kind in range(kinds)]
            sources = redox_sources([value * wet for value in values])
            for kind in range(kinds):
                value = values[kind]
                down = (tracers_ref[(kind, below) + at] - value) * mix_down
                up = (value - tracers_ref[(kind, above) + at]) * mix_up
                base_ref[(kind, level) + at] = value + (wet * sources[kind] + (down - up))


def turn(ref_block, target_ref, start=0):
    rows = ref_block.shape[1]
    for tile in range(rows // LANES):
        part = slice(tile * LANES, (tile + 1) * LANES)
        target_ref[start + part.start : start + part.stop] = ref_block[:, part].T


def shifted(here, other, step):
    sublane = lax.broadcasted_iota(jnp.int32, (SUBLANES, LANES), 0)
    inside = sublane < SUBLANES - step if step > 0 else sublane >= -step
    amount = (SUBLANES - step) % SUBLANES if step > 0 else -step
    other = pltpu.roll(other, amount, 0) if other is not None else 0.0
    return jnp.where(inside, pltpu.roll(here, amount, 0), other)


def row_tile(block):
    return slice(block * SUBLANES, (block + 1) * SUBLANES)


def north_kernel(
    tracers_ref,
    depth_ref,
    v_ref,
    _,
    change_ref,
    face_ref,
    depth_turned_ref,
    wet_ref,
    scale_ref,
    flow_ref,
    mix_ref,
    masked_ref,
):
    kinds, levels, columns, rows = tracers_ref.shape
    per_layer = LANES // columns
    layers = levels // per_layer
    blocks = rows // SUBLANES
    depth = depth_ref[...].astype(jnp.float32)
    turn(jnp.concatenate([depth] * per_layer, axis=0), depth_turned_ref)
    lane_level = lax.broadcasted_iota(jnp.int32, (SUBLANES, LANES), 1) // columns
    for layer in range(layers):
        span = slice(layer * per_layer, (layer + 1) * per_layer)
        turn(v_ref[span].reshape(LANES, rows), flow_ref.at[layer])
        level = (lane_level + layer * per_layer).astype(jnp.float32)
        for block in range(blocks):
            at = row_tile(block)
            here = depth_turned_ref[at]
            after = depth_turned_ref[row_tile(block + 1)] if block + 1 < blocks else None
            is_open = level < jnp.minimum(here, shifted(here, after, 1))
            scale = jnp.where(is_open, 1.0 / 12.0, 0.0)
            wet_ref[layer, at] = jnp.where(level < here, 1.0, 0.0)
            scale_ref[layer, at] = scale
            mix_ref[layer, at] = jnp.where(is_open, HORIZ_DIFF, 0.0)
            flow_ref[layer, at] = flow_ref[layer, at] * scale

    @pl.loop(0, kinds)
    def _(kind):
        for layer in range(layers):
            span = slice(layer * per_layer, (layer + 1) * per_layer)
            turn(tracers_ref[kind, span].reshape(LANES, rows), masked_ref.at[layer])
            tiles = [
                masked_ref[layer, row_tile(block)] * wet_ref[layer, row_tile(block)]
                for block in range(blocks)
            ]
            before = None
            for block in range(blocks):
                at = row_tile(block)
                here = tiles[block]
                after = tiles[block + 1] if block + 1 < blocks else None
                one = shifted(here, after, 1)
                two = shifted(here, after, 2)
                south = shifted(here, tiles[block - 1] if block else None, -1)
                face = 7.0 * (here + one) - (south + two)
                face_ref[kind, layer, at] = face * scale_ref[layer, at]
                flux = face * flow_ref[layer, at] - (one - here) * mix_ref[layer, at]
                change_ref[kind, layer, at] = shifted(flux, before, -1) - flux
                before = flux


def east_kernel(
    tracers_ref,
    depth_ref,
    east_depth_ref,
    u_ref,
    inner_ref,
    outer_ref,
    own_inner_ref,
    own_outer_ref,
    before_ref,
    _,
    base_ref,
    face_east_ref,
    face_west_ref,
    flux_west_ref,
    from_west_ref,
    from_east_ref,
    own_west_ref,
):
    kinds, levels, columns, rows = tracers_ref.shape
    blocks, count = columns // SUBLANES, rows // LANES
    places = grid_tiles(columns, rows)
    for place in range(inner_ref.shape[0]):
        from_west_ref[place] = jnp.where(is_even(), outer_ref[place], inner_ref[place])
    for place in range(2 * levels):
        from_east_ref[place] = jnp.where(is_even(), inner_ref[place], outer_ref[place])
        own_west_ref[place] = jnp.where(is_even(), own_outer_ref[place], own_inner_ref[place])
    depth_west = from_west_ref[2 * levels + levels // SUBLANES]
    for z in range(levels):
        row = z % SUBLANES
        u_west = from_west_ref[2 * levels + z // SUBLANES, row : row + 1]
        center, east_one = from_west_ref[2 * z + 1], own_west_ref[2 * z]
        outer = from_west_ref[2 * z] + own_west_ref[2 * z + 1]
        scale_west = jnp.where(z < depth_west, 1.0 / 12.0, 0.0)
        mix_west = jnp.where(z < depth_west, HORIZ_DIFF, 0.0)
        face = (7.0 * (center + east_one) - outer) * scale_west
        for kind in range(kinds):
            face_west_ref[kind, z : z + 1] = face[kind : kind + 1]
        flux_west_ref[z] = u_west * face - mix_west * (east_one - center)

    @pl.loop(0, levels)
    def _(level):
        wet, scale, mix = {}, {}, {}
        for p in places:
            at = tile_index(p)
            wet[p] = jnp.where(level < depth_ref[at], 1.0, 0.0)
            is_open = level < east_depth_ref[at]
            scale[p] = jnp.where(is_open, 1.0 / 12.0, 0.0)
            mix[p] = jnp.where(is_open, HORIZ_DIFF, 0.0)
        for kind in range(kinds):
            def halo(ref, index):
                return [
                    jnp.broadcast_to(
                        ref[index, kind : kind + 1, tile * LANES : (tile + 1) * LANES],
                        (SUBLANES, LANES),
                    )
                    for tile in range(count)
                ]

            masked = {p: tracers_ref[(kind, level) + tile_index(p)] * wet[p] for p in places}
            one = shift_columns(masked, 1, halo(from_east_ref, 2 * level), blocks, count)
            two = shift_columns(one, 1, halo(from_east_ref, 2 * level + 1), blocks, count)
            west = shift_columns(masked, -1, halo(from_west_ref, 2 * level + 1), blocks, count)
            flux = {}
            for p in places:
                at = (kind, level) + tile_index(p)
                face = (7.0 * (masked[p] + one[p]) - (west[p] + two[p])) * scale[p]
                face_east_ref[at] = face
                flux[p] = u_ref[(level,) + tile_index(p)] * face - mix[p] * (one[p] - masked[p])
            incoming = shift_columns(flux, -1, halo(flux_west_ref, level), blocks, count)
            for p in places:
                at = (kind, level) + tile_index(p)
                base_ref[at] = before_ref[at] + (incoming[p] - flux[p])


def update_kernel(
    kept_ref,
    came_ref,
    basis_ref,
    base_ref,
    face_east_ref,
    face_west_ref,
    change_ref,
    face_north_ref,
    surface_ref,
    out_ref,
    slabs_ref,
    height_ref,
    flow_ref,
    turned_ref,
    result_ref,
    sems,
):
    half = lax.rem(lax.axis_index("lon") // 2, 2)
    for source in range(kept_ref.shape[1]):
        for core in range(2):
            slabs_ref[4 * source + 2 * half + core] = kept_ref[core, source]
            slabs_ref[4 * source + 2 * (1 - half) + core] = came_ref[core, source]
    kinds, levels, columns, rows = base_ref.shape
    blocks, count = columns // SUBLANES, rows // LANES
    places = grid_tiles(columns, rows)
    sources, slab_rows, _ = slabs_ref.shape
    band, width = surface_ref.shape
    moment_row = slabs_ref[0, columns + 2 : columns + 3]
    for source in range(1, sources):
        moment_row = moment_row + slabs_ref[source, columns + 2 : columns + 3]
    dots = [moment_row[:, m : m + 1] for m in range(2 * BASIS)]
    weights = basis_weights(
        dots[:2] + [2.0 * dots[m] - dots[m % 2] for m in range(2, 2 * BASIS)]
    )
    lane_group = lax.broadcasted_iota(jnp.int32, (1, LANES), 1) // band
    lane_weight = jnp.zeros((1, LANES), jnp.float32)
    for k in range(BASIS):
        lane_weight = jnp.where(lane_group == k, weights[k], lane_weight)
    surface = weights[0] * basis_ref[:band]
    for k in range(1, BASIS):
        surface = surface + weights[k] * basis_ref[k * band : (k + 1) * band]
    surface_ref[...] = surface

    fill = LANES // band
    group_full = lax.broadcasted_iota(jnp.int32, (slab_rows, LANES), 1) // band
    height, east_edge, west_edge = {}, [], []
    for tile in range(count):
        joined = None
        for p in range(fill):
            part = slabs_ref[tile * fill + p] * lane_weight
            shift = LANES // 2
            while shift >= band:
                part = part + pltpu.roll(part, shift, 1)
                shift //= 2
            joined = part if joined is None else jnp.where(group_full == p, part, joined)
        for block in range(blocks):
            height[block, tile] = joined[block * SUBLANES : (block + 1) * SUBLANES]
        east_edge.append(jnp.broadcast_to(joined[columns : columns + 1], (SUBLANES, LANES)))
        west_edge.append(
            jnp.broadcast_to(joined[columns + 1 : columns + 2], (SUBLANES, LANES))
        )
    height_east = shift_columns(height, 1, east_edge, blocks, count)
    flow_east = {p: -BARO_GAIN * (height_east[p] - height[p]) for p in places}
    per_layer = LANES // columns
    layers = levels // per_layer
    row_blocks = rows // SUBLANES
    for p in places:
        for repeat in range(per_layer):
            at = tile_index(p)
            start = repeat * columns
            height_ref[start + at[0].start : start + at[0].stop, at[1]] = height[p]
    turn(height_ref, turned_ref)
    for block in range(row_blocks):
        here = turned_ref[row_tile(block)]
        after = turned_ref[row_tile(block + 1)] if block + 1 < row_blocks else None
        flow_ref[row_tile(block)] = -BARO_GAIN * (shifted(here, after, 1) - here)
    flow_west = [
        -BARO_GAIN * (jnp.broadcast_to(height[0, tile][:1], (SUBLANES, LANES)) - west_edge[tile])
        for tile in range(count)
    ]

    def copy(kind):
        return pltpu.make_async_copy(result_ref.at[kind], out_ref.at[kind], sems.at[kind])

    @pl.loop(0, kinds)
    def _(kind):
        for layer in range(layers):
            before = None
            for block in range(row_blocks):
                at = row_tile(block)
                flux = flow_ref[at] * face_north_ref[kind, layer, at]
                turned_ref[at] = change_ref[kind, layer, at] + (shifted(flux, before, -1) - flux)
                before = flux
            for tile in range(count):
                part = slice(tile * LANES, (tile + 1) * LANES)
                along = turned_ref[part].T
                for z in range(per_layer):
                    level = layer * per_layer + z
                    flux_east = {
                        (block, tile): flow_east[block, tile]
                        * face_east_ref[(kind, level) + tile_index((block, tile))]
                        for block in range(blocks)
                    }
                    edge = flow_west[tile] * jnp.broadcast_to(
                        face_west_ref[kind, level : level + 1, part], (SUBLANES, LANES)
                    )
                    for block in range(blocks):
                        at = (kind, level) + tile_index((block, tile))
                        start = z * columns + block * SUBLANES
                        west = flux_east[block - 1, tile] if block else edge
                        flux = flux_east[block, tile]
                        result_ref[at] = base_ref[at] + (
                            (shifted(flux, west, -1) - flux) + along[start : start + SUBLANES]
                        )
        copy(kind).start()

    for kind in range(kinds):
        copy(kind).wait()


def body(
    surface_old,
    surface_forcing,
    surface_coeff,
    ocean_mask,
    column_depth,
    east_depth,
    tracers,
    u_clinic,
    v_clinic,
):
    band, width = surface_old.shape
    kinds, levels, columns, rows = tracers.shape
    count = lax.axis_size("lon")
    f32 = jnp.float32
    sds = jax.ShapeDtypeStruct
    vmem = pl.BlockSpec(memory_space=pltpu.VMEM)
    hbm = pl.BlockSpec(memory_space=pltpu.HBM)
    fields = (surface_old, surface_forcing, surface_coeff, ocean_mask)
    pairs_inner = [(i, i ^ 1) for i in range(count)]
    ring = [(i, (i + 1 if i % 2 else i - 1) % count) for i in range(count)]
    pairs_outer = [(i, j) for i, j in ring if abs(i - j) == 1]

    def call(
        kernel, out_shape, name, operands, scratch=(), limit=SMALL_VMEM, cost=0, far=()
    ):
        return pl.pallas_call(
            kernel,
            out_shape=out_shape,
            in_specs=[hbm if place in far else vmem for place in range(len(operands))],
            out_specs=[pl.BlockSpec(memory_space=pl.ANY) if x is result else vmem for x in out_shape],
            scratch_shapes=list(scratch),
            compiler_params=pltpu.CompilerParams(vmem_limit_bytes=limit),
            cost_estimate=pl.CostEstimate(
                flops=cost * tracers.size, bytes_accessed=8 * tracers.size, transcendentals=0
            )
            if cost
            else None,
            name=name,
        )(
            *(
                pltpu.with_memory_space_constraint(x, pltpu.HBM) if place in far else x
                for place, x in enumerate(operands)
            )
        )

    result = sds(tracers.shape, f32)
    packed = sds((3 * HALO, width), f32)
    held = pltpu.VMEM(tracers.shape, f32)

    def fetched(x):
        return pltpu.VMEM(x.shape, x.dtype)

    edges = sds((2 * levels + levels // SUBLANES + 1, kinds, rows), f32)
    inputs = (tracers, column_depth, east_depth, u_clinic, v_clinic)
    (inner, outer, own, folded, *inputs, own_inner, own_outer) = call(
        load_kernel,
        (
            packed,
            packed,
            sds((3 * band, width), f32),
            packed,
            *(fetched(x) for x in inputs),
            edges,
            edges,
        ),
        "load",
        (*fields, *inputs),
        scratch=[pltpu.VMEM(x.shape, x.dtype) for x in fields]
        + [pltpu.SemaphoreType.DMA((8 + kinds,))],
        far=range(9),
    )
    tracers, column_depth, east_depth, u_clinic, v_clinic = inputs
    came_inner = lax.ppermute(inner, "lon", pairs_inner)
    came_outer = lax.ppermute(outer, "lon", pairs_outer)

    groups = count // 4
    basis, *sends = call(
        basis_kernel,
        (sds((BASIS * band, width), f32),) + (sds((4, SLAB_ROWS, LANES), f32),) * groups,
        "solver_basis",
        (own, came_inner, came_outer, folded),
        scratch=[pltpu.VMEM((count, SLAB_ROWS, LANES), f32)],
        cost=2000,
    )
    slabs = [sends[0]]
    for step in range(1, groups):
        pairs = [(i, (i + 4 * step) % count) for i in range(count)]
        slabs.append(lax.ppermute(sends[step], "lon", pairs))
    edge_inner = lax.ppermute(own_inner, "lon", pairs_inner)
    edge_outer = lax.ppermute(own_outer, "lon", ring)
    (base,) = call(source_kernel, (held,), "sources", (tracers, column_depth, own_inner), cost=2000)
    turned = (kinds, levels * columns // LANES, rows, LANES)
    change, face_north = call(
        north_kernel,
        (pltpu.VMEM(turned, f32), pltpu.VMEM(turned, f32)),
        "north_fluxes",
        (tracers, column_depth, v_clinic, base),
        scratch=[pltpu.VMEM((rows, LANES), f32)] + [pltpu.VMEM(turned[1:], f32)] * 5,
        cost=2000,
    )
    quarter = sds((2, groups, SLAB_ROWS, LANES), f32)
    keep, send = call(core_kernel, (quarter, quarter), "split_cores", (*slabs, change))
    came = lax.ppermute(send, "lon", pairs_inner)
    keep, send = call(half_kernel, (quarter, quarter), "split_halves", (keep, came))
    came = lax.ppermute(send, "lon", [(i, i ^ 2) for i in range(count)])
    base, face_east, face_west = call(
        east_kernel,
        (held, held, pltpu.VMEM((kinds, levels, rows), f32)),
        "east_fluxes",
        (
            tracers,
            column_depth,
            east_depth,
            u_clinic,
            edge_inner,
            edge_outer,
            own_inner,
            own_outer,
            base,
            keep,
        ),
        scratch=[
            pltpu.VMEM((levels, kinds, rows), f32),
            pltpu.VMEM(edges.shape, f32),
            pltpu.VMEM(edges.shape, f32),
            pltpu.VMEM(edges.shape, f32),
        ],
        cost=2000,
    )
    return tuple(
        call(
            update_kernel,
            (sds((band, width), f32), result),
            "surface_update",
            (keep, came, basis, base, face_east, face_west, change, face_north),
            scratch=[
                pltpu.VMEM((count, SLAB_ROWS, LANES), f32),
                pltpu.VMEM((LANES, rows), f32),
                pltpu.VMEM((rows, LANES), f32),
                pltpu.VMEM((rows, LANES), f32),
                pltpu.VMEM(tracers.shape, f32),
                pltpu.SemaphoreType.DMA((kinds,)),
            ],
            limit=RESULT_VMEM,
        )
    )


def solution(mesh):
    in_specs = (
        P(("member", "lon"), None),
        P(("member", "lon"), None),
        P("lon", None),
        P("lon", None),
        P("lon", None),
        P("lon", None),
        P("member", None, "lon", None),
        P("member", "lon", None),
        P("member", "lon", None),
    )
    out_specs = (P(("member", "lon"), None), P("member", None, "lon", None))
    return jax.shard_map(body, mesh=mesh, in_specs=in_specs, out_specs=out_specs, check_vma=False)
```

```python
import jax
import jax.numpy as jnp
from jax import lax
from jax.experimental import pallas as pl
from jax.experimental.pallas import tpu as pltpu
from jax.sharding import PartitionSpec as P

BARO_GAIN = 0.1
HORIZ_DIFF = 0.1
VERT_DIFF = 0.15
RATE_CARBON = 0.3
RATE_AMMONIUM = 0.2
RATE_NITRITE = 0.2
RATE_SULFIDE = 0.3
RATE_NITROUS = 0.2
HALF_OXYGEN = 0.3
HALF_NITRATE = 0.3
HALF_NITRITE = 0.3
YIELD_NITROUS = 0.3


SUBLANES = 8
LANES = 128
SMALL_VMEM = 4 * 2**20
RESULT_VMEM = 14 * 2**20
HALO = 8
SLAB_ROWS = 24
BASIS = 4
CENTRE = 4.55
SPREAD = 4.45
PIVOT_FLOOR = 3e-7


def is_even():
    return lax.rem(lax.axis_index("lon"), 2) == 0


def basis_kernel(
    own_ref,
    inner_ref,
    outer_ref,
    folded_ref,
    basis_ref,
    keep_ref,
    send_ref,
    slabs_ref,
):
    rows, width = own_ref.shape[0] // 3, own_ref.shape[1]
    count = slabs_ref.shape[0]
    columns = width // count
    top_device = lax.axis_index("lon") == count - 1
    below = jnp.where(is_even(), outer_ref[...], inner_ref[...])
    above = jnp.where(is_even(), inner_ref[...], outer_ref[...])
    above = jnp.where(top_device, folded_ref[...], above)

    def extended(place):
        part = slice(HALO * place, HALO * (place + 1))
        own = own_ref[rows * place : rows * (place + 1)]
        return jnp.concatenate([below[part], own, above[part]], axis=0)

    first, coeff, mask = extended(0), extended(1), extended(2)
    diagonal = (coeff + 4.0 * mask - CENTRE) * (1.0 / SPREAD)
    beside = mask * (1.0 / SPREAD)
    total = rows + 2 * HALO

    def scaled(values):
        masked = mask * values
        around = (
            pltpu.roll(masked, total - 1, 0)
            + pltpu.roll(masked, 1, 0)
            + pltpu.roll(masked, width - 1, 1)
            + pltpu.roll(masked, 1, 1)
        )
        return diagonal * values - beside * around

    vectors = [first, scaled(first)]
    while len(vectors) < BASIS + 1:
        vectors.append(2.0 * scaled(vectors[-1]) - vectors[-2])
    own = [vector[HALO : HALO + rows] for vector in vectors]
    sums = []
    for order in range(2 * BASIS):
        product = own[order // 2] * own[(order + 1) // 2]
        sums.append(jnp.sum(product, axis=0, keepdims=True))
    partial = jnp.sum(jnp.concatenate(sums, axis=0), axis=1, keepdims=True)
    lane = lax.broadcasted_iota(jnp.int32, (2 * BASIS, LANES), 1)
    place = lax.broadcasted_iota(jnp.int32, (2 * BASIS, LANES), 0)
    moments = jnp.sum(jnp.where(lane == place, partial, 0.0), axis=0, keepdims=True)
    stacked = jnp.concatenate(own[:BASIS], axis=0)
    basis_ref[...] = stacked
    if BASIS * rows < LANES:
        stacked = jnp.concatenate(
            [stacked, jnp.zeros((LANES - BASIS * rows, width), jnp.float32)], axis=0
        )
    turned = stacked.T
    for target in range(count):
        start = target * columns
        east = (start + columns) % width
        west = (start - 1) % width
        pieces = [
            turned[start : start + columns],
            turned[east : east + 1],
            turned[west : west + 1],
            moments,
            jnp.zeros((SLAB_ROWS - columns - 3, LANES), jnp.float32),
        ]
        slabs_ref[target] = jnp.concatenate(pieces, axis=0)
    core = lax.rem(lax.axis_index("lon"), 2)
    for pair in range(count // 2):
        keep_ref[pair] = slabs_ref[2 * pair + core]
        send_ref[pair] = slabs_ref[2 * pair + 1 - core]


def spread_kernel(kept_ref, came_ref, *out_refs):
    here = lax.axis_index("lon")
    core, group = lax.rem(here, 2), here // 4
    groups = len(out_refs)
    for step in range(groups):
        target = lax.rem(group + step, groups)
        for y in range(2):
            out_refs[step][y, core] = kept_ref[2 * target + y]
            out_refs[step][y, 1 - core] = came_ref[2 * target + y]


def half_kernel(*refs):
    came_refs, (_, keep_ref, send_ref) = refs[:-3], refs[-3:]
    here = lax.axis_index("lon")
    half, group = lax.rem(here // 2, 2), here // 4
    groups = len(came_refs)
    for step in range(groups):
        source = lax.rem(group + groups - step, groups)
        keep_ref[source] = came_refs[step][half]
        send_ref[source] = came_refs[step][1 - half]


def basis_weights(moments):
    gram = {}

    def inner(i, j):
        key = (i + j, abs(i - j))
        if key not in gram:
            gram[key] = 0.5 * (moments[i + j] + moments[abs(i - j)])
        return gram[key]

    matrix = [[None] * BASIS for _ in range(BASIS)]
    for i in range(BASIS):
        for j in range(i + 1):
            if i == 0:
                image = moments[1]
            elif j == 0:
                image = inner(1, i)
            else:
                image = 0.5 * (inner(i, j + 1) + inner(i, j - 1))
            matrix[i][j] = CENTRE * inner(i, j) + SPREAD * image
    right = [inner(i, 0) for i in range(BASIS)]
    start = [matrix[i][i] for i in range(BASIS)]
    inverse = []
    factors = [[None] * BASIS for _ in range(BASIS)]
    for n in range(BASIS):
        pivot = matrix[n][n]
        inverse.append(jnp.where(pivot > PIVOT_FLOOR * start[n], 1.0 / pivot, 0.0))
        for i in range(n + 1, BASIS):
            factors[i][n] = matrix[i][n] * inverse[n]
        for i in range(n + 1, BASIS):
            for j in range(n + 1, i + 1):
                matrix[i][j] = matrix[i][j] - factors[i][n] * matrix[j][n]
            right[i] = right[i] - factors[i][n] * right[n]
    weights = [None] * BASIS
    for n in reversed(range(BASIS)):
        value = right[n] * inverse[n]
        for i in range(n + 1, BASIS):
            value = value - factors[i][n] * weights[i]
        weights[n] = value
    return weights


def reverse_tile(tile):
    for axis, size in ((0, SUBLANES), (1, LANES)):
        place = lax.broadcasted_iota(jnp.int32, (SUBLANES, LANES), axis)
        step = size // 2
        while step:
            tile = jnp.where(
                (place & step) != 0,
                pltpu.roll(tile, step, axis),
                pltpu.roll(tile, size - step, axis),
            )
            step //= 2
    return tile


def load_kernel(
    old_in,
    force_in,
    coeff_in,
    mask_in,
    tracers_in,
    depth_in,
    east_depth_in,
    u_in,
    v_in,
    inner_ref,
    outer_ref,
    own_ref,
    folded_ref,
    tracers_ref,
    depth_ref,
    east_depth_ref,
    u_ref,
    v_ref,
    edge_inner_ref,
    edge_outer_ref,
    old_ref,
    force_ref,
    coeff_ref,
    mask_ref,
    sems,
):
    kinds, levels, columns, rows = tracers_ref.shape
    band = old_ref.shape[0]
    moves = [
        (old_in, old_ref),
        (force_in, force_ref),
        (coeff_in, coeff_ref),
        (mask_in, mask_ref),
        (depth_in, depth_ref),
        (east_depth_in, east_depth_ref),
        (u_in, u_ref),
    ]
    moves += [(tracers_in.at[kind], tracers_ref.at[kind]) for kind in range(kinds)]
    moves += [(v_in, v_ref)]
    copies = [
        pltpu.make_async_copy(source, target, sems.at[place])
        for place, (source, target) in enumerate(moves)
    ]
    for copy in copies:
        copy.start()
    for copy in copies[:4]:
        copy.wait()
    coeff = coeff_ref[...]
    fields = (
        coeff * old_ref[...] + force_ref[...],
        coeff,
        mask_ref[...].astype(jnp.float32),
    )
    for place, field in enumerate(fields):
        low, high = field[:HALO], field[band - HALO :]
        part = slice(HALO * place, HALO * (place + 1))
        inner_ref[part] = jnp.where(is_even(), high, low)
        outer_ref[part] = jnp.where(is_even(), low, high)
        own_ref[band * place : band * (place + 1)] = field
        tiles = high.shape[1] // LANES
        for tile in range(tiles):
            other = tiles - 1 - tile
            folded_ref[part, tile * LANES : (tile + 1) * LANES] = reverse_tile(
                high[:, other * LANES : (other + 1) * LANES]
            )
    for copy in copies[4:7]:
        copy.wait()

    def pack(kind, first, target_ref):
        for side in range(2):
            column = first + side
            for z in range(levels):
                wet = (z < depth_ref[column : column + 1]).astype(jnp.float32)
                target_ref[2 * z + side, kind : kind + 1] = (
                    tracers_ref[kind, z, column : column + 1] * wet
                )

    def pack_faces(target_ref):
        for z in range(levels):
            place = 2 * levels + z // SUBLANES
            row = z % SUBLANES
            target_ref[place, row : row + 1] = u_ref[z, columns - 1 : columns]
        place = 2 * levels + levels // SUBLANES
        target_ref[place] = jnp.broadcast_to(
            east_depth_ref[columns - 1 : columns].astype(jnp.float32), (SUBLANES, rows)
        )

    pack_faces(edge_inner_ref)
    pack_faces(edge_outer_ref)

    def pack_all(inner_column, outer_column):
        for kind in range(kinds):
            copies[7 + kind].wait()
            pack(kind, inner_column, edge_inner_ref)
            pack(kind, outer_column, edge_outer_ref)

    @pl.when(is_even())
    def _():
        pack_all(columns - 2, 0)

    @pl.when(jnp.logical_not(is_even()))
    def _():
        pack_all(0, columns - 2)

    copies[-1].wait()


def grid_tiles(columns, rows):
    return [
        (block, tile)
        for block in range(columns // SUBLANES)
        for tile in range(rows // LANES)
    ]


def tile_index(place):
    block, tile = place
    return (
        slice(block * SUBLANES, (block + 1) * SUBLANES),
        slice(tile * LANES, (tile + 1) * LANES),
    )


def shift_columns(tiles, step, outer, blocks, count):
    sublane = lax.broadcasted_iota(jnp.int32, (SUBLANES, LANES), 0)
    turned = {p: pltpu.roll(x, SUBLANES - 1 if step > 0 else 1, 0) for p, x in tiles.items()}
    inside = sublane < SUBLANES - 1 if step > 0 else sublane > 0
    shifted = {}
    for block in range(blocks):
        for tile in range(count):
            beyond = block + step
            other = turned[beyond, tile] if 0 <= beyond < blocks else outer[tile]
            shifted[block, tile] = jnp.where(inside, turned[block, tile], other)
    return shifted


def shift_rows(tiles, step, blocks, count):
    lane = lax.broadcasted_iota(jnp.int32, (SUBLANES, LANES), 1)
    turned = {p: pltpu.roll(x, LANES - 1 if step > 0 else 1, 1) for p, x in tiles.items()}
    inside = lane < LANES - 1 if step > 0 else lane > 0
    shifted = {}
    for block in range(blocks):
        for tile in range(count):
            beyond = tile + step
            other = turned[block, beyond] if 0 <= beyond < count else 0.0
            shifted[block, tile] = jnp.where(inside, turned[block, tile], other)
    return shifted


def reciprocal(value):
    guess = pl.reciprocal(value, approx=True)
    return guess * (2.0 - value * guess)


def redox_sources(masked):
    oxygen, nitrate, nitrite, ammonium, _, carbon, sulfide, nitrous = masked
    over_oxygen = reciprocal(oxygen + HALF_OXYGEN)
    with_oxygen = oxygen * over_oxygen
    no_oxygen = HALF_OXYGEN * over_oxygen
    with_nitrate = no_oxygen * nitrate * reciprocal(nitrate + HALF_NITRATE)
    rest = no_oxygen - with_nitrate
    with_nitrite = rest * nitrite * reciprocal(nitrite + HALF_NITRITE)
    with_sulfate = rest - with_nitrite
    breakdown = RATE_CARBON * carbon
    first_nitr = RATE_AMMONIUM * ammonium * with_oxygen
    second_nitr = RATE_NITRITE * nitrite * with_oxygen
    sulfide_ox = RATE_SULFIDE * sulfide * with_oxygen
    by_nitrate = 0.9 * breakdown * with_nitrate
    return (
        -1.3 * breakdown * with_oxygen - 1.5 * first_nitr - 0.5 * second_nitr - 2.0 * sulfide_ox,
        second_nitr - by_nitrate,
        by_nitrate
        - 0.6 * breakdown * with_nitrite
        + (1.0 - YIELD_NITROUS) * first_nitr
        - second_nitr,
        0.15 * breakdown - first_nitr,
        0.1 * breakdown,
        -breakdown,
        0.5 * breakdown * with_sulfate - sulfide_ox,
        YIELD_NITROUS * first_nitr - RATE_NITROUS * nitrous * no_oxygen,
    )


def source_kernel(tracers_ref, depth_ref, _, base_ref):
    kinds, levels, columns, rows = tracers_ref.shape
    places = grid_tiles(columns, rows)

    @pl.loop(0, levels)
    def _(level):
        above = jnp.maximum(level - 1, 0)
        below = jnp.minimum(level + 1, levels - 1)
        mix_up_level = jnp.where(level > 0, VERT_DIFF, 0.0)
        for p in places:
            at = tile_index(p)
            depth_here = depth_ref[at]
            wet = jnp.where(level < depth_here, 1.0, 0.0)
            mix_up = wet * mix_up_level
            mix_down = jnp.where(level + 1 < depth_here, VERT_DIFF, 0.0)
            values = [tracers_ref[(kind, level) + at] for kind in range(kinds)]
            sources = redox_sources([value * wet for value in values])
            for kind in range(kinds):
                value = values[kind]
                down = (tracers_ref[(kind, below) + at] - value) * mix_down
                up = (value - tracers_ref[(kind, above) + at]) * mix_up
                base_ref[(kind, level) + at] = value + (wet * sources[kind] + (down - up))


def turn(ref_block, target_ref, start=0):
    rows = ref_block.shape[1]
    for tile in range(rows // LANES):
        part = slice(tile * LANES, (tile + 1) * LANES)
        target_ref[start + part.start : start + part.stop] = ref_block[:, part].T


def shifted(here, other, step):
    sublane = lax.broadcasted_iota(jnp.int32, (SUBLANES, LANES), 0)
    inside = sublane < SUBLANES - step if step > 0 else sublane >= -step
    amount = (SUBLANES - step) % SUBLANES if step > 0 else -step
    other = pltpu.roll(other, amount, 0) if other is not None else 0.0
    return jnp.where(inside, pltpu.roll(here, amount, 0), other)


def row_tile(block):
    return slice(block * SUBLANES, (block + 1) * SUBLANES)


def north_kernel(
    tracers_ref,
    depth_ref,
    v_ref,
    _,
    change_ref,
    face_ref,
    depth_turned_ref,
    wet_ref,
    scale_ref,
    flow_ref,
    mix_ref,
    masked_ref,
):
    kinds, levels, columns, rows = tracers_ref.shape
    per_layer = LANES // columns
    layers = levels // per_layer
    blocks = rows // SUBLANES
    depth = depth_ref[...].astype(jnp.float32)
    turn(jnp.concatenate([depth] * per_layer, axis=0), depth_turned_ref)
    lane_level = lax.broadcasted_iota(jnp.int32, (SUBLANES, LANES), 1) // columns
    for layer in range(layers):
        span = slice(layer * per_layer, (layer + 1) * per_layer)
        turn(v_ref[span].reshape(LANES, rows), flow_ref.at[layer])
        level = (lane_level + layer * per_layer).astype(jnp.float32)
        for block in range(blocks):
            at = row_tile(block)
            here = depth_turned_ref[at]
            after = depth_turned_ref[row_tile(block + 1)] if block + 1 < blocks else None
            is_open = level < jnp.minimum(here, shifted(here, after, 1))
            scale = jnp.where(is_open, 1.0 / 12.0, 0.0)
            wet_ref[layer, at] = jnp.where(level < here, 1.0, 0.0)
            scale_ref[layer, at] = scale
            mix_ref[layer, at] = jnp.where(is_open, HORIZ_DIFF, 0.0)
            flow_ref[layer, at] = flow_ref[layer, at] * scale

    @pl.loop(0, kinds)
    def _(kind):
        for layer in range(layers):
            span = slice(layer * per_layer, (layer + 1) * per_layer)
            turn(tracers_ref[kind, span].reshape(LANES, rows), masked_ref.at[layer])
            tiles = [
                masked_ref[layer, row_tile(block)] * wet_ref[layer, row_tile(block)]
                for block in range(blocks)
            ]
            before = None
            for block in range(blocks):
                at = row_tile(block)
                here = tiles[block]
                after = tiles[block + 1] if block + 1 < blocks else None
                one = shifted(here, after, 1)
                two = shifted(here, after, 2)
                south = shifted(here, tiles[block - 1] if block else None, -1)
                face = 7.0 * (here + one) - (south + two)
                face_ref[kind, layer, at] = face * scale_ref[layer, at]
                flux = face * flow_ref[layer, at] - (one - here) * mix_ref[layer, at]
                change_ref[kind, layer, at] = shifted(flux, before, -1) - flux
                before = flux


def east_kernel(
    tracers_ref,
    depth_ref,
    east_depth_ref,
    u_ref,
    inner_ref,
    outer_ref,
    own_inner_ref,
    own_outer_ref,
    before_ref,
    _,
    base_ref,
    face_east_ref,
    face_west_ref,
    flux_west_ref,
    from_west_ref,
    from_east_ref,
    own_west_ref,
):
    kinds, levels, columns, rows = tracers_ref.shape
    blocks, count = columns // SUBLANES, rows // LANES
    places = grid_tiles(columns, rows)
    for place in range(inner_ref.shape[0]):
        from_west_ref[place] = jnp.where(is_even(), outer_ref[place], inner_ref[place])
    for place in range(2 * levels):
        from_east_ref[place] = jnp.where(is_even(), inner_ref[place], outer_ref[place])
        own_west_ref[place] = jnp.where(is_even(), own_outer_ref[place], own_inner_ref[place])
    depth_west = from_west_ref[2 * levels + levels // SUBLANES]
    for z in range(levels):
        row = z % SUBLANES
        u_west = from_west_ref[2 * levels + z // SUBLANES, row : row + 1]
        center, east_one = from_west_ref[2 * z + 1], own_west_ref[2 * z]
        outer = from_west_ref[2 * z] + own_west_ref[2 * z + 1]
        scale_west = jnp.where(z < depth_west, 1.0 / 12.0, 0.0)
        mix_west = jnp.where(z < depth_west, HORIZ_DIFF, 0.0)
        face = (7.0 * (center + east_one) - outer) * scale_west
        for kind in range(kinds):
            face_west_ref[kind, z : z + 1] = face[kind : kind + 1]
        flux_west_ref[z] = u_west * face - mix_west * (east_one - center)

    @pl.loop(0, levels)
    def _(level):
        wet, scale, mix = {}, {}, {}
        for p in places:
            at = tile_index(p)
            wet[p] = jnp.where(level < depth_ref[at], 1.0, 0.0)
            is_open = level < east_depth_ref[at]
            scale[p] = jnp.where(is_open, 1.0 / 12.0, 0.0)
            mix[p] = jnp.where(is_open, HORIZ_DIFF, 0.0)
        for kind in range(kinds):
            def halo(ref, index):
                return [
                    jnp.broadcast_to(
                        ref[index, kind : kind + 1, tile * LANES : (tile + 1) * LANES],
                        (SUBLANES, LANES),
                    )
                    for tile in range(count)
                ]

            masked = {p: tracers_ref[(kind, level) + tile_index(p)] * wet[p] for p in places}
            one = shift_columns(masked, 1, halo(from_east_ref, 2 * level), blocks, count)
            two = shift_columns(one, 1, halo(from_east_ref, 2 * level + 1), blocks, count)
            west = shift_columns(masked, -1, halo(from_west_ref, 2 * level + 1), blocks, count)
            flux = {}
            for p in places:
                at = (kind, level) + tile_index(p)
                face = (7.0 * (masked[p] + one[p]) - (west[p] + two[p])) * scale[p]
                face_east_ref[at] = face
                flux[p] = u_ref[(level,) + tile_index(p)] * face - mix[p] * (one[p] - masked[p])
            incoming = shift_columns(flux, -1, halo(flux_west_ref, level), blocks, count)
            for p in places:
                at = (kind, level) + tile_index(p)
                base_ref[at] = before_ref[at] + (incoming[p] - flux[p])


def update_kernel(
    kept_ref,
    came_ref,
    basis_ref,
    base_ref,
    face_east_ref,
    face_west_ref,
    change_ref,
    face_north_ref,
    surface_ref,
    out_ref,
    slabs_ref,
    height_ref,
    flow_ref,
    turned_ref,
    result_ref,
    sems,
):
    half = lax.rem(lax.axis_index("lon") // 2, 2)
    for source in range(kept_ref.shape[0]):
        for core in range(2):
            slabs_ref[4 * source + 2 * half + core] = kept_ref[source, core]
            slabs_ref[4 * source + 2 * (1 - half) + core] = came_ref[source, core]
    kinds, levels, columns, rows = base_ref.shape
    blocks, count = columns // SUBLANES, rows // LANES
    places = grid_tiles(columns, rows)
    sources, slab_rows, _ = slabs_ref.shape
    band, width = surface_ref.shape
    parts = [slabs_ref[source, columns + 2 : columns + 3] for source in range(sources)]
    while len(parts) > 1:
        parts = [a + b for a, b in zip(parts[::2], parts[1::2])]
    dots = [jnp.broadcast_to(parts[0][:, m : m + 1], (1, LANES)) for m in range(2 * BASIS)]
    weights = basis_weights(
        dots[:2] + [2.0 * dots[m] - dots[m % 2] for m in range(2, 2 * BASIS)]
    )
    lane_group = lax.broadcasted_iota(jnp.int32, (1, LANES), 1) // band
    lane_weight = jnp.zeros((1, LANES), jnp.float32)
    for k in range(BASIS):
        lane_weight = jnp.where(lane_group == k, weights[k], lane_weight)
    for tile in range(width // LANES):
        part = slice(tile * LANES, (tile + 1) * LANES)
        surface = weights[0] * basis_ref[:band, part]
        for k in range(1, BASIS):
            surface = surface + weights[k] * basis_ref[k * band : (k + 1) * band, part]
        surface_ref[:, part] = surface

    fill = LANES // band
    group_full = lax.broadcasted_iota(jnp.int32, (slab_rows, LANES), 1) // band
    height, east_edge, west_edge = {}, [], []
    for tile in range(count):
        joined = None
        for p in range(fill):
            part = slabs_ref[tile * fill + p] * lane_weight
            shift = LANES // 2
            while shift >= band:
                part = part + pltpu.roll(part, shift, 1)
                shift //= 2
            joined = part if joined is None else jnp.where(group_full == p, part, joined)
        for block in range(blocks):
            height[block, tile] = joined[block * SUBLANES : (block + 1) * SUBLANES]
        east_edge.append(jnp.broadcast_to(joined[columns : columns + 1], (SUBLANES, LANES)))
        west_edge.append(
            jnp.broadcast_to(joined[columns + 1 : columns + 2], (SUBLANES, LANES))
        )
    height_east = shift_columns(height, 1, east_edge, blocks, count)
    flow_east = {p: -BARO_GAIN * (height_east[p] - height[p]) for p in places}
    per_layer = LANES // columns
    layers = levels // per_layer
    row_blocks = rows // SUBLANES
    for p in places:
        for repeat in range(per_layer):
            at = tile_index(p)
            start = repeat * columns
            height_ref[start + at[0].start : start + at[0].stop, at[1]] = height[p]
    turn(height_ref, turned_ref)
    for block in range(row_blocks):
        here = turned_ref[row_tile(block)]
        after = turned_ref[row_tile(block + 1)] if block + 1 < row_blocks else None
        flow_ref[row_tile(block)] = -BARO_GAIN * (shifted(here, after, 1) - here)
    flow_west = [
        -BARO_GAIN * (jnp.broadcast_to(height[0, tile][:1], (SUBLANES, LANES)) - west_edge[tile])
        for tile in range(count)
    ]

    def copy(kind):
        return pltpu.make_async_copy(result_ref.at[kind], out_ref.at[kind], sems.at[kind])

    @pl.loop(0, kinds)
    def _(kind):
        for layer in range(layers):
            before = None
            for block in range(row_blocks):
                at = row_tile(block)
                flux = flow_ref[at] * face_north_ref[kind, layer, at]
                turned_ref[at] = change_ref[kind, layer, at] + (shifted(flux, before, -1) - flux)
                before = flux
            for tile in range(count):
                part = slice(tile * LANES, (tile + 1) * LANES)
                along = turned_ref[part].T
                for z in range(per_layer):
                    level = layer * per_layer + z
                    flux_east = {
                        (block, tile): flow_east[block, tile]
                        * face_east_ref[(kind, level) + tile_index((block, tile))]
                        for block in range(blocks)
                    }
                    edge = flow_west[tile] * jnp.broadcast_to(
                        face_west_ref[kind, level : level + 1, part], (SUBLANES, LANES)
                    )
                    for block in range(blocks):
                        at = (kind, level) + tile_index((block, tile))
                        start = z * columns + block * SUBLANES
                        west = flux_east[block - 1, tile] if block else edge
                        flux = flux_east[block, tile]
                        result_ref[at] = base_ref[at] + (
                            (shifted(flux, west, -1) - flux) + along[start : start + SUBLANES]
                        )
        copy(kind).start()

    for kind in range(kinds):
        copy(kind).wait()


def body(
    surface_old,
    surface_forcing,
    surface_coeff,
    ocean_mask,
    column_depth,
    east_depth,
    tracers,
    u_clinic,
    v_clinic,
):
    band, width = surface_old.shape
    kinds, levels, columns, rows = tracers.shape
    count = lax.axis_size("lon")
    f32 = jnp.float32
    sds = jax.ShapeDtypeStruct
    vmem = pl.BlockSpec(memory_space=pltpu.VMEM)
    hbm = pl.BlockSpec(memory_space=pltpu.HBM)
    fields = (surface_old, surface_forcing, surface_coeff, ocean_mask)
    pairs_inner = [(i, i ^ 1) for i in range(count)]
    ring = [(i, (i + 1 if i % 2 else i - 1) % count) for i in range(count)]
    pairs_outer = [(i, j) for i, j in ring if abs(i - j) == 1]

    def call(
        kernel, out_shape, name, operands, scratch=(), limit=SMALL_VMEM, cost=0, far=()
    ):
        return pl.pallas_call(
            kernel,
            out_shape=out_shape,
            in_specs=[hbm if place in far else vmem for place in range(len(operands))],
            out_specs=[pl.BlockSpec(memory_space=pl.ANY) if x is result else vmem for x in out_shape],
            scratch_shapes=list(scratch),
            compiler_params=pltpu.CompilerParams(vmem_limit_bytes=limit),
            cost_estimate=pl.CostEstimate(
                flops=cost * tracers.size, bytes_accessed=8 * tracers.size, transcendentals=0
            )
            if cost
            else None,
            name=name,
        )(
            *(
                pltpu.with_memory_space_constraint(x, pltpu.HBM) if place in far else x
                for place, x in enumerate(operands)
            )
        )

    result = sds(tracers.shape, f32)
    packed = sds((3 * HALO, width), f32)
    held = pltpu.VMEM(tracers.shape, f32)

    def fetched(x):
        return pltpu.VMEM(x.shape, x.dtype)

    edges = sds((2 * levels + levels // SUBLANES + 1, kinds, rows), f32)
    inputs = (tracers, column_depth, east_depth, u_clinic, v_clinic)
    (inner, outer, own, folded, *inputs, own_inner, own_outer) = call(
        load_kernel,
        (
            packed,
            packed,
            sds((3 * band, width), f32),
            packed,
            *(fetched(x) for x in inputs),
            edges,
            edges,
        ),
        "load",
        (*fields, *inputs),
        scratch=[pltpu.VMEM(x.shape, x.dtype) for x in fields]
        + [pltpu.SemaphoreType.DMA((8 + kinds,))],
        far=range(9),
    )
    tracers, column_depth, east_depth, u_clinic, v_clinic = inputs
    came_inner = lax.ppermute(inner, "lon", pairs_inner)
    came_outer = lax.ppermute(outer, "lon", pairs_outer)

    groups = count // 4
    half_slabs = sds((count // 2, SLAB_ROWS, LANES), f32)
    basis, keep, send = call(
        basis_kernel,
        (sds((BASIS * band, width), f32), half_slabs, half_slabs),
        "solver_basis",
        (own, came_inner, came_outer, folded),
        scratch=[pltpu.VMEM((count, SLAB_ROWS, LANES), f32)],
        cost=2000,
    )
    came = lax.ppermute(send, "lon", pairs_inner)
    sends = call(
        spread_kernel,
        (sds((2, 2, SLAB_ROWS, LANES), f32),) * groups,
        "spread_slabs",
        (keep, came),
    )
    slabs = [sends[0]]
    for step in range(1, groups):
        pairs = [(i, (i + 4 * step) % count) for i in range(count)]
        slabs.append(lax.ppermute(sends[step], "lon", pairs))
    edge_inner = lax.ppermute(own_inner, "lon", pairs_inner)
    edge_outer = lax.ppermute(own_outer, "lon", ring)
    (base,) = call(source_kernel, (held,), "sources", (tracers, column_depth, own_inner), cost=2000)
    turned = (kinds, levels * columns // LANES, rows, LANES)
    change, face_north = call(
        north_kernel,
        (pltpu.VMEM(turned, f32), pltpu.VMEM(turned, f32)),
        "north_fluxes",
        (tracers, column_depth, v_clinic, sends[0]),
        scratch=[pltpu.VMEM((rows, LANES), f32)] + [pltpu.VMEM(turned[1:], f32)] * 5,
        cost=2000,
    )
    quarter = sds((groups, 2, SLAB_ROWS, LANES), f32)
    keep, send = call(half_kernel, (quarter, quarter), "split_halves", (*slabs, change))
    came = lax.ppermute(send, "lon", [(i, i ^ 2) for i in range(count)])
    base, face_east, face_west = call(
        east_kernel,
        (held, held, pltpu.VMEM((kinds, levels, rows), f32)),
        "east_fluxes",
        (
            tracers,
            column_depth,
            east_depth,
            u_clinic,
            edge_inner,
            edge_outer,
            own_inner,
            own_outer,
            base,
            keep,
        ),
        scratch=[
            pltpu.VMEM((levels, kinds, rows), f32),
            pltpu.VMEM(edges.shape, f32),
            pltpu.VMEM(edges.shape, f32),
            pltpu.VMEM(edges.shape, f32),
        ],
        cost=2000,
    )
    return tuple(
        call(
            update_kernel,
            (sds((band, width), f32), result),
            "surface_update",
            (keep, came, basis, base, face_east, face_west, change, face_north),
            scratch=[
                pltpu.VMEM((count, SLAB_ROWS, LANES), f32),
                pltpu.VMEM((LANES, rows), f32),
                pltpu.VMEM((rows, LANES), f32),
                pltpu.VMEM((rows, LANES), f32),
                pltpu.VMEM(tracers.shape, f32),
                pltpu.SemaphoreType.DMA((kinds,)),
            ],
            limit=RESULT_VMEM,
        )
    )


def solution(mesh):
    in_specs = (
        P(("member", "lon"), None),
        P(("member", "lon"), None),
        P("lon", None),
        P("lon", None),
        P("lon", None),
        P("lon", None),
        P("member", None, "lon", None),
        P("member", "lon", None),
        P("member", "lon", None),
    )
    out_specs = (P(("member", "lon"), None), P("member", None, "lon", None))
    return jax.shard_map(body, mesh=mesh, in_specs=in_specs, out_specs=out_specs, check_vma=False)
```

```python
import jax
import jax.numpy as jnp
from jax import lax
from jax.experimental import pallas as pl
from jax.experimental.pallas import tpu as pltpu
from jax.sharding import PartitionSpec as P

BARO_GAIN = 0.1
HORIZ_DIFF = 0.1
VERT_DIFF = 0.15
RATE_CARBON = 0.3
RATE_AMMONIUM = 0.2
RATE_NITRITE = 0.2
RATE_SULFIDE = 0.3
RATE_NITROUS = 0.2
HALF_OXYGEN = 0.3
HALF_NITRATE = 0.3
HALF_NITRITE = 0.3
YIELD_NITROUS = 0.3


SUBLANES = 8
LANES = 128
SMALL_VMEM = 4 * 2**20
RESULT_VMEM = 14 * 2**20
HALO = 8
SLAB_ROWS = 24
BASIS = 4
CENTRE = 4.55
SPREAD = 4.45
PIVOT_FLOOR = 3e-7


def is_even():
    return lax.rem(lax.axis_index("lon"), 2) == 0


def pack_kernel(old_in, force_in, coeff_in, mask_in, inner_ref, outer_ref, own_ref, *scratch):
    old_ref, force_ref, coeff_ref, mask_ref, sems = scratch
    copies = [
        pltpu.make_async_copy(source, target, sems.at[place])
        for place, (source, target) in enumerate(
            zip((old_in, force_in, coeff_in, mask_in), (old_ref, force_ref, coeff_ref, mask_ref))
        )
    ]
    for copy in copies:
        copy.start()
    for copy in copies:
        copy.wait()
    rows = old_ref.shape[0]
    coeff = coeff_ref[...]
    fields = (
        coeff * old_ref[...] + force_ref[...],
        coeff,
        mask_ref[...].astype(jnp.float32),
    )
    for place, field in enumerate(fields):
        low, high = field[:HALO], field[rows - HALO :]
        part = slice(HALO * place, HALO * (place + 1))
        inner_ref[part] = jnp.where(is_even(), high, low)
        outer_ref[part] = jnp.where(is_even(), low, high)
        own_ref[rows * place : rows * (place + 1)] = field


def basis_kernel(
    own_ref,
    inner_ref,
    outer_ref,
    folded_ref,
    basis_ref,
    keep_ref,
    send_ref,
    slabs_ref,
):
    rows, width = own_ref.shape[0] // 3, own_ref.shape[1]
    count = slabs_ref.shape[0]
    columns = width // count
    top_device = lax.axis_index("lon") == count - 1
    below = jnp.where(is_even(), outer_ref[...], inner_ref[...])
    above = jnp.where(is_even(), inner_ref[...], outer_ref[...])
    above = jnp.where(top_device, folded_ref[...], above)

    def extended(place):
        part = slice(HALO * place, HALO * (place + 1))
        own = own_ref[rows * place : rows * (place + 1)]
        return jnp.concatenate([below[part], own, above[part]], axis=0)

    first, coeff, mask = extended(0), extended(1), extended(2)
    diagonal = (coeff + 4.0 * mask - CENTRE) * (1.0 / SPREAD)
    beside = mask * (1.0 / SPREAD)
    total = rows + 2 * HALO

    def scaled(values):
        masked = mask * values
        around = (
            pltpu.roll(masked, total - 1, 0)
            + pltpu.roll(masked, 1, 0)
            + pltpu.roll(masked, width - 1, 1)
            + pltpu.roll(masked, 1, 1)
        )
        return diagonal * values - beside * around

    vectors = [first, scaled(first)]
    while len(vectors) < BASIS + 1:
        vectors.append(2.0 * scaled(vectors[-1]) - vectors[-2])
    own = [vector[HALO : HALO + rows] for vector in vectors]
    sums = []
    for order in range(2 * BASIS):
        product = own[order // 2] * own[(order + 1) // 2]
        sums.append(jnp.sum(product, axis=0, keepdims=True))
    partial = jnp.sum(jnp.concatenate(sums, axis=0), axis=1, keepdims=True)
    lane = lax.broadcasted_iota(jnp.int32, (2 * BASIS, LANES), 1)
    place = lax.broadcasted_iota(jnp.int32, (2 * BASIS, LANES), 0)
    moments = jnp.sum(jnp.where(lane == place, partial, 0.0), axis=0, keepdims=True)
    stacked = jnp.concatenate(own[:BASIS], axis=0)
    basis_ref[...] = stacked
    if BASIS * rows < LANES:
        stacked = jnp.concatenate(
            [stacked, jnp.zeros((LANES - BASIS * rows, width), jnp.float32)], axis=0
        )
    turned = stacked.T
    for target in range(count):
        start = target * columns
        east = (start + columns) % width
        west = (start - 1) % width
        pieces = [
            turned[start : start + columns],
            turned[east : east + 1],
            turned[west : west + 1],
            moments,
            jnp.zeros((SLAB_ROWS - columns - 3, LANES), jnp.float32),
        ]
        slabs_ref[target] = jnp.concatenate(pieces, axis=0)
    core = lax.rem(lax.axis_index("lon"), 2)
    for pair in range(count // 2):
        keep_ref[pair] = slabs_ref[2 * pair + core]
        send_ref[pair] = slabs_ref[2 * pair + 1 - core]


def spread_kernel(kept_ref, came_ref, *out_refs):
    here = lax.axis_index("lon")
    core, group = lax.rem(here, 2), here // 4
    groups = len(out_refs)
    for step in range(groups):
        target = lax.rem(group + step, groups)
        for y in range(2):
            out_refs[step][y, core] = kept_ref[2 * target + y]
            out_refs[step][y, 1 - core] = came_ref[2 * target + y]


def half_kernel(*refs):
    came_refs, (_, keep_ref, send_ref) = refs[:-3], refs[-3:]
    here = lax.axis_index("lon")
    half, group = lax.rem(here // 2, 2), here // 4
    groups = len(came_refs)
    for step in range(groups):
        source = lax.rem(group + groups - step, groups)
        keep_ref[source] = came_refs[step][half]
        send_ref[source] = came_refs[step][1 - half]


def basis_weights(moments):
    gram = {}

    def inner(i, j):
        key = (i + j, abs(i - j))
        if key not in gram:
            gram[key] = 0.5 * (moments[i + j] + moments[abs(i - j)])
        return gram[key]

    matrix = [[None] * BASIS for _ in range(BASIS)]
    for i in range(BASIS):
        for j in range(i + 1):
            if i == 0:
                image = moments[1]
            elif j == 0:
                image = inner(1, i)
            else:
                image = 0.5 * (inner(i, j + 1) + inner(i, j - 1))
            matrix[i][j] = CENTRE * inner(i, j) + SPREAD * image
    right = [inner(i, 0) for i in range(BASIS)]
    start = [matrix[i][i] for i in range(BASIS)]
    inverse = []
    factors = [[None] * BASIS for _ in range(BASIS)]
    for n in range(BASIS):
        pivot = matrix[n][n]
        inverse.append(jnp.where(pivot > PIVOT_FLOOR * start[n], 1.0 / pivot, 0.0))
        for i in range(n + 1, BASIS):
            factors[i][n] = matrix[i][n] * inverse[n]
        for i in range(n + 1, BASIS):
            for j in range(n + 1, i + 1):
                matrix[i][j] = matrix[i][j] - factors[i][n] * matrix[j][n]
            right[i] = right[i] - factors[i][n] * right[n]
    weights = [None] * BASIS
    for n in reversed(range(BASIS)):
        value = right[n] * inverse[n]
        for i in range(n + 1, BASIS):
            value = value - factors[i][n] * weights[i]
        weights[n] = value
    return weights


def reverse_tile(tile):
    for axis, size in ((0, SUBLANES), (1, LANES)):
        place = lax.broadcasted_iota(jnp.int32, (SUBLANES, LANES), axis)
        step = size // 2
        while step:
            tile = jnp.where(
                (place & step) != 0,
                pltpu.roll(tile, step, axis),
                pltpu.roll(tile, size - step, axis),
            )
            step //= 2
    return tile


def fold_kernel(high_ref, _, folded_ref):
    tiles = high_ref.shape[1] // LANES
    for place in range(3):
        part = slice(HALO * place, HALO * (place + 1))
        for tile in range(tiles):
            other = tiles - 1 - tile
            folded_ref[part, tile * LANES : (tile + 1) * LANES] = reverse_tile(
                high_ref[part, other * LANES : (other + 1) * LANES]
            )


def edge_kernel(tracers_ref, depth_ref, east_depth_ref, u_ref, _, inner_ref, outer_ref):
    kinds, levels, columns, rows = tracers_ref.shape

    def pack(first, target_ref):
        for side in range(2):
            column = first + side
            for z in range(levels):
                wet = (z < depth_ref[column : column + 1]).astype(jnp.float32)
                for kind in range(kinds):
                    target_ref[2 * z + side, kind : kind + 1] = (
                        tracers_ref[kind, z, column : column + 1] * wet
                    )

    def pack_faces(target_ref):
        for z in range(levels):
            place = 2 * levels + z // SUBLANES
            row = z % SUBLANES
            target_ref[place, row : row + 1] = u_ref[z, columns - 1 :]
        place = 2 * levels + levels // SUBLANES
        target_ref[place] = jnp.broadcast_to(
            east_depth_ref[columns - 1 : columns].astype(jnp.float32), (SUBLANES, rows)
        )

    @pl.when(is_even())
    def _():
        pack(columns - 2, inner_ref)
        pack(0, outer_ref)

    @pl.when(jnp.logical_not(is_even()))
    def _():
        pack(0, inner_ref)
        pack(columns - 2, outer_ref)

    pack_faces(inner_ref)
    pack_faces(outer_ref)


def grid_tiles(columns, rows):
    return [
        (block, tile)
        for block in range(columns // SUBLANES)
        for tile in range(rows // LANES)
    ]


def tile_index(place):
    block, tile = place
    return (
        slice(block * SUBLANES, (block + 1) * SUBLANES),
        slice(tile * LANES, (tile + 1) * LANES),
    )


def shift_columns(tiles, step, outer, blocks, count):
    sublane = lax.broadcasted_iota(jnp.int32, (SUBLANES, LANES), 0)
    turned = {p: pltpu.roll(x, SUBLANES - 1 if step > 0 else 1, 0) for p, x in tiles.items()}
    inside = sublane < SUBLANES - 1 if step > 0 else sublane > 0
    shifted = {}
    for block in range(blocks):
        for tile in range(count):
            beyond = block + step
            other = turned[beyond, tile] if 0 <= beyond < blocks else outer[tile]
            shifted[block, tile] = jnp.where(inside, turned[block, tile], other)
    return shifted


def shift_rows(tiles, step, blocks, count):
    lane = lax.broadcasted_iota(jnp.int32, (SUBLANES, LANES), 1)
    turned = {p: pltpu.roll(x, LANES - 1 if step > 0 else 1, 1) for p, x in tiles.items()}
    inside = lane < LANES - 1 if step > 0 else lane > 0
    shifted = {}
    for block in range(blocks):
        for tile in range(count):
            beyond = tile + step
            other = turned[block, beyond] if 0 <= beyond < count else 0.0
            shifted[block, tile] = jnp.where(inside, turned[block, tile], other)
    return shifted


def reciprocal(value):
    guess = pl.reciprocal(value, approx=True)
    return guess * (2.0 - value * guess)


def redox_sources(masked):
    oxygen, nitrate, nitrite, ammonium, _, carbon, sulfide, nitrous = masked
    over_oxygen = reciprocal(oxygen + HALF_OXYGEN)
    with_oxygen = oxygen * over_oxygen
    no_oxygen = HALF_OXYGEN * over_oxygen
    with_nitrate = no_oxygen * nitrate * reciprocal(nitrate + HALF_NITRATE)
    rest = no_oxygen - with_nitrate
    with_nitrite = rest * nitrite * reciprocal(nitrite + HALF_NITRITE)
    with_sulfate = rest - with_nitrite
    breakdown = RATE_CARBON * carbon
    first_nitr = RATE_AMMONIUM * ammonium * with_oxygen
    second_nitr = RATE_NITRITE * nitrite * with_oxygen
    sulfide_ox = RATE_SULFIDE * sulfide * with_oxygen
    by_nitrate = 0.9 * breakdown * with_nitrate
    return (
        -1.3 * breakdown * with_oxygen - 1.5 * first_nitr - 0.5 * second_nitr - 2.0 * sulfide_ox,
        second_nitr - by_nitrate,
        by_nitrate
        - 0.6 * breakdown * with_nitrite
        + (1.0 - YIELD_NITROUS) * first_nitr
        - second_nitr,
        0.15 * breakdown - first_nitr,
        0.1 * breakdown,
        -breakdown,
        0.5 * breakdown * with_sulfate - sulfide_ox,
        YIELD_NITROUS * first_nitr - RATE_NITROUS * nitrous * no_oxygen,
    )


def source_kernel(tracers_ref, depth_ref, _, base_ref, masked_ref):
    kinds, levels, columns, rows = tracers_ref.shape
    places = grid_tiles(columns, rows)

    @pl.loop(0, levels)
    def _(level):
        above = jnp.maximum(level - 1, 0)
        below = jnp.minimum(level + 1, levels - 1)
        mix_up_level = jnp.where(level > 0, VERT_DIFF, 0.0)
        for p in places:
            at = tile_index(p)
            depth_here = depth_ref[at]
            wet = jnp.where(level < depth_here, 1.0, 0.0)
            mix_up = wet * mix_up_level
            mix_down = jnp.where(level + 1 < depth_here, VERT_DIFF, 0.0)
            values = [tracers_ref[(kind, level) + at] for kind in range(kinds)]
            masked = [value * wet for value in values]
            sources = redox_sources(masked)
            for kind in range(kinds):
                masked_ref[(kind, level) + at] = masked[kind]
                value = values[kind]
                down = (tracers_ref[(kind, below) + at] - value) * mix_down
                up = (value - tracers_ref[(kind, above) + at]) * mix_up
                base_ref[(kind, level) + at] = value + (sources[kind] + (down - up))


def turn(ref_block, target_ref, start=0):
    rows = ref_block.shape[1]
    for tile in range(rows // LANES):
        part = slice(tile * LANES, (tile + 1) * LANES)
        target_ref[start + part.start : start + part.stop] = ref_block[:, part].T


def shifted(here, other, step):
    sublane = lax.broadcasted_iota(jnp.int32, (SUBLANES, LANES), 0)
    inside = sublane < SUBLANES - step if step > 0 else sublane >= -step
    amount = (SUBLANES - step) % SUBLANES if step > 0 else -step
    other = pltpu.roll(other, amount, 0) if other is not None else 0.0
    return jnp.where(inside, pltpu.roll(here, amount, 0), other)


def row_tile(block):
    return slice(block * SUBLANES, (block + 1) * SUBLANES)


def north_kernel(
    masked_in,
    depth_ref,
    v_ref,
    _,
    change_ref,
    face_ref,
    depth_turned_ref,
    scale_ref,
    flow_ref,
    mix_ref,
    masked_ref,
):
    kinds, levels, columns, rows = masked_in.shape
    per_layer = LANES // columns
    layers = levels // per_layer
    blocks = rows // SUBLANES
    depth = depth_ref[...].astype(jnp.float32)
    turn(jnp.concatenate([depth] * per_layer, axis=0), depth_turned_ref)
    lane_level = lax.broadcasted_iota(jnp.int32, (SUBLANES, LANES), 1) // columns
    for layer in range(layers):
        span = slice(layer * per_layer, (layer + 1) * per_layer)
        turn(v_ref[span].reshape(LANES, rows), flow_ref.at[layer])
        level = (lane_level + layer * per_layer).astype(jnp.float32)
        for block in range(blocks):
            at = row_tile(block)
            here = depth_turned_ref[at]
            after = depth_turned_ref[row_tile(block + 1)] if block + 1 < blocks else None
            is_open = level < jnp.minimum(here, shifted(here, after, 1))
            scale = jnp.where(is_open, 1.0 / 12.0, 0.0)
            scale_ref[layer, at] = scale
            mix_ref[layer, at] = jnp.where(is_open, HORIZ_DIFF, 0.0)
            flow_ref[layer, at] = flow_ref[layer, at] * scale

    @pl.loop(0, kinds)
    def _(kind):
        for layer in range(layers):
            span = slice(layer * per_layer, (layer + 1) * per_layer)
            turn(masked_in[kind, span].reshape(LANES, rows), masked_ref.at[layer])
            tiles = [masked_ref[layer, row_tile(block)] for block in range(blocks)]
            before = None
            for block in range(blocks):
                at = row_tile(block)
                here = tiles[block]
                after = tiles[block + 1] if block + 1 < blocks else None
                one = shifted(here, after, 1)
                two = shifted(here, after, 2)
                south = shifted(here, tiles[block - 1] if block else None, -1)
                face = 7.0 * (here + one) - (south + two)
                face_ref[kind, layer, at] = face * scale_ref[layer, at]
                flux = face * flow_ref[layer, at] - (one - here) * mix_ref[layer, at]
                change_ref[kind, layer, at] = shifted(flux, before, -1) - flux
                before = flux


def east_kernel(
    masked_ref,
    east_depth_ref,
    u_ref,
    inner_ref,
    outer_ref,
    own_inner_ref,
    own_outer_ref,
    before_ref,
    _,
    base_ref,
    face_east_ref,
    face_west_ref,
    flux_west_ref,
    from_west_ref,
    from_east_ref,
    own_west_ref,
):
    kinds, levels, columns, rows = masked_ref.shape
    blocks, count = columns // SUBLANES, rows // LANES
    places = grid_tiles(columns, rows)
    for place in range(inner_ref.shape[0]):
        from_west_ref[place] = jnp.where(is_even(), outer_ref[place], inner_ref[place])
    for place in range(2 * levels):
        from_east_ref[place] = jnp.where(is_even(), inner_ref[place], outer_ref[place])
        own_west_ref[place] = jnp.where(is_even(), own_outer_ref[place], own_inner_ref[place])
    depth_west = from_west_ref[2 * levels + levels // SUBLANES]
    for z in range(levels):
        row = z % SUBLANES
        u_west = from_west_ref[2 * levels + z // SUBLANES, row : row + 1]
        center, east_one = from_west_ref[2 * z + 1], own_west_ref[2 * z]
        outer = from_west_ref[2 * z] + own_west_ref[2 * z + 1]
        scale_west = jnp.where(z < depth_west, 1.0 / 12.0, 0.0)
        mix_west = jnp.where(z < depth_west, HORIZ_DIFF, 0.0)
        face = (7.0 * (center + east_one) - outer) * scale_west
        for kind in range(kinds):
            face_west_ref[kind, z : z + 1] = face[kind : kind + 1]
        flux_west_ref[z] = u_west * face - mix_west * (east_one - center)

    @pl.loop(0, levels)
    def _(level):
        scale, mix = {}, {}
        for p in places:
            at = tile_index(p)
            is_open = level < east_depth_ref[at]
            scale[p] = jnp.where(is_open, 1.0 / 12.0, 0.0)
            mix[p] = jnp.where(is_open, HORIZ_DIFF, 0.0)
        for kind in range(kinds):
            def halo(ref, index):
                return [
                    jnp.broadcast_to(
                        ref[index, kind : kind + 1, tile * LANES : (tile + 1) * LANES],
                        (SUBLANES, LANES),
                    )
                    for tile in range(count)
                ]

            masked = {p: masked_ref[(kind, level) + tile_index(p)] for p in places}
            one = shift_columns(masked, 1, halo(from_east_ref, 2 * level), blocks, count)
            two = shift_columns(one, 1, halo(from_east_ref, 2 * level + 1), blocks, count)
            west = shift_columns(masked, -1, halo(from_west_ref, 2 * level + 1), blocks, count)
            flux = {}
            for p in places:
                at = (kind, level) + tile_index(p)
                face = (7.0 * (masked[p] + one[p]) - (west[p] + two[p])) * scale[p]
                face_east_ref[at] = face
                flux[p] = u_ref[(level,) + tile_index(p)] * face - mix[p] * (one[p] - masked[p])
            incoming = shift_columns(flux, -1, halo(flux_west_ref, level), blocks, count)
            for p in places:
                at = (kind, level) + tile_index(p)
                base_ref[at] = before_ref[at] + (incoming[p] - flux[p])


def update_kernel(
    kept_ref,
    came_ref,
    basis_ref,
    base_ref,
    face_east_ref,
    face_west_ref,
    change_ref,
    face_north_ref,
    surface_ref,
    out_ref,
    slabs_ref,
    height_ref,
    flow_ref,
    turned_ref,
    result_ref,
    sems,
):
    half = lax.rem(lax.axis_index("lon") // 2, 2)
    for source in range(kept_ref.shape[0]):
        for core in range(2):
            slabs_ref[4 * source + 2 * half + core] = kept_ref[source, core]
            slabs_ref[4 * source + 2 * (1 - half) + core] = came_ref[source, core]
    kinds, levels, columns, rows = base_ref.shape
    blocks, count = columns // SUBLANES, rows // LANES
    places = grid_tiles(columns, rows)
    sources, slab_rows, _ = slabs_ref.shape
    band, width = surface_ref.shape
    parts = [slabs_ref[source, columns + 2 : columns + 3] for source in range(sources)]
    while len(parts) > 1:
        parts = [a + b for a, b in zip(parts[::2], parts[1::2])]
    dots = [jnp.broadcast_to(parts[0][:, m : m + 1], (1, LANES)) for m in range(2 * BASIS)]
    weights = basis_weights(
        dots[:2] + [2.0 * dots[m] - dots[m % 2] for m in range(2, 2 * BASIS)]
    )
    lane_group = lax.broadcasted_iota(jnp.int32, (1, LANES), 1) // band
    lane_weight = jnp.zeros((1, LANES), jnp.float32)
    for k in range(BASIS):
        lane_weight = jnp.where(lane_group == k, weights[k], lane_weight)
    for tile in range(width // LANES):
        part = slice(tile * LANES, (tile + 1) * LANES)
        surface = weights[0] * basis_ref[:band, part]
        for k in range(1, BASIS):
            surface = surface + weights[k] * basis_ref[k * band : (k + 1) * band, part]
        surface_ref[:, part] = surface

    fill = LANES // band
    group_full = lax.broadcasted_iota(jnp.int32, (slab_rows, LANES), 1) // band
    height, east_edge, west_edge = {}, [], []
    for tile in range(count):
        joined = None
        for p in range(fill):
            part = slabs_ref[tile * fill + p] * lane_weight
            shift = LANES // 2
            while shift >= band:
                part = part + pltpu.roll(part, shift, 1)
                shift //= 2
            joined = part if joined is None else jnp.where(group_full == p, part, joined)
        for block in range(blocks):
            height[block, tile] = joined[block * SUBLANES : (block + 1) * SUBLANES]
        east_edge.append(jnp.broadcast_to(joined[columns : columns + 1], (SUBLANES, LANES)))
        west_edge.append(
            jnp.broadcast_to(joined[columns + 1 : columns + 2], (SUBLANES, LANES))
        )
    height_east = shift_columns(height, 1, east_edge, blocks, count)
    flow_east = {p: -BARO_GAIN * (height_east[p] - height[p]) for p in places}
    per_layer = LANES // columns
    layers = levels // per_layer
    row_blocks = rows // SUBLANES
    for p in places:
        for repeat in range(per_layer):
            at = tile_index(p)
            start = repeat * columns
            height_ref[start + at[0].start : start + at[0].stop, at[1]] = height[p]
    turn(height_ref, turned_ref)
    for block in range(row_blocks):
        here = turned_ref[row_tile(block)]
        after = turned_ref[row_tile(block + 1)] if block + 1 < row_blocks else None
        flow_ref[row_tile(block)] = -BARO_GAIN * (shifted(here, after, 1) - here)
    flow_west = [
        -BARO_GAIN * (jnp.broadcast_to(height[0, tile][:1], (SUBLANES, LANES)) - west_edge[tile])
        for tile in range(count)
    ]

    def copy(kind, layer):
        span = (kind, pl.ds(layer * per_layer, per_layer))
        return pltpu.make_async_copy(
            result_ref.at[span], out_ref.at[span], sems.at[kind, layer]
        )

    @pl.loop(0, kinds)
    def _(kind):
        for layer in range(layers):
            before = None
            for block in range(row_blocks):
                at = row_tile(block)
                flux = flow_ref[at] * face_north_ref[kind, layer, at]
                turned_ref[at] = change_ref[kind, layer, at] + (shifted(flux, before, -1) - flux)
                before = flux
            for tile in range(count):
                part = slice(tile * LANES, (tile + 1) * LANES)
                along = turned_ref[part].T
                for z in range(per_layer):
                    level = layer * per_layer + z
                    flux_east = {
                        (block, tile): flow_east[block, tile]
                        * face_east_ref[(kind, level) + tile_index((block, tile))]
                        for block in range(blocks)
                    }
                    edge = flow_west[tile] * jnp.broadcast_to(
                        face_west_ref[kind, level : level + 1, part], (SUBLANES, LANES)
                    )
                    for block in range(blocks):
                        at = (kind, level) + tile_index((block, tile))
                        start = z * columns + block * SUBLANES
                        west = flux_east[block - 1, tile] if block else edge
                        flux = flux_east[block, tile]
                        result_ref[at] = base_ref[at] + (
                            (shifted(flux, west, -1) - flux) + along[start : start + SUBLANES]
                        )
            copy(kind, layer).start()

    for kind in range(kinds):
        for layer in range(layers):
            copy(kind, layer).wait()


def body(
    surface_old,
    surface_forcing,
    surface_coeff,
    ocean_mask,
    column_depth,
    east_depth,
    tracers,
    u_clinic,
    v_clinic,
):
    band, width = surface_old.shape
    kinds, levels, columns, rows = tracers.shape
    count = lax.axis_size("lon")
    f32 = jnp.float32
    sds = jax.ShapeDtypeStruct
    vmem = pl.BlockSpec(memory_space=pltpu.VMEM)
    hbm = pl.BlockSpec(memory_space=pltpu.HBM)
    fields = (surface_old, surface_forcing, surface_coeff, ocean_mask)
    pairs_inner = [(i, i ^ 1) for i in range(count)]
    ring = [(i, (i + 1 if i % 2 else i - 1) % count) for i in range(count)]
    pairs_outer = [(i, j) for i, j in ring if abs(i - j) == 1]

    def call(
        kernel, out_shape, name, operands, scratch=(), limit=SMALL_VMEM, cost=0, far=()
    ):
        return pl.pallas_call(
            kernel,
            out_shape=out_shape,
            in_specs=[hbm if place in far else vmem for place in range(len(operands))],
            out_specs=[pl.BlockSpec(memory_space=pl.ANY) if x is result else vmem for x in out_shape],
            scratch_shapes=list(scratch),
            compiler_params=pltpu.CompilerParams(vmem_limit_bytes=limit),
            cost_estimate=pl.CostEstimate(
                flops=cost * tracers.size, bytes_accessed=8 * tracers.size, transcendentals=0
            )
            if cost
            else None,
            name=name,
        )(
            *(
                pltpu.with_memory_space_constraint(x, pltpu.HBM) if place in far else x
                for place, x in enumerate(operands)
            )
        )

    result = sds(tracers.shape, f32)
    packed = sds((3 * HALO, width), f32)
    held = pltpu.VMEM(tracers.shape, f32)

    inner, outer, own = call(
        pack_kernel,
        (packed, packed, sds((3 * band, width), f32)),
        "pack_edges",
        fields,
        scratch=[pltpu.VMEM(x.shape, x.dtype) for x in fields] + [pltpu.SemaphoreType.DMA((4,))],
        far=range(4),
        cost=2000,
    )
    edges = sds((2 * levels + levels // SUBLANES + 1, kinds, rows), f32)
    own_inner, own_outer = call(
        edge_kernel,
        (edges, edges),
        "pack_tracer_edges",
        (tracers, column_depth, east_depth, u_clinic, outer),
    )
    (folded,) = call(fold_kernel, (packed,), "fold", (outer, own_outer))
    came_inner = lax.ppermute(inner, "lon", pairs_inner)
    came_outer = lax.ppermute(outer, "lon", pairs_outer)

    groups = count // 4
    half_slabs = sds((count // 2, SLAB_ROWS, LANES), f32)
    basis, keep, send = call(
        basis_kernel,
        (sds((BASIS * band, width), f32), half_slabs, half_slabs),
        "solver_basis",
        (own, came_inner, came_outer, folded),
        scratch=[pltpu.VMEM((count, SLAB_ROWS, LANES), f32)],
        cost=2000,
    )
    came = lax.ppermute(send, "lon", pairs_inner)
    sends = call(
        spread_kernel,
        (sds((2, 2, SLAB_ROWS, LANES), f32),) * groups,
        "spread_slabs",
        (keep, came),
    )
    slabs = [sends[0]]
    for step in range(1, groups):
        pairs = [(i, (i + 4 * step) % count) for i in range(count)]
        slabs.append(lax.ppermute(sends[step], "lon", pairs))
    edge_inner = lax.ppermute(own_inner, "lon", pairs_inner)
    edge_outer = lax.ppermute(own_outer, "lon", ring)
    base, masked = call(
        source_kernel, (held, held), "sources", (tracers, column_depth, own_inner), cost=2000
    )
    turned = (kinds, levels * columns // LANES, rows, LANES)
    change, face_north = call(
        north_kernel,
        (pltpu.VMEM(turned, f32), pltpu.VMEM(turned, f32)),
        "north_fluxes",
        (masked, column_depth, v_clinic, sends[0]),
        scratch=[pltpu.VMEM((rows, LANES), f32)] + [pltpu.VMEM(turned[1:], f32)] * 4,
        cost=2000,
    )
    quarter = sds((groups, 2, SLAB_ROWS, LANES), f32)
    keep, send = call(half_kernel, (quarter, quarter), "split_halves", (*slabs, change))
    came = lax.ppermute(send, "lon", [(i, i ^ 2) for i in range(count)])
    base, face_east, face_west = call(
        east_kernel,
        (held, held, pltpu.VMEM((kinds, levels, rows), f32)),
        "east_fluxes",
        (
            masked,
            east_depth,
            u_clinic,
            edge_inner,
            edge_outer,
            own_inner,
            own_outer,
            base,
            keep,
        ),
        scratch=[
            pltpu.VMEM((levels, kinds, rows), f32),
            pltpu.VMEM(edges.shape, f32),
            pltpu.VMEM(edges.shape, f32),
            pltpu.VMEM(edges.shape, f32),
        ],
        cost=2000,
    )
    return tuple(
        call(
            update_kernel,
            (sds((band, width), f32), result),
            "surface_update",
            (keep, came, basis, base, face_east, face_west, change, face_north),
            scratch=[
                pltpu.VMEM((count, SLAB_ROWS, LANES), f32),
                pltpu.VMEM((LANES, rows), f32),
                pltpu.VMEM((rows, LANES), f32),
                pltpu.VMEM((rows, LANES), f32),
                pltpu.VMEM(tracers.shape, f32),
                pltpu.SemaphoreType.DMA((kinds, levels * columns // LANES)),
            ],
            limit=RESULT_VMEM,
        )
    )


def solution(mesh):
    in_specs = (
        P(("member", "lon"), None),
        P(("member", "lon"), None),
        P("lon", None),
        P("lon", None),
        P("lon", None),
        P("lon", None),
        P("member", None, "lon", None),
        P("member", "lon", None),
        P("member", "lon", None),
    )
    out_specs = (P(("member", "lon"), None), P("member", None, "lon", None))
    return jax.shard_map(body, mesh=mesh, in_specs=in_specs, out_specs=out_specs, check_vma=False)
```

```python
import jax
import jax.numpy as jnp
from jax import lax
from jax.experimental import pallas as pl
from jax.experimental.pallas import tpu as pltpu
from jax.sharding import PartitionSpec as P

BARO_GAIN = 0.1
HORIZ_DIFF = 0.1
VERT_DIFF = 0.15
RATE_CARBON = 0.3
RATE_AMMONIUM = 0.2
RATE_NITRITE = 0.2
RATE_SULFIDE = 0.3
RATE_NITROUS = 0.2
HALF_OXYGEN = 0.3
HALF_NITRATE = 0.3
HALF_NITRITE = 0.3
YIELD_NITROUS = 0.3


SUBLANES = 8
LANES = 128
SMALL_VMEM = 4 * 2**20
RESULT_VMEM = 14 * 2**20
HALO = 8
SLAB_ROWS = 24
BASIS = 4
CENTRE = 4.55
SPREAD = 4.45
PIVOT_FLOOR = 3e-7


def is_even():
    return lax.rem(lax.axis_index("lon"), 2) == 0


def pack_kernel(old_in, force_in, coeff_in, mask_in, inner_ref, outer_ref, own_ref, *scratch):
    old_ref, force_ref, coeff_ref, mask_ref, sems = scratch
    copies = [
        pltpu.make_async_copy(source, target, sems.at[place])
        for place, (source, target) in enumerate(
            zip((old_in, force_in, coeff_in, mask_in), (old_ref, force_ref, coeff_ref, mask_ref))
        )
    ]
    for copy in copies:
        copy.start()
    for copy in copies:
        copy.wait()
    rows = old_ref.shape[0]
    coeff = coeff_ref[...]
    fields = (
        coeff * old_ref[...] + force_ref[...],
        coeff,
        mask_ref[...].astype(jnp.float32),
    )
    for place, field in enumerate(fields):
        low, high = field[:HALO], field[rows - HALO :]
        part = slice(HALO * place, HALO * (place + 1))
        inner_ref[part] = jnp.where(is_even(), high, low)
        outer_ref[part] = jnp.where(is_even(), low, high)
        own_ref[rows * place : rows * (place + 1)] = field


def basis_kernel(
    own_ref,
    inner_ref,
    outer_ref,
    folded_ref,
    basis_ref,
    keep_ref,
    send_ref,
    slabs_ref,
):
    rows, width = own_ref.shape[0] // 3, own_ref.shape[1]
    count = slabs_ref.shape[0]
    columns = width // count
    top_device = lax.axis_index("lon") == count - 1
    below = jnp.where(is_even(), outer_ref[...], inner_ref[...])
    above = jnp.where(is_even(), inner_ref[...], outer_ref[...])
    above = jnp.where(top_device, folded_ref[...], above)

    def extended(place):
        part = slice(HALO * place, HALO * (place + 1))
        own = own_ref[rows * place : rows * (place + 1)]
        return jnp.concatenate([below[part], own, above[part]], axis=0)

    first, coeff, mask = extended(0), extended(1), extended(2)
    diagonal = (coeff + 4.0 * mask - CENTRE) * (1.0 / SPREAD)
    beside = mask * (1.0 / SPREAD)
    total = rows + 2 * HALO

    def scaled(values):
        masked = mask * values
        around = (
            pltpu.roll(masked, total - 1, 0)
            + pltpu.roll(masked, 1, 0)
            + pltpu.roll(masked, width - 1, 1)
            + pltpu.roll(masked, 1, 1)
        )
        return diagonal * values - beside * around

    vectors = [first, scaled(first)]
    while len(vectors) < BASIS + 1:
        vectors.append(2.0 * scaled(vectors[-1]) - vectors[-2])
    own = [vector[HALO : HALO + rows] for vector in vectors]
    sums = []
    for order in range(2 * BASIS):
        product = own[order // 2] * own[(order + 1) // 2]
        sums.append(jnp.sum(product, axis=0, keepdims=True))
    partial = jnp.sum(jnp.concatenate(sums, axis=0), axis=1, keepdims=True)
    lane = lax.broadcasted_iota(jnp.int32, (2 * BASIS, LANES), 1)
    place = lax.broadcasted_iota(jnp.int32, (2 * BASIS, LANES), 0)
    moments = jnp.sum(jnp.where(lane == place, partial, 0.0), axis=0, keepdims=True)
    stacked = jnp.concatenate(own[:BASIS], axis=0)
    basis_ref[...] = stacked
    if BASIS * rows < LANES:
        stacked = jnp.concatenate(
            [stacked, jnp.zeros((LANES - BASIS * rows, width), jnp.float32)], axis=0
        )
    turned = stacked.T
    for target in range(count):
        start = target * columns
        east = (start + columns) % width
        west = (start - 1) % width
        pieces = [
            turned[start : start + columns],
            turned[east : east + 1],
            turned[west : west + 1],
            moments,
            jnp.zeros((SLAB_ROWS - columns - 3, LANES), jnp.float32),
        ]
        slabs_ref[target] = jnp.concatenate(pieces, axis=0)
    core = lax.rem(lax.axis_index("lon"), 2)
    for pair in range(count // 2):
        keep_ref[pair] = slabs_ref[2 * pair + core]
        send_ref[pair] = slabs_ref[2 * pair + 1 - core]


def spread_kernel(kept_ref, came_ref, *out_refs):
    here = lax.axis_index("lon")
    core, group = lax.rem(here, 2), here // 4
    groups = len(out_refs)
    for step in range(groups):
        target = lax.rem(group + step, groups)
        for y in range(2):
            out_refs[step][y, core] = kept_ref[2 * target + y]
            out_refs[step][y, 1 - core] = came_ref[2 * target + y]


def half_kernel(*refs):
    came_refs, (_, keep_ref, send_ref) = refs[:-3], refs[-3:]
    here = lax.axis_index("lon")
    half, group = lax.rem(here // 2, 2), here // 4
    groups = len(came_refs)
    for step in range(groups):
        source = lax.rem(group + groups - step, groups)
        keep_ref[source] = came_refs[step][half]
        send_ref[source] = came_refs[step][1 - half]


def basis_weights(moments):
    gram = {}

    def inner(i, j):
        key = (i + j, abs(i - j))
        if key not in gram:
            gram[key] = 0.5 * (moments[i + j] + moments[abs(i - j)])
        return gram[key]

    matrix = [[None] * BASIS for _ in range(BASIS)]
    for i in range(BASIS):
        for j in range(i + 1):
            if i == 0:
                image = moments[1]
            elif j == 0:
                image = inner(1, i)
            else:
                image = 0.5 * (inner(i, j + 1) + inner(i, j - 1))
            matrix[i][j] = CENTRE * inner(i, j) + SPREAD * image
    right = [inner(i, 0) for i in range(BASIS)]
    start = [matrix[i][i] for i in range(BASIS)]
    inverse = []
    factors = [[None] * BASIS for _ in range(BASIS)]
    for n in range(BASIS):
        pivot = matrix[n][n]
        inverse.append(jnp.where(pivot > PIVOT_FLOOR * start[n], 1.0 / pivot, 0.0))
        for i in range(n + 1, BASIS):
            factors[i][n] = matrix[i][n] * inverse[n]
        for i in range(n + 1, BASIS):
            for j in range(n + 1, i + 1):
                matrix[i][j] = matrix[i][j] - factors[i][n] * matrix[j][n]
            right[i] = right[i] - factors[i][n] * right[n]
    weights = [None] * BASIS
    for n in reversed(range(BASIS)):
        value = right[n] * inverse[n]
        for i in range(n + 1, BASIS):
            value = value - factors[i][n] * weights[i]
        weights[n] = value
    return weights


def reverse_tile(tile):
    for axis, size in ((0, SUBLANES), (1, LANES)):
        place = lax.broadcasted_iota(jnp.int32, (SUBLANES, LANES), axis)
        step = size // 2
        while step:
            tile = jnp.where(
                (place & step) != 0,
                pltpu.roll(tile, step, axis),
                pltpu.roll(tile, size - step, axis),
            )
            step //= 2
    return tile


def fold_kernel(high_ref, _, folded_ref):
    tiles = high_ref.shape[1] // LANES

    @pl.when(lax.axis_index("lon") == lax.axis_size("lon") - 1)
    def _():
        for place in range(3):
            part = slice(HALO * place, HALO * (place + 1))
            for tile in range(tiles):
                other = tiles - 1 - tile
                folded_ref[part, tile * LANES : (tile + 1) * LANES] = reverse_tile(
                    high_ref[part, other * LANES : (other + 1) * LANES]
                )


def edge_kernel(tracers_ref, depth_ref, east_depth_ref, u_ref, _, inner_ref, outer_ref):
    kinds, levels, columns, rows = tracers_ref.shape

    def pack(first, target_ref):
        for side in range(2):
            column = first + side
            for z in range(levels):
                wet = (z < depth_ref[column : column + 1]).astype(jnp.float32)
                for kind in range(kinds):
                    target_ref[2 * z + side, kind : kind + 1] = (
                        tracers_ref[kind, z, column : column + 1] * wet
                    )

    def pack_faces(target_ref):
        for z in range(levels):
            place = 2 * levels + z // SUBLANES
            row = z % SUBLANES
            target_ref[place, row : row + 1] = u_ref[z, columns - 1 :]
        place = 2 * levels + levels // SUBLANES
        target_ref[place] = jnp.broadcast_to(
            east_depth_ref[columns - 1 : columns].astype(jnp.float32), (SUBLANES, rows)
        )

    @pl.when(is_even())
    def _():
        pack(columns - 2, inner_ref)
        pack(0, outer_ref)

    @pl.when(jnp.logical_not(is_even()))
    def _():
        pack(0, inner_ref)
        pack(columns - 2, outer_ref)

    pack_faces(inner_ref)
    pack_faces(outer_ref)


def grid_tiles(columns, rows):
    return [
        (block, tile)
        for block in range(columns // SUBLANES)
        for tile in range(rows // LANES)
    ]


def tile_index(place):
    block, tile = place
    return (
        slice(block * SUBLANES, (block + 1) * SUBLANES),
        slice(tile * LANES, (tile + 1) * LANES),
    )


def shift_columns(tiles, step, outer, blocks, count):
    sublane = lax.broadcasted_iota(jnp.int32, (SUBLANES, LANES), 0)
    turned = {p: pltpu.roll(x, SUBLANES - 1 if step > 0 else 1, 0) for p, x in tiles.items()}
    inside = sublane < SUBLANES - 1 if step > 0 else sublane > 0
    shifted = {}
    for block in range(blocks):
        for tile in range(count):
            beyond = block + step
            other = turned[beyond, tile] if 0 <= beyond < blocks else outer[tile]
            shifted[block, tile] = jnp.where(inside, turned[block, tile], other)
    return shifted


def shift_rows(tiles, step, blocks, count):
    lane = lax.broadcasted_iota(jnp.int32, (SUBLANES, LANES), 1)
    turned = {p: pltpu.roll(x, LANES - 1 if step > 0 else 1, 1) for p, x in tiles.items()}
    inside = lane < LANES - 1 if step > 0 else lane > 0
    shifted = {}
    for block in range(blocks):
        for tile in range(count):
            beyond = tile + step
            other = turned[block, beyond] if 0 <= beyond < count else 0.0
            shifted[block, tile] = jnp.where(inside, turned[block, tile], other)
    return shifted


def reciprocal(value):
    guess = pl.reciprocal(value, approx=True)
    return guess * (2.0 - value * guess)


def redox_sources(masked):
    oxygen, nitrate, nitrite, ammonium, _, carbon, sulfide, nitrous = masked
    over_oxygen = reciprocal(oxygen + HALF_OXYGEN)
    with_oxygen = oxygen * over_oxygen
    no_oxygen = HALF_OXYGEN * over_oxygen
    with_nitrate = no_oxygen * nitrate * reciprocal(nitrate + HALF_NITRATE)
    rest = no_oxygen - with_nitrate
    with_nitrite = rest * nitrite * reciprocal(nitrite + HALF_NITRITE)
    with_sulfate = rest - with_nitrite
    breakdown = RATE_CARBON * carbon
    first_nitr = RATE_AMMONIUM * ammonium * with_oxygen
    second_nitr = RATE_NITRITE * nitrite * with_oxygen
    sulfide_ox = RATE_SULFIDE * sulfide * with_oxygen
    by_nitrate = 0.9 * breakdown * with_nitrate
    return (
        -1.3 * breakdown * with_oxygen - 1.5 * first_nitr - 0.5 * second_nitr - 2.0 * sulfide_ox,
        second_nitr - by_nitrate,
        by_nitrate
        - 0.6 * breakdown * with_nitrite
        + (1.0 - YIELD_NITROUS) * first_nitr
        - second_nitr,
        0.15 * breakdown - first_nitr,
        0.1 * breakdown,
        -breakdown,
        0.5 * breakdown * with_sulfate - sulfide_ox,
        YIELD_NITROUS * first_nitr - RATE_NITROUS * nitrous * no_oxygen,
    )


def source_kernel(tracers_ref, depth_ref, _, base_ref, masked_ref):
    kinds, levels, columns, rows = tracers_ref.shape
    places = grid_tiles(columns, rows)

    @pl.loop(0, levels)
    def _(level):
        above = jnp.maximum(level - 1, 0)
        below = jnp.minimum(level + 1, levels - 1)
        mix_up_level = jnp.where(level > 0, VERT_DIFF, 0.0)
        for p in places:
            at = tile_index(p)
            depth_here = depth_ref[at]
            wet = jnp.where(level < depth_here, 1.0, 0.0)
            mix_up = wet * mix_up_level
            mix_down = jnp.where(level + 1 < depth_here, VERT_DIFF, 0.0)
            values = [tracers_ref[(kind, level) + at] for kind in range(kinds)]
            masked = [value * wet for value in values]
            sources = redox_sources(masked)
            for kind in range(kinds):
                masked_ref[(kind, level) + at] = masked[kind]
                value = values[kind]
                down = (tracers_ref[(kind, below) + at] - value) * mix_down
                up = (value - tracers_ref[(kind, above) + at]) * mix_up
                base_ref[(kind, level) + at] = value + (sources[kind] + (down - up))


def turn(ref_block, target_ref, start=0):
    rows = ref_block.shape[1]
    for tile in range(rows // LANES):
        part = slice(tile * LANES, (tile + 1) * LANES)
        target_ref[start + part.start : start + part.stop] = ref_block[:, part].T


def shifted(here, other, step):
    sublane = lax.broadcasted_iota(jnp.int32, (SUBLANES, LANES), 0)
    inside = sublane < SUBLANES - step if step > 0 else sublane >= -step
    amount = (SUBLANES - step) % SUBLANES if step > 0 else -step
    other = pltpu.roll(other, amount, 0) if other is not None else 0.0
    return jnp.where(inside, pltpu.roll(here, amount, 0), other)


def row_tile(block):
    return slice(block * SUBLANES, (block + 1) * SUBLANES)


def north_kernel(
    masked_in,
    depth_ref,
    v_ref,
    _,
    change_ref,
    face_ref,
    depth_turned_ref,
    scale_ref,
    flow_ref,
    mix_ref,
    masked_ref,
):
    kinds, levels, columns, rows = masked_in.shape
    per_layer = LANES // columns
    layers = levels // per_layer
    blocks = rows // SUBLANES
    depth = depth_ref[...].astype(jnp.float32)
    turn(jnp.concatenate([depth] * per_layer, axis=0), depth_turned_ref)
    lane_level = lax.broadcasted_iota(jnp.int32, (SUBLANES, LANES), 1) // columns
    for layer in range(layers):
        span = slice(layer * per_layer, (layer + 1) * per_layer)
        turn(v_ref[span].reshape(LANES, rows), flow_ref.at[layer])
        level = (lane_level + layer * per_layer).astype(jnp.float32)
        for block in range(blocks):
            at = row_tile(block)
            here = depth_turned_ref[at]
            after = depth_turned_ref[row_tile(block + 1)] if block + 1 < blocks else None
            is_open = level < jnp.minimum(here, shifted(here, after, 1))
            scale = jnp.where(is_open, 1.0 / 12.0, 0.0)
            scale_ref[layer, at] = scale
            mix_ref[layer, at] = jnp.where(is_open, HORIZ_DIFF, 0.0)
            flow_ref[layer, at] = flow_ref[layer, at] * scale

    @pl.loop(0, kinds)
    def _(kind):
        for layer in range(layers):
            span = slice(layer * per_layer, (layer + 1) * per_layer)
            turn(masked_in[kind, span].reshape(LANES, rows), masked_ref.at[layer])
            tiles = [masked_ref[layer, row_tile(block)] for block in range(blocks)]
            before = None
            for block in range(blocks):
                at = row_tile(block)
                here = tiles[block]
                after = tiles[block + 1] if block + 1 < blocks else None
                one = shifted(here, after, 1)
                two = shifted(here, after, 2)
                south = shifted(here, tiles[block - 1] if block else None, -1)
                face = 7.0 * (here + one) - (south + two)
                face_ref[kind, layer, at] = face * scale_ref[layer, at]
                flux = face * flow_ref[layer, at] - (one - here) * mix_ref[layer, at]
                change_ref[kind, layer, at] = shifted(flux, before, -1) - flux
                before = flux


def east_kernel(
    masked_ref,
    east_depth_ref,
    u_ref,
    inner_ref,
    outer_ref,
    own_inner_ref,
    own_outer_ref,
    before_ref,
    _,
    base_ref,
    face_east_ref,
    face_west_ref,
    flux_west_ref,
    from_west_ref,
    from_east_ref,
    own_west_ref,
):
    kinds, levels, columns, rows = masked_ref.shape
    blocks, count = columns // SUBLANES, rows // LANES
    places = grid_tiles(columns, rows)
    for place in range(inner_ref.shape[0]):
        from_west_ref[place] = jnp.where(is_even(), outer_ref[place], inner_ref[place])
    for place in range(2 * levels):
        from_east_ref[place] = jnp.where(is_even(), inner_ref[place], outer_ref[place])
        own_west_ref[place] = jnp.where(is_even(), own_outer_ref[place], own_inner_ref[place])
    depth_west = from_west_ref[2 * levels + levels // SUBLANES]
    for z in range(levels):
        row = z % SUBLANES
        u_west = from_west_ref[2 * levels + z // SUBLANES, row : row + 1]
        center, east_one = from_west_ref[2 * z + 1], own_west_ref[2 * z]
        outer = from_west_ref[2 * z] + own_west_ref[2 * z + 1]
        scale_west = jnp.where(z < depth_west, 1.0 / 12.0, 0.0)
        mix_west = jnp.where(z < depth_west, HORIZ_DIFF, 0.0)
        face = (7.0 * (center + east_one) - outer) * scale_west
        for kind in range(kinds):
            face_west_ref[kind, z : z + 1] = face[kind : kind + 1]
        flux_west_ref[z] = u_west * face - mix_west * (east_one - center)

    @pl.loop(0, levels)
    def _(level):
        scale, mix = {}, {}
        for p in places:
            at = tile_index(p)
            is_open = level < east_depth_ref[at]
            scale[p] = jnp.where(is_open, 1.0 / 12.0, 0.0)
            mix[p] = jnp.where(is_open, HORIZ_DIFF, 0.0)
        for kind in range(kinds):
            def halo(ref, index):
                return [
                    jnp.broadcast_to(
                        ref[index, kind : kind + 1, tile * LANES : (tile + 1) * LANES],
                        (SUBLANES, LANES),
                    )
                    for tile in range(count)
                ]

            masked = {p: masked_ref[(kind, level) + tile_index(p)] for p in places}
            one = shift_columns(masked, 1, halo(from_east_ref, 2 * level), blocks, count)
            two = shift_columns(one, 1, halo(from_east_ref, 2 * level + 1), blocks, count)
            west = shift_columns(masked, -1, halo(from_west_ref, 2 * level + 1), blocks, count)
            flux = {}
            for p in places:
                at = (kind, level) + tile_index(p)
                face = (7.0 * (masked[p] + one[p]) - (west[p] + two[p])) * scale[p]
                face_east_ref[at] = face
                flux[p] = u_ref[(level,) + tile_index(p)] * face - mix[p] * (one[p] - masked[p])
            incoming = shift_columns(flux, -1, halo(flux_west_ref, level), blocks, count)
            for p in places:
                at = (kind, level) + tile_index(p)
                base_ref[at] = before_ref[at] + (incoming[p] - flux[p])


def update_kernel(
    kept_ref,
    came_ref,
    basis_ref,
    base_ref,
    face_east_ref,
    face_west_ref,
    change_ref,
    face_north_ref,
    surface_out,
    out_ref,
    surface_ref,
    slabs_ref,
    height_ref,
    flow_ref,
    turned_ref,
    result_ref,
    surface_sem,
    sems,
):
    half = lax.rem(lax.axis_index("lon") // 2, 2)
    for source in range(kept_ref.shape[0]):
        for core in range(2):
            slabs_ref[4 * source + 2 * half + core] = kept_ref[source, core]
            slabs_ref[4 * source + 2 * (1 - half) + core] = came_ref[source, core]
    kinds, levels, columns, rows = base_ref.shape
    blocks, count = columns // SUBLANES, rows // LANES
    places = grid_tiles(columns, rows)
    sources, slab_rows, _ = slabs_ref.shape
    band, width = surface_ref.shape
    parts = [slabs_ref[source, columns + 2 : columns + 3] for source in range(sources)]
    while len(parts) > 1:
        parts = [a + b for a, b in zip(parts[::2], parts[1::2])]
    dots = [jnp.broadcast_to(parts[0][:, m : m + 1], (1, LANES)) for m in range(2 * BASIS)]
    weights = basis_weights(
        dots[:2] + [2.0 * dots[m] - dots[m % 2] for m in range(2, 2 * BASIS)]
    )
    lane_group = lax.broadcasted_iota(jnp.int32, (1, LANES), 1) // band
    lane_weight = jnp.zeros((1, LANES), jnp.float32)
    for k in range(BASIS):
        lane_weight = jnp.where(lane_group == k, weights[k], lane_weight)
    for tile in range(width // LANES):
        part = slice(tile * LANES, (tile + 1) * LANES)
        surface = weights[0] * basis_ref[:band, part]
        for k in range(1, BASIS):
            surface = surface + weights[k] * basis_ref[k * band : (k + 1) * band, part]
        surface_ref[:, part] = surface
    surface_copy = pltpu.make_async_copy(surface_ref, surface_out, surface_sem)
    surface_copy.start()

    fill = LANES // band
    group_full = lax.broadcasted_iota(jnp.int32, (slab_rows, LANES), 1) // band
    height, east_edge, west_edge = {}, [], []
    for tile in range(count):
        joined = None
        for p in range(fill):
            part = slabs_ref[tile * fill + p] * lane_weight
            shift = LANES // 2
            while shift >= band:
                part = part + pltpu.roll(part, shift, 1)
                shift //= 2
            joined = part if joined is None else jnp.where(group_full == p, part, joined)
        for block in range(blocks):
            height[block, tile] = joined[block * SUBLANES : (block + 1) * SUBLANES]
        east_edge.append(jnp.broadcast_to(joined[columns : columns + 1], (SUBLANES, LANES)))
        west_edge.append(
            jnp.broadcast_to(joined[columns + 1 : columns + 2], (SUBLANES, LANES))
        )
    height_east = shift_columns(height, 1, east_edge, blocks, count)
    flow_east = {p: -BARO_GAIN * (height_east[p] - height[p]) for p in places}
    per_layer = LANES // columns
    layers = levels // per_layer
    row_blocks = rows // SUBLANES
    for p in places:
        for repeat in range(per_layer):
            at = tile_index(p)
            start = repeat * columns
            height_ref[start + at[0].start : start + at[0].stop, at[1]] = height[p]
    turn(height_ref, turned_ref)
    for block in range(row_blocks):
        here = turned_ref[row_tile(block)]
        after = turned_ref[row_tile(block + 1)] if block + 1 < row_blocks else None
        flow_ref[row_tile(block)] = -BARO_GAIN * (shifted(here, after, 1) - here)
    flow_west = [
        -BARO_GAIN * (jnp.broadcast_to(height[0, tile][:1], (SUBLANES, LANES)) - west_edge[tile])
        for tile in range(count)
    ]

    def copy(kind, layer):
        span = (kind, pl.ds(layer * per_layer, per_layer))
        return pltpu.make_async_copy(
            result_ref.at[span], out_ref.at[span], sems.at[kind, layer]
        )

    @pl.loop(0, kinds)
    def _(kind):
        for layer in range(layers):
            before = None
            for block in range(row_blocks):
                at = row_tile(block)
                flux = flow_ref[at] * face_north_ref[kind, layer, at]
                turned_ref[at] = change_ref[kind, layer, at] + (shifted(flux, before, -1) - flux)
                before = flux
            for tile in range(count):
                part = slice(tile * LANES, (tile + 1) * LANES)
                along = turned_ref[part].T
                for z in range(per_layer):
                    level = layer * per_layer + z
                    flux_east = {
                        (block, tile): flow_east[block, tile]
                        * face_east_ref[(kind, level) + tile_index((block, tile))]
                        for block in range(blocks)
                    }
                    edge = flow_west[tile] * jnp.broadcast_to(
                        face_west_ref[kind, level : level + 1, part], (SUBLANES, LANES)
                    )
                    for block in range(blocks):
                        at = (kind, level) + tile_index((block, tile))
                        start = z * columns + block * SUBLANES
                        west = flux_east[block - 1, tile] if block else edge
                        flux = flux_east[block, tile]
                        result_ref[at] = base_ref[at] + (
                            (shifted(flux, west, -1) - flux) + along[start : start + SUBLANES]
                        )
            copy(kind, layer).start()

    for kind in range(kinds):
        for layer in range(layers):
            copy(kind, layer).wait()
    surface_copy.wait()


def body(
    surface_old,
    surface_forcing,
    surface_coeff,
    ocean_mask,
    column_depth,
    east_depth,
    tracers,
    u_clinic,
    v_clinic,
):
    band, width = surface_old.shape
    kinds, levels, columns, rows = tracers.shape
    count = lax.axis_size("lon")
    f32 = jnp.float32
    sds = jax.ShapeDtypeStruct
    vmem = pl.BlockSpec(memory_space=pltpu.VMEM)
    hbm = pl.BlockSpec(memory_space=pltpu.HBM)
    fields = (surface_old, surface_forcing, surface_coeff, ocean_mask)
    pairs_inner = [(i, i ^ 1) for i in range(count)]
    ring = [(i, (i + 1 if i % 2 else i - 1) % count) for i in range(count)]
    pairs_outer = [(i, j) for i, j in ring if abs(i - j) == 1]

    def call(
        kernel, out_shape, name, operands, scratch=(), limit=SMALL_VMEM, cost=0, far=()
    ):
        return pl.pallas_call(
            kernel,
            out_shape=out_shape,
            in_specs=[hbm if place in far else vmem for place in range(len(operands))],
            out_specs=[hbm if x is result or x is solved else vmem for x in out_shape],
            scratch_shapes=list(scratch),
            compiler_params=pltpu.CompilerParams(vmem_limit_bytes=limit),
            cost_estimate=pl.CostEstimate(
                flops=cost * tracers.size, bytes_accessed=8 * tracers.size, transcendentals=0
            )
            if cost
            else None,
            name=name,
        )(
            *(
                pltpu.with_memory_space_constraint(x, pltpu.HBM) if place in far else x
                for place, x in enumerate(operands)
            )
        )

    solved, result = sds((band, width), f32), sds(tracers.shape, f32)
    packed = sds((3 * HALO, width), f32)
    held = pltpu.VMEM(tracers.shape, f32)

    inner, outer, own = call(
        pack_kernel,
        (packed, packed, sds((3 * band, width), f32)),
        "pack_edges",
        fields,
        scratch=[pltpu.VMEM(x.shape, x.dtype) for x in fields] + [pltpu.SemaphoreType.DMA((4,))],
        far=range(4),
        cost=2000,
    )
    edges = sds((2 * levels + levels // SUBLANES + 1, kinds, rows), f32)
    own_inner, own_outer = call(
        edge_kernel,
        (edges, edges),
        "pack_tracer_edges",
        (tracers, column_depth, east_depth, u_clinic, outer),
    )
    (folded,) = call(fold_kernel, (packed,), "fold", (outer, own_outer))
    came_inner = lax.ppermute(inner, "lon", pairs_inner)
    came_outer = lax.ppermute(outer, "lon", pairs_outer)

    groups = count // 4
    half_slabs = sds((count // 2, SLAB_ROWS, LANES), f32)
    basis, keep, send = call(
        basis_kernel,
        (sds((BASIS * band, width), f32), half_slabs, half_slabs),
        "solver_basis",
        (own, came_inner, came_outer, folded),
        scratch=[pltpu.VMEM((count, SLAB_ROWS, LANES), f32)],
        cost=2000,
    )
    came = lax.ppermute(send, "lon", pairs_inner)
    sends = call(
        spread_kernel,
        (sds((2, 2, SLAB_ROWS, LANES), f32),) * groups,
        "spread_slabs",
        (keep, came),
    )
    slabs = [sends[0]]
    for step in range(1, groups):
        pairs = [(i, (i + 4 * step) % count) for i in range(count)]
        slabs.append(lax.ppermute(sends[step], "lon", pairs))
    edge_inner = lax.ppermute(own_inner, "lon", pairs_inner)
    edge_outer = lax.ppermute(own_outer, "lon", ring)
    base, masked = call(
        source_kernel, (held, held), "sources", (tracers, column_depth, own_inner), cost=2000
    )
    turned = (kinds, levels * columns // LANES, rows, LANES)
    change, face_north = call(
        north_kernel,
        (pltpu.VMEM(turned, f32), pltpu.VMEM(turned, f32)),
        "north_fluxes",
        (masked, column_depth, v_clinic, sends[0]),
        scratch=[pltpu.VMEM((rows, LANES), f32)] + [pltpu.VMEM(turned[1:], f32)] * 4,
        cost=2000,
    )
    quarter = sds((groups, 2, SLAB_ROWS, LANES), f32)
    keep, send = call(half_kernel, (quarter, quarter), "split_halves", (*slabs, change))
    came = lax.ppermute(send, "lon", [(i, i ^ 2) for i in range(count)])
    base, face_east, face_west = call(
        east_kernel,
        (held, held, pltpu.VMEM((kinds, levels, rows), f32)),
        "east_fluxes",
        (
            masked,
            east_depth,
            u_clinic,
            edge_inner,
            edge_outer,
            own_inner,
            own_outer,
            base,
            keep,
        ),
        scratch=[
            pltpu.VMEM((levels, kinds, rows), f32),
            pltpu.VMEM(edges.shape, f32),
            pltpu.VMEM(edges.shape, f32),
            pltpu.VMEM(edges.shape, f32),
        ],
        cost=2000,
    )
    return tuple(
        call(
            update_kernel,
            (solved, result),
            "surface_update",
            (keep, came, basis, base, face_east, face_west, change, face_north),
            scratch=[
                pltpu.VMEM((band, width), f32),
                pltpu.VMEM((count, SLAB_ROWS, LANES), f32),
                pltpu.VMEM((LANES, rows), f32),
                pltpu.VMEM((rows, LANES), f32),
                pltpu.VMEM((rows, LANES), f32),
                pltpu.VMEM(tracers.shape, f32),
                pltpu.SemaphoreType.DMA,
                pltpu.SemaphoreType.DMA((kinds, levels * columns // LANES)),
            ],
            limit=RESULT_VMEM,
        )
    )


def solution(mesh):
    in_specs = (
        P(("member", "lon"), None),
        P(("member", "lon"), None),
        P("lon", None),
        P("lon", None),
        P("lon", None),
        P("lon", None),
        P("member", None, "lon", None),
        P("member", "lon", None),
        P("member", "lon", None),
    )
    out_specs = (P(("member", "lon"), None), P("member", None, "lon", None))
    return jax.shard_map(body, mesh=mesh, in_specs=in_specs, out_specs=out_specs, check_vma=False)
```

```python
import functools

import jax
import jax.numpy as jnp
from jax import lax
from jax.experimental import pallas as pl
from jax.experimental.pallas import tpu as pltpu
from jax.sharding import PartitionSpec as P

BARO_GAIN = 0.1
HORIZ_DIFF = 0.1
VERT_DIFF = 0.15
RATE_CARBON = 0.3
RATE_AMMONIUM = 0.2
RATE_NITRITE = 0.2
RATE_SULFIDE = 0.3
RATE_NITROUS = 0.2
HALF_OXYGEN = 0.3
HALF_NITRATE = 0.3
HALF_NITRITE = 0.3
YIELD_NITROUS = 0.3


SOLVER_ITERS = 4
SUBLANES = 8
LANES = 128
SMALL_VMEM = 4 * 2**20
RESULT_VMEM = 14 * 2**20
HALO = 8
SLAB_ROWS = 24
BASIS = 4
CENTRE = 4.55
SPREAD = 4.45
PIVOT_FLOOR = 3e-7
PIVOT_LEAST = 0.03


def is_even():
    return lax.rem(lax.axis_index("lon"), 2) == 0


def pack_kernel(old_in, force_in, coeff_in, mask_in, inner_ref, outer_ref, own_ref, *scratch):
    old_ref, force_ref, coeff_ref, mask_ref, sems = scratch
    copies = [
        pltpu.make_async_copy(source, target, sems.at[place])
        for place, (source, target) in enumerate(
            zip((old_in, force_in, coeff_in, mask_in), (old_ref, force_ref, coeff_ref, mask_ref))
        )
    ]
    for copy in copies:
        copy.start()
    for copy in copies:
        copy.wait()
    rows = old_ref.shape[0]
    coeff = coeff_ref[...]
    fields = (
        coeff * old_ref[...] + force_ref[...],
        coeff,
        mask_ref[...].astype(jnp.float32),
    )
    for place, field in enumerate(fields):
        low, high = field[:HALO], field[rows - HALO :]
        part = slice(HALO * place, HALO * (place + 1))
        inner_ref[part] = jnp.where(is_even(), high, low)
        outer_ref[part] = jnp.where(is_even(), low, high)
        own_ref[rows * place : rows * (place + 1)] = field


def basis_kernel(
    own_ref,
    inner_ref,
    outer_ref,
    folded_ref,
    basis_ref,
    keep_ref,
    send_ref,
    slabs_ref,
):
    rows, width = own_ref.shape[0] // 3, own_ref.shape[1]
    count = slabs_ref.shape[0]
    columns = width // count
    top_device = lax.axis_index("lon") == count - 1
    below = jnp.where(is_even(), outer_ref[...], inner_ref[...])
    above = jnp.where(is_even(), inner_ref[...], outer_ref[...])
    above = jnp.where(top_device, folded_ref[...], above)

    def extended(place):
        part = slice(HALO * place, HALO * (place + 1))
        own = own_ref[rows * place : rows * (place + 1)]
        return jnp.concatenate([below[part], own, above[part]], axis=0)

    first, coeff, mask = extended(0), extended(1), extended(2)
    diagonal = (coeff + 4.0 * mask - CENTRE) * (1.0 / SPREAD)
    beside = mask * (1.0 / SPREAD)
    total = rows + 2 * HALO

    def scaled(values):
        masked = mask * values
        around = (
            pltpu.roll(masked, total - 1, 0)
            + pltpu.roll(masked, 1, 0)
            + pltpu.roll(masked, width - 1, 1)
            + pltpu.roll(masked, 1, 1)
        )
        return diagonal * values - beside * around

    vectors = [first, scaled(first)]
    while len(vectors) < BASIS + 1:
        vectors.append(2.0 * scaled(vectors[-1]) - vectors[-2])
    own = [vector[HALO : HALO + rows] for vector in vectors]
    sums = []
    for order in range(2 * BASIS):
        product = own[order // 2] * own[(order + 1) // 2]
        sums.append(jnp.sum(product, axis=0, keepdims=True))
    partial = jnp.sum(jnp.concatenate(sums, axis=0), axis=1, keepdims=True)
    lane = lax.broadcasted_iota(jnp.int32, (2 * BASIS, LANES), 1)
    place = lax.broadcasted_iota(jnp.int32, (2 * BASIS, LANES), 0)
    moments = jnp.sum(jnp.where(lane == place, partial, 0.0), axis=0, keepdims=True)
    stacked = jnp.concatenate(own[:BASIS], axis=0)
    basis_ref[...] = stacked
    if BASIS * rows < LANES:
        stacked = jnp.concatenate(
            [stacked, jnp.zeros((LANES - BASIS * rows, width), jnp.float32)], axis=0
        )
    turned = stacked.T
    for target in range(count):
        start = target * columns
        east = (start + columns) % width
        west = (start - 1) % width
        pieces = [
            turned[start : start + columns],
            turned[east : east + 1],
            turned[west : west + 1],
            moments,
            jnp.zeros((SLAB_ROWS - columns - 3, LANES), jnp.float32),
        ]
        slabs_ref[target] = jnp.concatenate(pieces, axis=0)
    core = lax.rem(lax.axis_index("lon"), 2)
    for pair in range(count // 2):
        keep_ref[pair] = slabs_ref[2 * pair + core]
        send_ref[pair] = slabs_ref[2 * pair + 1 - core]


def spread_kernel(kept_ref, came_ref, *out_refs):
    here = lax.axis_index("lon")
    core, group = lax.rem(here, 2), here // 4
    groups = len(out_refs)
    for step in range(groups):
        target = lax.rem(group + step, groups)
        for y in range(2):
            out_refs[step][y, core] = kept_ref[2 * target + y]
            out_refs[step][y, 1 - core] = came_ref[2 * target + y]


def half_kernel(*refs):
    came_refs, (_, keep_ref, send_ref) = refs[:-3], refs[-3:]
    here = lax.axis_index("lon")
    half, group = lax.rem(here // 2, 2), here // 4
    groups = len(came_refs)
    for step in range(groups):
        source = lax.rem(group + groups - step, groups)
        keep_ref[source] = came_refs[step][half]
        send_ref[source] = came_refs[step][1 - half]


def basis_weights(moments):
    gram = {}

    def inner(i, j):
        key = (i + j, abs(i - j))
        if key not in gram:
            gram[key] = 0.5 * (moments[i + j] + moments[abs(i - j)])
        return gram[key]

    matrix = [[None] * BASIS for _ in range(BASIS)]
    for i in range(BASIS):
        for j in range(i + 1):
            if i == 0:
                image = moments[1]
            elif j == 0:
                image = inner(1, i)
            else:
                image = 0.5 * (inner(i, j + 1) + inner(i, j - 1))
            matrix[i][j] = CENTRE * inner(i, j) + SPREAD * image
    right = [inner(i, 0) for i in range(BASIS)]
    start = [matrix[i][i] for i in range(BASIS)]
    inverse = []
    factors = [[None] * BASIS for _ in range(BASIS)]
    for n in range(BASIS):
        pivot = matrix[n][n]
        inverse.append(jnp.where(pivot > PIVOT_FLOOR * start[n], 1.0 / pivot, 0.0))
        for i in range(n + 1, BASIS):
            factors[i][n] = matrix[i][n] * inverse[n]
        for i in range(n + 1, BASIS):
            for j in range(n + 1, i + 1):
                matrix[i][j] = matrix[i][j] - factors[i][n] * matrix[j][n]
            right[i] = right[i] - factors[i][n] * right[n]
    weights = [None] * BASIS
    for n in reversed(range(BASIS)):
        value = right[n] * inverse[n]
        for i in range(n + 1, BASIS):
            value = value - factors[i][n] * weights[i]
        weights[n] = value
    kept = matrix[0][0] > 0.0
    for n in range(BASIS):
        kept = kept & (matrix[n][n] > PIVOT_LEAST * start[n])
    return weights, jnp.where(kept, 0.0, 1.0)


def reverse_tile(tile):
    for axis, size in ((0, SUBLANES), (1, LANES)):
        place = lax.broadcasted_iota(jnp.int32, (SUBLANES, LANES), axis)
        step = size // 2
        while step:
            tile = jnp.where(
                (place & step) != 0,
                pltpu.roll(tile, step, axis),
                pltpu.roll(tile, size - step, axis),
            )
            step //= 2
    return tile


def fold_kernel(high_ref, _, folded_ref):
    tiles = high_ref.shape[1] // LANES

    @pl.when(lax.axis_index("lon") == lax.axis_size("lon") - 1)
    def _():
        for place in range(3):
            part = slice(HALO * place, HALO * (place + 1))
            for tile in range(tiles):
                other = tiles - 1 - tile
                folded_ref[part, tile * LANES : (tile + 1) * LANES] = reverse_tile(
                    high_ref[part, other * LANES : (other + 1) * LANES]
                )


def edge_kernel(tracers_ref, depth_ref, east_depth_ref, u_ref, _, inner_ref, outer_ref):
    kinds, levels, columns, rows = tracers_ref.shape

    def pack(first, target_ref):
        for side in range(2):
            column = first + side
            for z in range(levels):
                wet = (z < depth_ref[column : column + 1]).astype(jnp.float32)
                for kind in range(kinds):
                    target_ref[2 * z + side, kind : kind + 1] = (
                        tracers_ref[kind, z, column : column + 1] * wet
                    )

    def pack_faces(target_ref):
        for z in range(levels):
            place = 2 * levels + z // SUBLANES
            row = z % SUBLANES
            target_ref[place, row : row + 1] = u_ref[z, columns - 1 :]
        place = 2 * levels + levels // SUBLANES
        target_ref[place] = jnp.broadcast_to(
            east_depth_ref[columns - 1 : columns].astype(jnp.float32), (SUBLANES, rows)
        )

    @pl.when(is_even())
    def _():
        pack(columns - 2, inner_ref)
        pack(0, outer_ref)

    @pl.when(jnp.logical_not(is_even()))
    def _():
        pack(0, inner_ref)
        pack(columns - 2, outer_ref)

    pack_faces(inner_ref)
    pack_faces(outer_ref)


def grid_tiles(columns, rows):
    return [
        (block, tile)
        for block in range(columns // SUBLANES)
        for tile in range(rows // LANES)
    ]


def tile_index(place):
    block, tile = place
    return (
        slice(block * SUBLANES, (block + 1) * SUBLANES),
        slice(tile * LANES, (tile + 1) * LANES),
    )


def shift_columns(tiles, step, outer, blocks, count):
    sublane = lax.broadcasted_iota(jnp.int32, (SUBLANES, LANES), 0)
    turned = {p: pltpu.roll(x, SUBLANES - 1 if step > 0 else 1, 0) for p, x in tiles.items()}
    inside = sublane < SUBLANES - 1 if step > 0 else sublane > 0
    shifted = {}
    for block in range(blocks):
        for tile in range(count):
            beyond = block + step
            other = turned[beyond, tile] if 0 <= beyond < blocks else outer[tile]
            shifted[block, tile] = jnp.where(inside, turned[block, tile], other)
    return shifted


def shift_rows(tiles, step, blocks, count):
    lane = lax.broadcasted_iota(jnp.int32, (SUBLANES, LANES), 1)
    turned = {p: pltpu.roll(x, LANES - 1 if step > 0 else 1, 1) for p, x in tiles.items()}
    inside = lane < LANES - 1 if step > 0 else lane > 0
    shifted = {}
    for block in range(blocks):
        for tile in range(count):
            beyond = tile + step
            other = turned[block, beyond] if 0 <= beyond < count else 0.0
            shifted[block, tile] = jnp.where(inside, turned[block, tile], other)
    return shifted


def reciprocal(value):
    guess = pl.reciprocal(value, approx=True)
    return guess * (2.0 - value * guess)


def redox_sources(masked):
    oxygen, nitrate, nitrite, ammonium, _, carbon, sulfide, nitrous = masked
    over_oxygen = reciprocal(oxygen + HALF_OXYGEN)
    with_oxygen = oxygen * over_oxygen
    no_oxygen = HALF_OXYGEN * over_oxygen
    with_nitrate = no_oxygen * nitrate * reciprocal(nitrate + HALF_NITRATE)
    rest = no_oxygen - with_nitrate
    with_nitrite = rest * nitrite * reciprocal(nitrite + HALF_NITRITE)
    with_sulfate = rest - with_nitrite
    breakdown = RATE_CARBON * carbon
    first_nitr = RATE_AMMONIUM * ammonium * with_oxygen
    second_nitr = RATE_NITRITE * nitrite * with_oxygen
    sulfide_ox = RATE_SULFIDE * sulfide * with_oxygen
    by_nitrate = 0.9 * breakdown * with_nitrate
    return (
        -1.3 * breakdown * with_oxygen - 1.5 * first_nitr - 0.5 * second_nitr - 2.0 * sulfide_ox,
        second_nitr - by_nitrate,
        by_nitrate
        - 0.6 * breakdown * with_nitrite
        + (1.0 - YIELD_NITROUS) * first_nitr
        - second_nitr,
        0.15 * breakdown - first_nitr,
        0.1 * breakdown,
        -breakdown,
        0.5 * breakdown * with_sulfate - sulfide_ox,
        YIELD_NITROUS * first_nitr - RATE_NITROUS * nitrous * no_oxygen,
    )


def source_kernel(first, tracers_ref, depth_ref, _, base_ref, masked_ref):
    kinds, levels, columns, rows = tracers_ref.shape
    places = grid_tiles(columns, rows)

    @pl.loop(0, base_ref.shape[1])
    def _(place):
        level = first + place
        above = jnp.maximum(level - 1, 0)
        below = jnp.minimum(level + 1, levels - 1)
        mix_up_level = jnp.where(level > 0, VERT_DIFF, 0.0)
        for p in places:
            at = tile_index(p)
            depth_here = depth_ref[at]
            wet = jnp.where(level < depth_here, 1.0, 0.0)
            mix_up = wet * mix_up_level
            mix_down = jnp.where(level + 1 < depth_here, VERT_DIFF, 0.0)
            values = [tracers_ref[(kind, level) + at] for kind in range(kinds)]
            masked = [value * wet for value in values]
            sources = redox_sources(masked)
            for kind in range(kinds):
                masked_ref[(kind, place) + at] = masked[kind]
                value = values[kind]
                down = (tracers_ref[(kind, below) + at] - value) * mix_down
                up = (value - tracers_ref[(kind, above) + at]) * mix_up
                base_ref[(kind, place) + at] = value + (sources[kind] + (down - up))


def turn(ref_block, target_ref, start=0):
    rows = ref_block.shape[1]
    for tile in range(rows // LANES):
        part = slice(tile * LANES, (tile + 1) * LANES)
        target_ref[start + part.start : start + part.stop] = ref_block[:, part].T


def shifted(here, other, step):
    sublane = lax.broadcasted_iota(jnp.int32, (SUBLANES, LANES), 0)
    inside = sublane < SUBLANES - step if step > 0 else sublane >= -step
    amount = (SUBLANES - step) % SUBLANES if step > 0 else -step
    other = pltpu.roll(other, amount, 0) if other is not None else 0.0
    return jnp.where(inside, pltpu.roll(here, amount, 0), other)


def row_tile(block):
    return slice(block * SUBLANES, (block + 1) * SUBLANES)


def north_kernel(depth_ref, v_ref, _, *refs):
    masked_ins, refs = refs[:-7], refs[-7:]
    change_ref, face_ref, depth_turned_ref, scale_ref, flow_ref, mix_ref, masked_ref = refs
    kinds, per_layer, columns, rows = masked_ins[0].shape
    layers = len(masked_ins)
    blocks = rows // SUBLANES
    depth = depth_ref[...].astype(jnp.float32)
    turn(jnp.concatenate([depth] * per_layer, axis=0), depth_turned_ref)
    lane_level = lax.broadcasted_iota(jnp.int32, (SUBLANES, LANES), 1) // columns
    for layer in range(layers):
        span = slice(layer * per_layer, (layer + 1) * per_layer)
        turn(v_ref[span].reshape(LANES, rows), flow_ref.at[layer])
        level = (lane_level + layer * per_layer).astype(jnp.float32)
        for block in range(blocks):
            at = row_tile(block)
            here = depth_turned_ref[at]
            after = depth_turned_ref[row_tile(block + 1)] if block + 1 < blocks else None
            is_open = level < jnp.minimum(here, shifted(here, after, 1))
            scale = jnp.where(is_open, 1.0 / 12.0, 0.0)
            scale_ref[layer, at] = scale
            mix_ref[layer, at] = jnp.where(is_open, HORIZ_DIFF, 0.0)
            flow_ref[layer, at] = flow_ref[layer, at] * scale

    @pl.loop(0, kinds)
    def _(kind):
        for layer in range(layers):
            turn(masked_ins[layer][kind].reshape(LANES, rows), masked_ref.at[layer])
            tiles = [masked_ref[layer, row_tile(block)] for block in range(blocks)]
            before = None
            for block in range(blocks):
                at = row_tile(block)
                here = tiles[block]
                after = tiles[block + 1] if block + 1 < blocks else None
                one = shifted(here, after, 1)
                two = shifted(here, after, 2)
                south = shifted(here, tiles[block - 1] if block else None, -1)
                face = 7.0 * (here + one) - (south + two)
                face_ref[kind, layer, at] = face * scale_ref[layer, at]
                flux = face * flow_ref[layer, at] - (one - here) * mix_ref[layer, at]
                change_ref[kind, layer, at] = shifted(flux, before, -1) - flux
                before = flux


def east_kernel(
    layers,
    east_depth_ref,
    u_ref,
    inner_ref,
    outer_ref,
    own_inner_ref,
    own_outer_ref,
    _,
    *refs,
):
    masked_refs, before_refs, refs = refs[:layers], refs[layers : 2 * layers], refs[2 * layers :]
    (
        base_ref,
        face_east_ref,
        face_west_ref,
        flux_west_ref,
        from_west_ref,
        from_east_ref,
        own_west_ref,
    ) = refs
    kinds, levels, columns, rows = base_ref.shape
    per_layer = levels // layers
    blocks, count = columns // SUBLANES, rows // LANES
    places = grid_tiles(columns, rows)
    for place in range(inner_ref.shape[0]):
        from_west_ref[place] = jnp.where(is_even(), outer_ref[place], inner_ref[place])
    for place in range(2 * levels):
        from_east_ref[place] = jnp.where(is_even(), inner_ref[place], outer_ref[place])
        own_west_ref[place] = jnp.where(is_even(), own_outer_ref[place], own_inner_ref[place])
    depth_west = from_west_ref[2 * levels + levels // SUBLANES]
    for z in range(levels):
        row = z % SUBLANES
        u_west = from_west_ref[2 * levels + z // SUBLANES, row : row + 1]
        center, east_one = from_west_ref[2 * z + 1], own_west_ref[2 * z]
        outer = from_west_ref[2 * z] + own_west_ref[2 * z + 1]
        scale_west = jnp.where(z < depth_west, 1.0 / 12.0, 0.0)
        mix_west = jnp.where(z < depth_west, HORIZ_DIFF, 0.0)
        face = (7.0 * (center + east_one) - outer) * scale_west
        for kind in range(kinds):
            face_west_ref[kind, z : z + 1] = face[kind : kind + 1]
        flux_west_ref[z] = u_west * face - mix_west * (east_one - center)

    def one_level(place, layer):
        level = layer * per_layer + place
        masked_ref, before_ref = masked_refs[layer], before_refs[layer]
        scale, mix = {}, {}
        for p in places:
            at = tile_index(p)
            is_open = level < east_depth_ref[at]
            scale[p] = jnp.where(is_open, 1.0 / 12.0, 0.0)
            mix[p] = jnp.where(is_open, HORIZ_DIFF, 0.0)
        for kind in range(kinds):
            def halo(ref, index):
                return [
                    jnp.broadcast_to(
                        ref[index, kind : kind + 1, tile * LANES : (tile + 1) * LANES],
                        (SUBLANES, LANES),
                    )
                    for tile in range(count)
                ]

            masked = {p: masked_ref[(kind, place) + tile_index(p)] for p in places}
            one = shift_columns(masked, 1, halo(from_east_ref, 2 * level), blocks, count)
            two = shift_columns(one, 1, halo(from_east_ref, 2 * level + 1), blocks, count)
            west = shift_columns(masked, -1, halo(from_west_ref, 2 * level + 1), blocks, count)
            flux = {}
            for p in places:
                at = (kind, level) + tile_index(p)
                face = (7.0 * (masked[p] + one[p]) - (west[p] + two[p])) * scale[p]
                face_east_ref[at] = face
                flux[p] = u_ref[(level,) + tile_index(p)] * face - mix[p] * (one[p] - masked[p])
            incoming = shift_columns(flux, -1, halo(flux_west_ref, level), blocks, count)
            for p in places:
                at = (kind, level) + tile_index(p)
                base_ref[at] = before_ref[(kind, place) + tile_index(p)] + (
                    incoming[p] - flux[p]
                )

    for layer in range(layers):
        pl.loop(0, per_layer)(functools.partial(one_level, layer=layer))


def update_kernel(
    kept_ref,
    came_ref,
    basis_ref,
    base_ref,
    face_east_ref,
    face_west_ref,
    change_ref,
    face_north_ref,
    surface_out,
    out_ref,
    weak_ref,
    surface_ref,
    slabs_ref,
    height_ref,
    flow_ref,
    turned_ref,
    result_ref,
    surface_sem,
    sems,
):
    half = lax.rem(lax.axis_index("lon") // 2, 2)
    for source in range(kept_ref.shape[0]):
        for core in range(2):
            slabs_ref[4 * source + 2 * half + core] = kept_ref[source, core]
            slabs_ref[4 * source + 2 * (1 - half) + core] = came_ref[source, core]
    kinds, levels, columns, rows = base_ref.shape
    blocks, count = columns // SUBLANES, rows // LANES
    places = grid_tiles(columns, rows)
    sources, slab_rows, _ = slabs_ref.shape
    band, width = surface_ref.shape
    parts = [slabs_ref[source, columns + 2 : columns + 3] for source in range(sources)]
    while len(parts) > 1:
        parts = [a + b for a, b in zip(parts[::2], parts[1::2])]
    dots = [jnp.broadcast_to(parts[0][:, m : m + 1], (1, LANES)) for m in range(2 * BASIS)]
    weights, weak = basis_weights(
        dots[:2] + [2.0 * dots[m] - dots[m % 2] for m in range(2, 2 * BASIS)]
    )
    weak_ref[...] = jnp.broadcast_to(weak, (SUBLANES, LANES))
    lane_group = lax.broadcasted_iota(jnp.int32, (1, LANES), 1) // band
    lane_weight = jnp.zeros((1, LANES), jnp.float32)
    for k in range(BASIS):
        lane_weight = jnp.where(lane_group == k, weights[k], lane_weight)
    for tile in range(width // LANES):
        part = slice(tile * LANES, (tile + 1) * LANES)
        surface = weights[0] * basis_ref[:band, part]
        for k in range(1, BASIS):
            surface = surface + weights[k] * basis_ref[k * band : (k + 1) * band, part]
        surface_ref[:, part] = surface
    surface_copy = pltpu.make_async_copy(surface_ref, surface_out, surface_sem)
    surface_copy.start()

    fill = LANES // band
    group_full = lax.broadcasted_iota(jnp.int32, (slab_rows, LANES), 1) // band
    height, east_edge, west_edge = {}, [], []
    for tile in range(count):
        joined = None
        for p in range(fill):
            part = slabs_ref[tile * fill + p] * lane_weight
            shift = LANES // 2
            while shift >= band:
                part = part + pltpu.roll(part, shift, 1)
                shift //= 2
            joined = part if joined is None else jnp.where(group_full == p, part, joined)
        for block in range(blocks):
            height[block, tile] = joined[block * SUBLANES : (block + 1) * SUBLANES]
        east_edge.append(jnp.broadcast_to(joined[columns : columns + 1], (SUBLANES, LANES)))
        west_edge.append(
            jnp.broadcast_to(joined[columns + 1 : columns + 2], (SUBLANES, LANES))
        )
    height_east = shift_columns(height, 1, east_edge, blocks, count)
    flow_east = {p: -BARO_GAIN * (height_east[p] - height[p]) for p in places}
    per_layer = LANES // columns
    layers = levels // per_layer
    row_blocks = rows // SUBLANES
    for p in places:
        for repeat in range(per_layer):
            at = tile_index(p)
            start = repeat * columns
            height_ref[start + at[0].start : start + at[0].stop, at[1]] = height[p]
    turn(height_ref, turned_ref)
    for block in range(row_blocks):
        here = turned_ref[row_tile(block)]
        after = turned_ref[row_tile(block + 1)] if block + 1 < row_blocks else None
        flow_ref[row_tile(block)] = -BARO_GAIN * (shifted(here, after, 1) - here)
    flow_west = [
        -BARO_GAIN * (jnp.broadcast_to(height[0, tile][:1], (SUBLANES, LANES)) - west_edge[tile])
        for tile in range(count)
    ]

    def copy(kind, layer):
        span = (kind, pl.ds(layer * per_layer, per_layer))
        return pltpu.make_async_copy(
            result_ref.at[span], out_ref.at[span], sems.at[kind, layer]
        )

    @pl.loop(0, kinds)
    def _(kind):
        for layer in range(layers):
            before = None
            for block in range(row_blocks):
                at = row_tile(block)
                flux = flow_ref[at] * face_north_ref[kind, layer, at]
                turned_ref[at] = change_ref[kind, layer, at] + (shifted(flux, before, -1) - flux)
                before = flux
            for tile in range(count):
                part = slice(tile * LANES, (tile + 1) * LANES)
                along = turned_ref[part].T
                for z in range(per_layer):
                    level = layer * per_layer + z
                    flux_east = {
                        (block, tile): flow_east[block, tile]
                        * face_east_ref[(kind, level) + tile_index((block, tile))]
                        for block in range(blocks)
                    }
                    edge = flow_west[tile] * jnp.broadcast_to(
                        face_west_ref[kind, level : level + 1, part], (SUBLANES, LANES)
                    )
                    for block in range(blocks):
                        at = (kind, level) + tile_index((block, tile))
                        start = z * columns + block * SUBLANES
                        west = flux_east[block - 1, tile] if block else edge
                        flux = flux_east[block, tile]
                        result_ref[at] = base_ref[at] + (
                            (shifted(flux, west, -1) - flux) + along[start : start + SUBLANES]
                        )
            copy(kind, layer).start()

    for kind in range(kinds):
        for layer in range(layers):
            copy(kind, layer).wait()
    surface_copy.wait()


def body(
    surface_old,
    surface_forcing,
    surface_coeff,
    ocean_mask,
    column_depth,
    east_depth,
    tracers,
    u_clinic,
    v_clinic,
):
    given = (
        surface_old,
        surface_forcing,
        surface_coeff,
        ocean_mask,
        column_depth,
        east_depth,
        tracers,
        u_clinic,
        v_clinic,
    )
    band, width = surface_old.shape
    kinds, levels, columns, rows = tracers.shape
    count = lax.axis_size("lon")
    f32 = jnp.float32
    sds = jax.ShapeDtypeStruct
    vmem = pl.BlockSpec(memory_space=pltpu.VMEM)
    hbm = pl.BlockSpec(memory_space=pltpu.HBM)
    fields = (surface_old, surface_forcing, surface_coeff, ocean_mask)
    pairs_inner = [(i, i ^ 1) for i in range(count)]
    ring = [(i, (i + 1 if i % 2 else i - 1) % count) for i in range(count)]
    pairs_outer = [(i, j) for i, j in ring if abs(i - j) == 1]

    def call(
        kernel, out_shape, name, operands, scratch=(), limit=SMALL_VMEM, cost=0, far=()
    ):
        return pl.pallas_call(
            kernel,
            out_shape=out_shape,
            in_specs=[hbm if place in far else vmem for place in range(len(operands))],
            out_specs=[hbm if x is result or x is solved else vmem for x in out_shape],
            scratch_shapes=list(scratch),
            compiler_params=pltpu.CompilerParams(vmem_limit_bytes=limit),
            cost_estimate=pl.CostEstimate(
                flops=cost * tracers.size, bytes_accessed=8 * tracers.size, transcendentals=0
            )
            if cost
            else None,
            name=name,
        )(
            *(
                pltpu.with_memory_space_constraint(x, pltpu.HBM) if place in far else x
                for place, x in enumerate(operands)
            )
        )

    solved, result = sds((band, width), f32), sds(tracers.shape, f32)
    packed = sds((3 * HALO, width), f32)
    held = pltpu.VMEM(tracers.shape, f32)

    inner, outer, own = call(
        pack_kernel,
        (packed, packed, sds((3 * band, width), f32)),
        "pack_edges",
        fields,
        scratch=[pltpu.VMEM(x.shape, x.dtype) for x in fields] + [pltpu.SemaphoreType.DMA((4,))],
        far=range(4),
        cost=2000,
    )
    edges = sds((2 * levels + levels // SUBLANES + 1, kinds, rows), f32)
    own_inner, own_outer = call(
        edge_kernel,
        (edges, edges),
        "pack_tracer_edges",
        (tracers, column_depth, east_depth, u_clinic, outer),
    )
    (folded,) = call(fold_kernel, (packed,), "fold", (outer, own_outer))
    came_inner = lax.ppermute(inner, "lon", pairs_inner)
    came_outer = lax.ppermute(outer, "lon", pairs_outer)

    groups = count // 4
    half_slabs = sds((count // 2, SLAB_ROWS, LANES), f32)
    basis, keep, send = call(
        basis_kernel,
        (sds((BASIS * band, width), f32), half_slabs, half_slabs),
        "solver_basis",
        (own, came_inner, came_outer, folded),
        scratch=[pltpu.VMEM((count, SLAB_ROWS, LANES), f32)],
        cost=2000,
    )
    came = lax.ppermute(send, "lon", pairs_inner)
    sends = call(
        spread_kernel,
        (sds((2, 2, SLAB_ROWS, LANES), f32),) * groups,
        "spread_slabs",
        (keep, came),
    )
    slabs = [sends[0]]
    for step in range(1, groups):
        pairs = [(i, (i + 4 * step) % count) for i in range(count)]
        slabs.append(lax.ppermute(sends[step], "lon", pairs))
    edge_inner = lax.ppermute(own_inner, "lon", pairs_inner)
    edge_outer = lax.ppermute(own_outer, "lon", ring)
    layers = levels * columns // LANES
    part = pltpu.VMEM((kinds, levels // layers, columns, rows), f32)
    bases, masked = [], []
    for layer in range(layers):
        found = call(
            functools.partial(source_kernel, layer * (levels // layers)),
            (part, part),
            f"sources_{layer}",
            (tracers, column_depth, sends[0] if layer else own_inner),
            cost=2000,
        )
        bases.append(found[0])
        masked.append(found[1])
    turned = (kinds, levels * columns // LANES, rows, LANES)
    change, face_north = call(
        north_kernel,
        (pltpu.VMEM(turned, f32), pltpu.VMEM(turned, f32)),
        "north_fluxes",
        (column_depth, v_clinic, sends[0], *masked),
        scratch=[pltpu.VMEM((rows, LANES), f32)] + [pltpu.VMEM(turned[1:], f32)] * 4,
        cost=2000,
    )
    quarter = sds((groups, 2, SLAB_ROWS, LANES), f32)
    keep, send = call(half_kernel, (quarter, quarter), "split_halves", (*slabs, change))
    came = lax.ppermute(send, "lon", [(i, i ^ 2) for i in range(count)])
    base, face_east, face_west = call(
        functools.partial(east_kernel, layers),
        (held, held, pltpu.VMEM((kinds, levels, rows), f32)),
        "east_fluxes",
        (
            east_depth,
            u_clinic,
            edge_inner,
            edge_outer,
            own_inner,
            own_outer,
            keep,
            *masked,
            *bases,
        ),
        scratch=[
            pltpu.VMEM((levels, kinds, rows), f32),
            pltpu.VMEM(edges.shape, f32),
            pltpu.VMEM(edges.shape, f32),
            pltpu.VMEM(edges.shape, f32),
        ],
        cost=2000,
    )
    surface, tracers_new, weak = (
        call(
            update_kernel,
            (solved, result, sds((SUBLANES, LANES), f32)),
            "surface_update",
            (keep, came, basis, base, face_east, face_west, change, face_north),
            scratch=[
                pltpu.VMEM((band, width), f32),
                pltpu.VMEM((count, SLAB_ROWS, LANES), f32),
                pltpu.VMEM((LANES, rows), f32),
                pltpu.VMEM((rows, LANES), f32),
                pltpu.VMEM((rows, LANES), f32),
                pltpu.VMEM(tracers.shape, f32),
                pltpu.SemaphoreType.DMA,
                pltpu.SemaphoreType.DMA((kinds, levels * columns // LANES)),
            ],
            limit=RESULT_VMEM,
        )
    )
    return lax.cond(
        weak[0, 0] > 0.0, lambda: plain_body(*given), lambda: (surface, tracers_new)
    )


def padded_2(block, sides, width, periodic):
    for axis, dim in sides:
        count = lax.axis_size(axis)
        forward = [(i, i + 1) for i in range(count - 1)]
        if periodic:
            forward.append((count - 1, 0))
        backward = [(target, source) for source, target in forward]
        low = lax.ppermute(
            lax.slice_in_dim(block, block.shape[dim] - width, None, axis=dim), axis, forward
        )
        high = lax.ppermute(lax.slice_in_dim(block, 0, width, axis=dim), axis, backward)
        block = jnp.concatenate([low, block, high], axis=dim)
    return block


def apply_operator(values_in, mask_float, coeff):
    masked = mask_float * values_in
    padded = padded_2(masked, (("lon", 0),), 1, False)
    top_device = lax.axis_index("lon") == lax.axis_size("lon") - 1
    folded = jnp.where(top_device, masked[-1:, ::-1], padded[-1:])
    northern = jnp.concatenate([padded[2:-1], folded], axis=0)
    southern = padded[:-2]
    eastern = jnp.roll(masked, -1, axis=1)
    western = jnp.roll(masked, 1, axis=1)
    return (coeff + 4.0 * mask_float) * values_in - mask_float * (
        northern + southern + eastern + western
    )


def squared_total(residual):
    return lax.psum(jnp.sum(residual * residual), "lon")


def plain_solve(right_side, mask_float, coeff):
    solution = jnp.zeros_like(right_side)
    residual = right_side
    direction = right_side
    norm_now = squared_total(residual)
    for sweep in range(SOLVER_ITERS):
        applied = apply_operator(direction, mask_float, coeff)
        curvature = lax.psum(jnp.sum(direction * applied), "lon")
        step_size = norm_now / curvature
        solution = solution + step_size * direction
        residual = residual - step_size * applied
        norm_next = squared_total(residual)
        direction = residual + norm_next / norm_now * direction
        norm_now = norm_next
    return solution


def open_faces(column_depth, east_depth, east_baro, north_baro, u_clinic, v_clinic):
    level_index = lax.broadcasted_iota(jnp.int32, u_clinic.shape, 0)
    wet = (level_index < column_depth[None]).astype(jnp.float32)
    east_open = (level_index < east_depth[None]).astype(jnp.float32)
    north_open = wet * jnp.concatenate([wet[:, :, 1:], jnp.zeros_like(wet[:, :, :1])], axis=2)
    below_open = wet * jnp.concatenate([wet[1:], jnp.zeros_like(wet[:1])], axis=0)
    east_flow = (u_clinic + east_baro[None]) * east_open
    north_flow = (v_clinic + north_baro[None]) * north_open
    return (wet, east_open, north_open, below_open, east_flow, north_flow)


def meridional_vertical(masked, north_flow, north_open, below_open):
    count_rows = masked.shape[-1]
    pad_widths = [(0, 0)] * (masked.ndim - 1) + [(2, 2)]
    padded = jnp.pad(masked, pad_widths)
    south_one = padded[..., 1 : count_rows + 1]
    north_one = padded[..., 3 : count_rows + 3]
    north_two = padded[..., 4 : count_rows + 4]
    face_north = (7.0 * (masked + north_one) - (south_one + north_two)) / 12.0
    flux_north = north_flow * face_north - HORIZ_DIFF * (north_one - masked) * north_open
    flux_south = jnp.concatenate(
        [jnp.zeros_like(flux_north[..., :1]), flux_north[..., :-1]], axis=-1
    )
    below = jnp.concatenate([masked[..., 1:, :, :], jnp.zeros_like(masked[..., :1, :, :])], axis=-3)
    flux_down = VERT_DIFF * (below - masked) * below_open
    flux_up = jnp.concatenate(
        [jnp.zeros_like(flux_down[..., :1, :, :]), flux_down[..., :-1, :, :]], axis=-3
    )
    return flux_south - flux_north + (flux_down - flux_up)


def plain_sources(masked):
    oxygen = masked[0]
    nitrate = masked[1]
    nitrite = masked[2]
    ammonium = masked[3]
    carbon = masked[5]
    sulfide = masked[6]
    nitrous = masked[7]
    breakdown = RATE_CARBON * carbon
    with_oxygen = oxygen / (oxygen + HALF_OXYGEN)
    with_nitrate = (1.0 - with_oxygen) * nitrate / (nitrate + HALF_NITRATE)
    with_nitrite = (1.0 - with_oxygen - with_nitrate) * nitrite / (nitrite + HALF_NITRITE)
    with_sulfate = 1.0 - with_oxygen - with_nitrate - with_nitrite
    first_nitr = RATE_AMMONIUM * ammonium * with_oxygen
    second_nitr = RATE_NITRITE * nitrite * with_oxygen
    sulfide_ox = RATE_SULFIDE * sulfide * with_oxygen
    return jnp.stack(
        [
            -1.3 * breakdown * with_oxygen
            - 1.5 * first_nitr
            - 0.5 * second_nitr
            - 2.0 * sulfide_ox,
            -0.9 * breakdown * with_nitrate + second_nitr,
            0.9 * breakdown * with_nitrate
            - 0.6 * breakdown * with_nitrite
            + (1.0 - YIELD_NITROUS) * first_nitr
            - second_nitr,
            0.15 * breakdown - first_nitr,
            0.1 * breakdown,
            -breakdown,
            0.5 * breakdown * with_sulfate - sulfide_ox,
            YIELD_NITROUS * first_nitr - RATE_NITROUS * nitrous * (1.0 - with_oxygen),
        ]
    )


def plain_body(
    surface_old,
    surface_forcing,
    surface_coeff,
    ocean_mask,
    column_depth,
    east_depth,
    tracers,
    u_clinic,
    v_clinic,
):
    mask_float = ocean_mask.astype(jnp.float32)
    right_side = surface_coeff * surface_old + surface_forcing
    surface = plain_solve(right_side, mask_float, surface_coeff)
    band_flow = -BARO_GAIN * (jnp.roll(surface, -1, axis=1) - surface)
    moved = lax.all_to_all(
        jnp.stack([surface, band_flow]), "lon", split_axis=2, concat_axis=1, tiled=True
    )
    strip_surface = moved[0].T
    east_baro = moved[1].T
    above_surface = jnp.concatenate([strip_surface[:, 1:], strip_surface[:, -1:]], axis=1)
    north_baro = -BARO_GAIN * (above_surface - strip_surface)
    wet, east_open, north_open, below_open, east_flow, north_flow = open_faces(
        column_depth, east_depth, east_baro, north_baro, u_clinic, v_clinic
    )
    masked = tracers * wet[None]
    tracer_count = masked.shape[0]
    columns_here = masked.shape[2]
    stacked = jnp.concatenate([masked, east_flow[None], east_open[None]], axis=0)
    padded = padded_2(stacked, (("lon", 2),), 2, True)
    tracer_pad = padded[:tracer_count]
    west_flow = padded[tracer_count, :, 1:2]
    west_open = padded[tracer_count + 1, :, 1:2]
    flow_all = jnp.concatenate([west_flow, east_flow], axis=1)
    open_all = jnp.concatenate([west_open, east_open], axis=1)
    center = tracer_pad[:, :, 1 : columns_here + 2]
    east_one = tracer_pad[:, :, 2 : columns_here + 3]
    west_one = tracer_pad[:, :, 0 : columns_here + 1]
    east_two = tracer_pad[:, :, 3 : columns_here + 4]
    face_east = (7.0 * (center + east_one) - (west_one + east_two)) / 12.0
    flux_all = flow_all[None] * face_east - HORIZ_DIFF * (east_one - center) * open_all[None]
    conv_east = flux_all[:, :, :-1] - flux_all[:, :, 1:]
    transport = conv_east + meridional_vertical(
        masked, north_flow[None], north_open[None], below_open[None]
    )
    tendency = transport + plain_sources(masked)
    tracers_new = tracers + wet[None] * tendency
    return (surface, tracers_new)


def solution(mesh):
    in_specs = (
        P(("member", "lon"), None),
        P(("member", "lon"), None),
        P("lon", None),
        P("lon", None),
        P("lon", None),
        P("lon", None),
        P("member", None, "lon", None),
        P("member", "lon", None),
        P("member", "lon", None),
    )
    out_specs = (P(("member", "lon"), None), P("member", None, "lon", None))
    return jax.shard_map(body, mesh=mesh, in_specs=in_specs, out_specs=out_specs, check_vma=False)
```

```python
import functools

import jax
import jax.numpy as jnp
from jax import lax
from jax.experimental import pallas as pl
from jax.experimental.pallas import tpu as pltpu
from jax.sharding import PartitionSpec as P

BARO_GAIN = 0.1
HORIZ_DIFF = 0.1
VERT_DIFF = 0.15
RATE_CARBON = 0.3
RATE_AMMONIUM = 0.2
RATE_NITRITE = 0.2
RATE_SULFIDE = 0.3
RATE_NITROUS = 0.2
HALF_OXYGEN = 0.3
HALF_NITRATE = 0.3
HALF_NITRITE = 0.3
YIELD_NITROUS = 0.3


SOLVER_ITERS = 4
SUBLANES = 8
LANES = 128
SMALL_VMEM = 4 * 2**20
RESULT_VMEM = 14 * 2**20
HALO = 8
SLAB_ROWS = 24
BASIS = 4
CENTRE = 4.55
SPREAD = 4.45
PIVOT_FLOOR = 3e-7
PIVOT_LEAST = 0.03


def is_even():
    return lax.rem(lax.axis_index("lon"), 2) == 0


def pack_kernel(old_in, force_in, coeff_in, mask_in, inner_ref, outer_ref, own_ref, *scratch):
    old_ref, force_ref, coeff_ref, mask_ref, sems = scratch
    copies = [
        pltpu.make_async_copy(source, target, sems.at[place])
        for place, (source, target) in enumerate(
            zip((old_in, force_in, coeff_in, mask_in), (old_ref, force_ref, coeff_ref, mask_ref))
        )
    ]
    for copy in copies:
        copy.start()
    for copy in copies:
        copy.wait()
    rows = old_ref.shape[0]
    coeff = coeff_ref[...]
    fields = (
        coeff * old_ref[...] + force_ref[...],
        coeff,
        mask_ref[...].astype(jnp.float32),
    )
    for place, field in enumerate(fields):
        low, high = field[:HALO], field[rows - HALO :]
        part = slice(HALO * place, HALO * (place + 1))
        inner_ref[part] = jnp.where(is_even(), high, low)
        outer_ref[part] = jnp.where(is_even(), low, high)
        own_ref[rows * place : rows * (place + 1)] = field


def basis_kernel(
    own_ref,
    inner_ref,
    outer_ref,
    folded_ref,
    basis_ref,
    keep_ref,
    send_ref,
    slabs_ref,
):
    rows, width = own_ref.shape[0] // 3, own_ref.shape[1]
    count = slabs_ref.shape[0]
    columns = width // count
    top_device = lax.axis_index("lon") == count - 1
    below = jnp.where(is_even(), outer_ref[...], inner_ref[...])
    above = jnp.where(is_even(), inner_ref[...], outer_ref[...])
    above = jnp.where(top_device, folded_ref[...], above)

    def extended(place):
        part = slice(HALO * place, HALO * (place + 1))
        own = own_ref[rows * place : rows * (place + 1)]
        return jnp.concatenate([below[part], own, above[part]], axis=0)

    first, coeff, mask = extended(0), extended(1), extended(2)
    diagonal = (coeff + 4.0 * mask - CENTRE) * (1.0 / SPREAD)
    beside = mask * (1.0 / SPREAD)
    total = rows + 2 * HALO

    def scaled(values):
        masked = mask * values
        around = (
            pltpu.roll(masked, total - 1, 0)
            + pltpu.roll(masked, 1, 0)
            + pltpu.roll(masked, width - 1, 1)
            + pltpu.roll(masked, 1, 1)
        )
        return diagonal * values - beside * around

    vectors = [first, scaled(first)]
    while len(vectors) < BASIS + 1:
        vectors.append(2.0 * scaled(vectors[-1]) - vectors[-2])
    own = [vector[HALO : HALO + rows] for vector in vectors]
    sums = []
    for order in range(2 * BASIS):
        product = own[order // 2] * own[(order + 1) // 2]
        sums.append(jnp.sum(product, axis=0, keepdims=True))
    partial = jnp.sum(jnp.concatenate(sums, axis=0), axis=1, keepdims=True)
    lane = lax.broadcasted_iota(jnp.int32, (2 * BASIS, LANES), 1)
    place = lax.broadcasted_iota(jnp.int32, (2 * BASIS, LANES), 0)
    moments = jnp.sum(jnp.where(lane == place, partial, 0.0), axis=0, keepdims=True)
    stacked = jnp.concatenate(own[:BASIS], axis=0)
    basis_ref[...] = stacked
    if BASIS * rows < LANES:
        stacked = jnp.concatenate(
            [stacked, jnp.zeros((LANES - BASIS * rows, width), jnp.float32)], axis=0
        )
    turned = stacked.T
    for target in range(count):
        start = target * columns
        east = (start + columns) % width
        west = (start - 1) % width
        pieces = [
            turned[start : start + columns],
            turned[east : east + 1],
            turned[west : west + 1],
            moments,
            jnp.zeros((SLAB_ROWS - columns - 3, LANES), jnp.float32),
        ]
        slabs_ref[target] = jnp.concatenate(pieces, axis=0)
    core = lax.rem(lax.axis_index("lon"), 2)
    for pair in range(count // 2):
        keep_ref[pair] = slabs_ref[2 * pair + core]
        send_ref[pair] = slabs_ref[2 * pair + 1 - core]


def spread_kernel(kept_ref, came_ref, *out_refs):
    here = lax.axis_index("lon")
    core, group = lax.rem(here, 2), here // 4
    groups = len(out_refs)
    for step in range(groups):
        target = lax.rem(group + step, groups)
        for y in range(2):
            out_refs[step][y, core] = kept_ref[2 * target + y]
            out_refs[step][y, 1 - core] = came_ref[2 * target + y]


def half_kernel(*refs):
    came_refs, (_, keep_ref, send_ref) = refs[:-3], refs[-3:]
    here = lax.axis_index("lon")
    half, group = lax.rem(here // 2, 2), here // 4
    groups = len(came_refs)
    for step in range(groups):
        source = lax.rem(group + groups - step, groups)
        keep_ref[source] = came_refs[step][half]
        send_ref[source] = came_refs[step][1 - half]


def basis_weights(moments):
    gram = {}

    def inner(i, j):
        key = (i + j, abs(i - j))
        if key not in gram:
            gram[key] = 0.5 * (moments[i + j] + moments[abs(i - j)])
        return gram[key]

    matrix = [[None] * BASIS for _ in range(BASIS)]
    for i in range(BASIS):
        for j in range(i + 1):
            if i == 0:
                image = moments[1]
            elif j == 0:
                image = inner(1, i)
            else:
                image = 0.5 * (inner(i, j + 1) + inner(i, j - 1))
            matrix[i][j] = CENTRE * inner(i, j) + SPREAD * image
    right = [inner(i, 0) for i in range(BASIS)]
    start = [matrix[i][i] for i in range(BASIS)]
    inverse = []
    factors = [[None] * BASIS for _ in range(BASIS)]
    for n in range(BASIS):
        pivot = matrix[n][n]
        inverse.append(jnp.where(pivot > PIVOT_FLOOR * start[n], 1.0 / pivot, 0.0))
        for i in range(n + 1, BASIS):
            factors[i][n] = matrix[i][n] * inverse[n]
        for i in range(n + 1, BASIS):
            for j in range(n + 1, i + 1):
                matrix[i][j] = matrix[i][j] - factors[i][n] * matrix[j][n]
            right[i] = right[i] - factors[i][n] * right[n]
    weights = [None] * BASIS
    for n in reversed(range(BASIS)):
        value = right[n] * inverse[n]
        for i in range(n + 1, BASIS):
            value = value - factors[i][n] * weights[i]
        weights[n] = value
    kept = matrix[0][0] > 0.0
    for n in range(BASIS):
        kept = kept & (matrix[n][n] > PIVOT_LEAST * start[n])
    return weights, jnp.where(kept, 0.0, 1.0)


def reverse_tile(tile):
    for axis, size in ((0, SUBLANES), (1, LANES)):
        place = lax.broadcasted_iota(jnp.int32, (SUBLANES, LANES), axis)
        step = size // 2
        while step:
            tile = jnp.where(
                (place & step) != 0,
                pltpu.roll(tile, step, axis),
                pltpu.roll(tile, size - step, axis),
            )
            step //= 2
    return tile


def fold_kernel(high_ref, _, folded_ref):
    tiles = high_ref.shape[1] // LANES

    @pl.when(lax.axis_index("lon") == lax.axis_size("lon") - 1)
    def _():
        for place in range(3):
            part = slice(HALO * place, HALO * (place + 1))
            for tile in range(tiles):
                other = tiles - 1 - tile
                folded_ref[part, tile * LANES : (tile + 1) * LANES] = reverse_tile(
                    high_ref[part, other * LANES : (other + 1) * LANES]
                )


def edge_kernel(tracers_ref, depth_ref, east_depth_ref, u_ref, _, inner_ref, outer_ref):
    kinds, levels, columns, rows = tracers_ref.shape

    def pack(first, target_ref):
        for side in range(2):
            column = first + side
            for z in range(levels):
                wet = (z < depth_ref[column : column + 1]).astype(jnp.float32)
                for kind in range(kinds):
                    target_ref[2 * z + side, kind : kind + 1] = (
                        tracers_ref[kind, z, column : column + 1] * wet
                    )

    def pack_faces(target_ref):
        for z in range(levels):
            place = 2 * levels + z // SUBLANES
            row = z % SUBLANES
            target_ref[place, row : row + 1] = u_ref[z, columns - 1 :]
        place = 2 * levels + levels // SUBLANES
        target_ref[place] = jnp.broadcast_to(
            east_depth_ref[columns - 1 : columns].astype(jnp.float32), (SUBLANES, rows)
        )

    @pl.when(is_even())
    def _():
        pack(columns - 2, inner_ref)
        pack(0, outer_ref)

    @pl.when(jnp.logical_not(is_even()))
    def _():
        pack(0, inner_ref)
        pack(columns - 2, outer_ref)

    pack_faces(inner_ref)
    pack_faces(outer_ref)


def grid_tiles(columns, rows):
    return [
        (block, tile)
        for block in range(columns // SUBLANES)
        for tile in range(rows // LANES)
    ]


def tile_index(place):
    block, tile = place
    return (
        slice(block * SUBLANES, (block + 1) * SUBLANES),
        slice(tile * LANES, (tile + 1) * LANES),
    )


def shift_columns(tiles, step, outer, blocks, count):
    sublane = lax.broadcasted_iota(jnp.int32, (SUBLANES, LANES), 0)
    turned = {p: pltpu.roll(x, SUBLANES - 1 if step > 0 else 1, 0) for p, x in tiles.items()}
    inside = sublane < SUBLANES - 1 if step > 0 else sublane > 0
    shifted = {}
    for block in range(blocks):
        for tile in range(count):
            beyond = block + step
            other = turned[beyond, tile] if 0 <= beyond < blocks else outer[tile]
            shifted[block, tile] = jnp.where(inside, turned[block, tile], other)
    return shifted


def shift_rows(tiles, step, blocks, count):
    lane = lax.broadcasted_iota(jnp.int32, (SUBLANES, LANES), 1)
    turned = {p: pltpu.roll(x, LANES - 1 if step > 0 else 1, 1) for p, x in tiles.items()}
    inside = lane < LANES - 1 if step > 0 else lane > 0
    shifted = {}
    for block in range(blocks):
        for tile in range(count):
            beyond = tile + step
            other = turned[block, beyond] if 0 <= beyond < count else 0.0
            shifted[block, tile] = jnp.where(inside, turned[block, tile], other)
    return shifted


def reciprocal(value):
    guess = pl.reciprocal(value, approx=True)
    return guess * (2.0 - value * guess)


def redox_sources(masked):
    oxygen, nitrate, nitrite, ammonium, _, carbon, sulfide, nitrous = masked
    over_oxygen = reciprocal(oxygen + HALF_OXYGEN)
    with_oxygen = oxygen * over_oxygen
    no_oxygen = HALF_OXYGEN * over_oxygen
    with_nitrate = no_oxygen * nitrate * reciprocal(nitrate + HALF_NITRATE)
    rest = no_oxygen - with_nitrate
    with_nitrite = rest * nitrite * reciprocal(nitrite + HALF_NITRITE)
    with_sulfate = rest - with_nitrite
    breakdown = RATE_CARBON * carbon
    first_nitr = RATE_AMMONIUM * ammonium * with_oxygen
    second_nitr = RATE_NITRITE * nitrite * with_oxygen
    sulfide_ox = RATE_SULFIDE * sulfide * with_oxygen
    by_nitrate = 0.9 * breakdown * with_nitrate
    return (
        -1.3 * breakdown * with_oxygen - 1.5 * first_nitr - 0.5 * second_nitr - 2.0 * sulfide_ox,
        second_nitr - by_nitrate,
        by_nitrate
        - 0.6 * breakdown * with_nitrite
        + (1.0 - YIELD_NITROUS) * first_nitr
        - second_nitr,
        0.15 * breakdown - first_nitr,
        0.1 * breakdown,
        -breakdown,
        0.5 * breakdown * with_sulfate - sulfide_ox,
        YIELD_NITROUS * first_nitr - RATE_NITROUS * nitrous * no_oxygen,
    )


def source_kernel(first, tracers_ref, depth_ref, _, base_ref, masked_ref):
    kinds, levels, columns, rows = tracers_ref.shape
    places = grid_tiles(columns, rows)

    @pl.loop(0, base_ref.shape[1])
    def _(place):
        level = first + place
        above = jnp.maximum(level - 1, 0)
        below = jnp.minimum(level + 1, levels - 1)
        mix_up_level = jnp.where(level > 0, VERT_DIFF, 0.0)
        for p in places:
            at = tile_index(p)
            depth_here = depth_ref[at]
            wet = jnp.where(level < depth_here, 1.0, 0.0)
            mix_up = wet * mix_up_level
            mix_down = jnp.where(level + 1 < depth_here, VERT_DIFF, 0.0)
            values = [tracers_ref[(kind, level) + at] for kind in range(kinds)]
            masked = [value * wet for value in values]
            sources = redox_sources(masked)
            for kind in range(kinds):
                masked_ref[(kind, place) + at] = masked[kind]
                value = values[kind]
                down = (tracers_ref[(kind, below) + at] - value) * mix_down
                up = (value - tracers_ref[(kind, above) + at]) * mix_up
                base_ref[(kind, place) + at] = value + (sources[kind] + (down - up))


def turn(ref_block, target_ref, start=0):
    rows = ref_block.shape[1]
    for tile in range(rows // LANES):
        part = slice(tile * LANES, (tile + 1) * LANES)
        target_ref[start + part.start : start + part.stop] = ref_block[:, part].T


def shifted(here, other, step):
    sublane = lax.broadcasted_iota(jnp.int32, (SUBLANES, LANES), 0)
    inside = sublane < SUBLANES - step if step > 0 else sublane >= -step
    amount = (SUBLANES - step) % SUBLANES if step > 0 else -step
    other = pltpu.roll(other, amount, 0) if other is not None else 0.0
    return jnp.where(inside, pltpu.roll(here, amount, 0), other)


def row_tile(block):
    return slice(block * SUBLANES, (block + 1) * SUBLANES)


def north_kernel(depth_ref, v_ref, _, *refs):
    masked_ins, refs = refs[:-7], refs[-7:]
    change_ref, face_ref, depth_turned_ref, scale_ref, flow_ref, mix_ref, masked_ref = refs
    kinds, per_layer, columns, rows = masked_ins[0].shape
    layers = len(masked_ins)
    blocks = rows // SUBLANES
    depth = depth_ref[...].astype(jnp.float32)
    turn(jnp.concatenate([depth] * per_layer, axis=0), depth_turned_ref)
    lane_level = lax.broadcasted_iota(jnp.int32, (SUBLANES, LANES), 1) // columns
    for layer in range(layers):
        span = slice(layer * per_layer, (layer + 1) * per_layer)
        turn(v_ref[span].reshape(LANES, rows), flow_ref.at[layer])
        level = (lane_level + layer * per_layer).astype(jnp.float32)
        for block in range(blocks):
            at = row_tile(block)
            here = depth_turned_ref[at]
            after = depth_turned_ref[row_tile(block + 1)] if block + 1 < blocks else None
            is_open = level < jnp.minimum(here, shifted(here, after, 1))
            scale = jnp.where(is_open, 1.0 / 12.0, 0.0)
            scale_ref[layer, at] = scale
            mix_ref[layer, at] = jnp.where(is_open, HORIZ_DIFF, 0.0)
            flow_ref[layer, at] = flow_ref[layer, at] * scale

    @pl.loop(0, kinds)
    def _(kind):
        for layer in range(layers):
            turn(masked_ins[layer][kind].reshape(LANES, rows), masked_ref.at[layer])
            tiles = [masked_ref[layer, row_tile(block)] for block in range(blocks)]
            before = None
            for block in range(blocks):
                at = row_tile(block)
                here = tiles[block]
                after = tiles[block + 1] if block + 1 < blocks else None
                one = shifted(here, after, 1)
                two = shifted(here, after, 2)
                south = shifted(here, tiles[block - 1] if block else None, -1)
                face = 7.0 * (here + one) - (south + two)
                face_ref[kind, layer, at] = face * scale_ref[layer, at]
                flux = face * flow_ref[layer, at] - (one - here) * mix_ref[layer, at]
                change_ref[kind, layer, at] = shifted(flux, before, -1) - flux
                before = flux


def east_kernel(
    layers,
    east_depth_ref,
    u_ref,
    inner_ref,
    outer_ref,
    own_inner_ref,
    own_outer_ref,
    _,
    *refs,
):
    masked_refs, before_refs, refs = refs[:layers], refs[layers : 2 * layers], refs[2 * layers :]
    (
        base_ref,
        face_east_ref,
        face_west_ref,
        flux_west_ref,
        from_west_ref,
        from_east_ref,
        own_west_ref,
    ) = refs
    kinds, levels, columns, rows = base_ref.shape
    per_layer = levels // layers
    blocks, count = columns // SUBLANES, rows // LANES
    places = grid_tiles(columns, rows)
    for place in range(inner_ref.shape[0]):
        from_west_ref[place] = jnp.where(is_even(), outer_ref[place], inner_ref[place])
    for place in range(2 * levels):
        from_east_ref[place] = jnp.where(is_even(), inner_ref[place], outer_ref[place])
        own_west_ref[place] = jnp.where(is_even(), own_outer_ref[place], own_inner_ref[place])
    depth_west = from_west_ref[2 * levels + levels // SUBLANES]
    for z in range(levels):
        row = z % SUBLANES
        u_west = from_west_ref[2 * levels + z // SUBLANES, row : row + 1]
        center, east_one = from_west_ref[2 * z + 1], own_west_ref[2 * z]
        outer = from_west_ref[2 * z] + own_west_ref[2 * z + 1]
        scale_west = jnp.where(z < depth_west, 1.0 / 12.0, 0.0)
        mix_west = jnp.where(z < depth_west, HORIZ_DIFF, 0.0)
        face = (7.0 * (center + east_one) - outer) * scale_west
        for kind in range(kinds):
            face_west_ref[kind, z : z + 1] = face[kind : kind + 1]
        flux_west_ref[z] = u_west * face - mix_west * (east_one - center)

    def one_level(place, layer):
        level = layer * per_layer + place
        masked_ref, before_ref = masked_refs[layer], before_refs[layer]
        scale, mix = {}, {}
        for p in places:
            at = tile_index(p)
            is_open = level < east_depth_ref[at]
            scale[p] = jnp.where(is_open, 1.0 / 12.0, 0.0)
            mix[p] = jnp.where(is_open, HORIZ_DIFF, 0.0)
        for kind in range(kinds):
            def halo(ref, index):
                return [
                    jnp.broadcast_to(
                        ref[index, kind : kind + 1, tile * LANES : (tile + 1) * LANES],
                        (SUBLANES, LANES),
                    )
                    for tile in range(count)
                ]

            masked = {p: masked_ref[(kind, place) + tile_index(p)] for p in places}
            one = shift_columns(masked, 1, halo(from_east_ref, 2 * level), blocks, count)
            two = shift_columns(one, 1, halo(from_east_ref, 2 * level + 1), blocks, count)
            west = shift_columns(masked, -1, halo(from_west_ref, 2 * level + 1), blocks, count)
            flux = {}
            for p in places:
                at = (kind, level) + tile_index(p)
                face = (7.0 * (masked[p] + one[p]) - (west[p] + two[p])) * scale[p]
                face_east_ref[at] = face
                flux[p] = u_ref[(level,) + tile_index(p)] * face - mix[p] * (one[p] - masked[p])
            incoming = shift_columns(flux, -1, halo(flux_west_ref, level), blocks, count)
            for p in places:
                at = (kind, level) + tile_index(p)
                base_ref[at] = before_ref[(kind, place) + tile_index(p)] + (
                    incoming[p] - flux[p]
                )

    for layer in range(layers):
        pl.loop(0, per_layer)(functools.partial(one_level, layer=layer))


def update_kernel(
    kept_ref,
    came_ref,
    basis_ref,
    base_ref,
    face_east_ref,
    face_west_ref,
    change_ref,
    face_north_ref,
    surface_out,
    out_ref,
    weak_ref,
    surface_ref,
    slabs_ref,
    height_ref,
    flow_ref,
    turned_ref,
    result_ref,
    surface_sem,
    sems,
):
    half = lax.rem(lax.axis_index("lon") // 2, 2)
    for source in range(kept_ref.shape[0]):
        for core in range(2):
            slabs_ref[4 * source + 2 * half + core] = kept_ref[source, core]
            slabs_ref[4 * source + 2 * (1 - half) + core] = came_ref[source, core]
    kinds, levels, columns, rows = base_ref.shape
    blocks, count = columns // SUBLANES, rows // LANES
    places = grid_tiles(columns, rows)
    sources, slab_rows, _ = slabs_ref.shape
    band, width = surface_ref.shape
    parts = [slabs_ref[source, columns + 2 : columns + 3] for source in range(sources)]
    while len(parts) > 1:
        parts = [a + b for a, b in zip(parts[::2], parts[1::2])]
    dots = [jnp.broadcast_to(parts[0][:, m : m + 1], (1, LANES)) for m in range(2 * BASIS)]
    weights, weak = basis_weights(
        dots[:2] + [2.0 * dots[m] - dots[m % 2] for m in range(2, 2 * BASIS)]
    )
    weak_ref[...] = weak[:, :1]
    lane_group = lax.broadcasted_iota(jnp.int32, (1, LANES), 1) // band
    lane_weight = jnp.zeros((1, LANES), jnp.float32)
    for k in range(BASIS):
        lane_weight = jnp.where(lane_group == k, weights[k], lane_weight)
    for tile in range(width // LANES):
        part = slice(tile * LANES, (tile + 1) * LANES)
        surface = weights[0] * basis_ref[:band, part]
        for k in range(1, BASIS):
            surface = surface + weights[k] * basis_ref[k * band : (k + 1) * band, part]
        surface_ref[:, part] = surface
    surface_copy = pltpu.make_async_copy(surface_ref, surface_out, surface_sem)
    surface_copy.start()

    fill = LANES // band
    group_full = lax.broadcasted_iota(jnp.int32, (slab_rows, LANES), 1) // band
    height, east_edge, west_edge = {}, [], []
    for tile in range(count):
        joined = None
        for p in range(fill):
            part = slabs_ref[tile * fill + p] * lane_weight
            shift = LANES // 2
            while shift >= band:
                part = part + pltpu.roll(part, shift, 1)
                shift //= 2
            joined = part if joined is None else jnp.where(group_full == p, part, joined)
        for block in range(blocks):
            height[block, tile] = joined[block * SUBLANES : (block + 1) * SUBLANES]
        east_edge.append(jnp.broadcast_to(joined[columns : columns + 1], (SUBLANES, LANES)))
        west_edge.append(
            jnp.broadcast_to(joined[columns + 1 : columns + 2], (SUBLANES, LANES))
        )
    height_east = shift_columns(height, 1, east_edge, blocks, count)
    flow_east = {p: -BARO_GAIN * (height_east[p] - height[p]) for p in places}
    per_layer = LANES // columns
    layers = levels // per_layer
    row_blocks = rows // SUBLANES
    for p in places:
        for repeat in range(per_layer):
            at = tile_index(p)
            start = repeat * columns
            height_ref[start + at[0].start : start + at[0].stop, at[1]] = height[p]
    turn(height_ref, turned_ref)
    for block in range(row_blocks):
        here = turned_ref[row_tile(block)]
        after = turned_ref[row_tile(block + 1)] if block + 1 < row_blocks else None
        flow_ref[row_tile(block)] = -BARO_GAIN * (shifted(here, after, 1) - here)
    flow_west = [
        -BARO_GAIN * (jnp.broadcast_to(height[0, tile][:1], (SUBLANES, LANES)) - west_edge[tile])
        for tile in range(count)
    ]

    def copy(kind, layer):
        span = (kind, pl.ds(layer * per_layer, per_layer))
        return pltpu.make_async_copy(
            result_ref.at[span], out_ref.at[span], sems.at[kind, layer]
        )

    @pl.loop(0, kinds)
    def _(kind):
        for layer in range(layers):
            before = None
            for block in range(row_blocks):
                at = row_tile(block)
                flux = flow_ref[at] * face_north_ref[kind, layer, at]
                turned_ref[at] = change_ref[kind, layer, at] + (shifted(flux, before, -1) - flux)
                before = flux
            for tile in range(count):
                part = slice(tile * LANES, (tile + 1) * LANES)
                along = turned_ref[part].T
                for z in range(per_layer):
                    level = layer * per_layer + z
                    flux_east = {
                        (block, tile): flow_east[block, tile]
                        * face_east_ref[(kind, level) + tile_index((block, tile))]
                        for block in range(blocks)
                    }
                    edge = flow_west[tile] * jnp.broadcast_to(
                        face_west_ref[kind, level : level + 1, part], (SUBLANES, LANES)
                    )
                    for block in range(blocks):
                        at = (kind, level) + tile_index((block, tile))
                        start = z * columns + block * SUBLANES
                        west = flux_east[block - 1, tile] if block else edge
                        flux = flux_east[block, tile]
                        result_ref[at] = base_ref[at] + (
                            (shifted(flux, west, -1) - flux) + along[start : start + SUBLANES]
                        )
            copy(kind, layer).start()

    for kind in range(kinds):
        for layer in range(layers):
            copy(kind, layer).wait()
    surface_copy.wait()


def body(
    surface_old,
    surface_forcing,
    surface_coeff,
    ocean_mask,
    column_depth,
    east_depth,
    tracers,
    u_clinic,
    v_clinic,
):
    given = (
        surface_old,
        surface_forcing,
        surface_coeff,
        ocean_mask,
        column_depth,
        east_depth,
        tracers,
        u_clinic,
        v_clinic,
    )
    band, width = surface_old.shape
    kinds, levels, columns, rows = tracers.shape
    count = lax.axis_size("lon")
    f32 = jnp.float32
    sds = jax.ShapeDtypeStruct
    vmem = pl.BlockSpec(memory_space=pltpu.VMEM)
    hbm = pl.BlockSpec(memory_space=pltpu.HBM)
    fields = (surface_old, surface_forcing, surface_coeff, ocean_mask)
    pairs_inner = [(i, i ^ 1) for i in range(count)]
    ring = [(i, (i + 1 if i % 2 else i - 1) % count) for i in range(count)]
    pairs_outer = [(i, j) for i, j in ring if abs(i - j) == 1]

    def call(
        kernel, out_shape, name, operands, scratch=(), limit=SMALL_VMEM, cost=0, far=()
    ):
        return pl.pallas_call(
            kernel,
            out_shape=out_shape,
            in_specs=[hbm if place in far else vmem for place in range(len(operands))],
            out_specs=[hbm if x is result or x is solved else vmem for x in out_shape],
            scratch_shapes=list(scratch),
            compiler_params=pltpu.CompilerParams(vmem_limit_bytes=limit),
            cost_estimate=pl.CostEstimate(
                flops=cost * tracers.size, bytes_accessed=8 * tracers.size, transcendentals=0
            )
            if cost
            else None,
            name=name,
        )(
            *(
                pltpu.with_memory_space_constraint(x, pltpu.HBM) if place in far else x
                for place, x in enumerate(operands)
            )
        )

    solved, result = sds((band, width), f32), sds(tracers.shape, f32)
    packed = sds((3 * HALO, width), f32)
    held = pltpu.VMEM(tracers.shape, f32)

    inner, outer, own = call(
        pack_kernel,
        (packed, packed, sds((3 * band, width), f32)),
        "pack_edges",
        fields,
        scratch=[pltpu.VMEM(x.shape, x.dtype) for x in fields] + [pltpu.SemaphoreType.DMA((4,))],
        far=range(4),
        cost=2000,
    )
    edges = sds((2 * levels + levels // SUBLANES + 1, kinds, rows), f32)
    own_inner, own_outer = call(
        edge_kernel,
        (edges, edges),
        "pack_tracer_edges",
        (tracers, column_depth, east_depth, u_clinic, outer),
    )
    (folded,) = call(fold_kernel, (packed,), "fold", (outer, own_outer))
    came_inner = lax.ppermute(inner, "lon", pairs_inner)
    came_outer = lax.ppermute(outer, "lon", pairs_outer)

    groups = count // 4
    half_slabs = sds((count // 2, SLAB_ROWS, LANES), f32)
    basis, keep, send = call(
        basis_kernel,
        (sds((BASIS * band, width), f32), half_slabs, half_slabs),
        "solver_basis",
        (own, came_inner, came_outer, folded),
        scratch=[pltpu.VMEM((count, SLAB_ROWS, LANES), f32)],
        cost=2000,
    )
    came = lax.ppermute(send, "lon", pairs_inner)
    sends = call(
        spread_kernel,
        (sds((2, 2, SLAB_ROWS, LANES), f32),) * groups,
        "spread_slabs",
        (keep, came),
    )
    slabs = [sends[0]]
    for step in range(1, groups):
        pairs = [(i, (i + 4 * step) % count) for i in range(count)]
        slabs.append(lax.ppermute(sends[step], "lon", pairs))
    edge_inner = lax.ppermute(own_inner, "lon", pairs_inner)
    edge_outer = lax.ppermute(own_outer, "lon", ring)
    layers = levels * columns // LANES
    part = pltpu.VMEM((kinds, levels // layers, columns, rows), f32)
    bases, masked = [], []
    for layer in range(layers):
        found = call(
            functools.partial(source_kernel, layer * (levels // layers)),
            (part, part),
            f"sources_{layer}",
            (tracers, column_depth, sends[0] if layer else own_inner),
            cost=2000,
        )
        bases.append(found[0])
        masked.append(found[1])
    turned = (kinds, levels * columns // LANES, rows, LANES)
    change, face_north = call(
        north_kernel,
        (pltpu.VMEM(turned, f32), pltpu.VMEM(turned, f32)),
        "north_fluxes",
        (column_depth, v_clinic, sends[0], *masked),
        scratch=[pltpu.VMEM((rows, LANES), f32)] + [pltpu.VMEM(turned[1:], f32)] * 4,
        cost=2000,
    )
    quarter = sds((groups, 2, SLAB_ROWS, LANES), f32)
    keep, send = call(half_kernel, (quarter, quarter), "split_halves", (*slabs, change))
    came = lax.ppermute(send, "lon", [(i, i ^ 2) for i in range(count)])
    base, face_east, face_west = call(
        functools.partial(east_kernel, layers),
        (held, held, pltpu.VMEM((kinds, levels, rows), f32)),
        "east_fluxes",
        (
            east_depth,
            u_clinic,
            edge_inner,
            edge_outer,
            own_inner,
            own_outer,
            keep,
            *masked,
            *bases,
        ),
        scratch=[
            pltpu.VMEM((levels, kinds, rows), f32),
            pltpu.VMEM(edges.shape, f32),
            pltpu.VMEM(edges.shape, f32),
            pltpu.VMEM(edges.shape, f32),
        ],
        cost=2000,
    )
    surface, tracers_new, weak = (
        call(
            update_kernel,
            (solved, result, sds((1, 1), f32)),
            "surface_update",
            (keep, came, basis, base, face_east, face_west, change, face_north),
            scratch=[
                pltpu.VMEM((band, width), f32),
                pltpu.VMEM((count, SLAB_ROWS, LANES), f32),
                pltpu.VMEM((LANES, rows), f32),
                pltpu.VMEM((rows, LANES), f32),
                pltpu.VMEM((rows, LANES), f32),
                pltpu.VMEM(tracers.shape, f32),
                pltpu.SemaphoreType.DMA,
                pltpu.SemaphoreType.DMA((kinds, levels * columns // LANES)),
            ],
            limit=RESULT_VMEM,
        )
    )
    return lax.cond(
        weak.reshape(()) > 0.0, lambda: plain_body(*given), lambda: (surface, tracers_new)
    )


def padded_2(block, sides, width, periodic):
    for axis, dim in sides:
        count = lax.axis_size(axis)
        forward = [(i, i + 1) for i in range(count - 1)]
        if periodic:
            forward.append((count - 1, 0))
        backward = [(target, source) for source, target in forward]
        low = lax.ppermute(
            lax.slice_in_dim(block, block.shape[dim] - width, None, axis=dim), axis, forward
        )
        high = lax.ppermute(lax.slice_in_dim(block, 0, width, axis=dim), axis, backward)
        block = jnp.concatenate([low, block, high], axis=dim)
    return block


def apply_operator(values_in, mask_float, coeff):
    masked = mask_float * values_in
    padded = padded_2(masked, (("lon", 0),), 1, False)
    top_device = lax.axis_index("lon") == lax.axis_size("lon") - 1
    folded = jnp.where(top_device, masked[-1:, ::-1], padded[-1:])
    northern = jnp.concatenate([padded[2:-1], folded], axis=0)
    southern = padded[:-2]
    eastern = jnp.roll(masked, -1, axis=1)
    western = jnp.roll(masked, 1, axis=1)
    return (coeff + 4.0 * mask_float) * values_in - mask_float * (
        northern + southern + eastern + western
    )


def squared_total(residual):
    return lax.psum(jnp.sum(residual * residual), "lon")


def plain_solve(right_side, mask_float, coeff):
    solution = jnp.zeros_like(right_side)
    residual = right_side
    direction = right_side
    norm_now = squared_total(residual)
    for sweep in range(SOLVER_ITERS):
        applied = apply_operator(direction, mask_float, coeff)
        curvature = lax.psum(jnp.sum(direction * applied), "lon")
        step_size = norm_now / curvature
        solution = solution + step_size * direction
        residual = residual - step_size * applied
        norm_next = squared_total(residual)
        direction = residual + norm_next / norm_now * direction
        norm_now = norm_next
    return solution


def open_faces(column_depth, east_depth, east_baro, north_baro, u_clinic, v_clinic):
    level_index = lax.broadcasted_iota(jnp.int32, u_clinic.shape, 0)
    wet = (level_index < column_depth[None]).astype(jnp.float32)
    east_open = (level_index < east_depth[None]).astype(jnp.float32)
    north_open = wet * jnp.concatenate([wet[:, :, 1:], jnp.zeros_like(wet[:, :, :1])], axis=2)
    below_open = wet * jnp.concatenate([wet[1:], jnp.zeros_like(wet[:1])], axis=0)
    east_flow = (u_clinic + east_baro[None]) * east_open
    north_flow = (v_clinic + north_baro[None]) * north_open
    return (wet, east_open, north_open, below_open, east_flow, north_flow)


def meridional_vertical(masked, north_flow, north_open, below_open):
    count_rows = masked.shape[-1]
    pad_widths = [(0, 0)] * (masked.ndim - 1) + [(2, 2)]
    padded = jnp.pad(masked, pad_widths)
    south_one = padded[..., 1 : count_rows + 1]
    north_one = padded[..., 3 : count_rows + 3]
    north_two = padded[..., 4 : count_rows + 4]
    face_north = (7.0 * (masked + north_one) - (south_one + north_two)) / 12.0
    flux_north = north_flow * face_north - HORIZ_DIFF * (north_one - masked) * north_open
    flux_south = jnp.concatenate(
        [jnp.zeros_like(flux_north[..., :1]), flux_north[..., :-1]], axis=-1
    )
    below = jnp.concatenate([masked[..., 1:, :, :], jnp.zeros_like(masked[..., :1, :, :])], axis=-3)
    flux_down = VERT_DIFF * (below - masked) * below_open
    flux_up = jnp.concatenate(
        [jnp.zeros_like(flux_down[..., :1, :, :]), flux_down[..., :-1, :, :]], axis=-3
    )
    return flux_south - flux_north + (flux_down - flux_up)


def plain_sources(masked):
    oxygen = masked[0]
    nitrate = masked[1]
    nitrite = masked[2]
    ammonium = masked[3]
    carbon = masked[5]
    sulfide = masked[6]
    nitrous = masked[7]
    breakdown = RATE_CARBON * carbon
    with_oxygen = oxygen / (oxygen + HALF_OXYGEN)
    with_nitrate = (1.0 - with_oxygen) * nitrate / (nitrate + HALF_NITRATE)
    with_nitrite = (1.0 - with_oxygen - with_nitrate) * nitrite / (nitrite + HALF_NITRITE)
    with_sulfate = 1.0 - with_oxygen - with_nitrate - with_nitrite
    first_nitr = RATE_AMMONIUM * ammonium * with_oxygen
    second_nitr = RATE_NITRITE * nitrite * with_oxygen
    sulfide_ox = RATE_SULFIDE * sulfide * with_oxygen
    return jnp.stack(
        [
            -1.3 * breakdown * with_oxygen
            - 1.5 * first_nitr
            - 0.5 * second_nitr
            - 2.0 * sulfide_ox,
            -0.9 * breakdown * with_nitrate + second_nitr,
            0.9 * breakdown * with_nitrate
            - 0.6 * breakdown * with_nitrite
            + (1.0 - YIELD_NITROUS) * first_nitr
            - second_nitr,
            0.15 * breakdown - first_nitr,
            0.1 * breakdown,
            -breakdown,
            0.5 * breakdown * with_sulfate - sulfide_ox,
            YIELD_NITROUS * first_nitr - RATE_NITROUS * nitrous * (1.0 - with_oxygen),
        ]
    )


def plain_body(
    surface_old,
    surface_forcing,
    surface_coeff,
    ocean_mask,
    column_depth,
    east_depth,
    tracers,
    u_clinic,
    v_clinic,
):
    mask_float = ocean_mask.astype(jnp.float32)
    right_side = surface_coeff * surface_old + surface_forcing
    surface = plain_solve(right_side, mask_float, surface_coeff)
    band_flow = -BARO_GAIN * (jnp.roll(surface, -1, axis=1) - surface)
    moved = lax.all_to_all(
        jnp.stack([surface, band_flow]), "lon", split_axis=2, concat_axis=1, tiled=True
    )
    strip_surface = moved[0].T
    east_baro = moved[1].T
    above_surface = jnp.concatenate([strip_surface[:, 1:], strip_surface[:, -1:]], axis=1)
    north_baro = -BARO_GAIN * (above_surface - strip_surface)
    wet, east_open, north_open, below_open, east_flow, north_flow = open_faces(
        column_depth, east_depth, east_baro, north_baro, u_clinic, v_clinic
    )
    masked = tracers * wet[None]
    tracer_count = masked.shape[0]
    columns_here = masked.shape[2]
    stacked = jnp.concatenate([masked, east_flow[None], east_open[None]], axis=0)
    padded = padded_2(stacked, (("lon", 2),), 2, True)
    tracer_pad = padded[:tracer_count]
    west_flow = padded[tracer_count, :, 1:2]
    west_open = padded[tracer_count + 1, :, 1:2]
    flow_all = jnp.concatenate([west_flow, east_flow], axis=1)
    open_all = jnp.concatenate([west_open, east_open], axis=1)
    center = tracer_pad[:, :, 1 : columns_here + 2]
    east_one = tracer_pad[:, :, 2 : columns_here + 3]
    west_one = tracer_pad[:, :, 0 : columns_here + 1]
    east_two = tracer_pad[:, :, 3 : columns_here + 4]
    face_east = (7.0 * (center + east_one) - (west_one + east_two)) / 12.0
    flux_all = flow_all[None] * face_east - HORIZ_DIFF * (east_one - center) * open_all[None]
    conv_east = flux_all[:, :, :-1] - flux_all[:, :, 1:]
    transport = conv_east + meridional_vertical(
        masked, north_flow[None], north_open[None], below_open[None]
    )
    tendency = transport + plain_sources(masked)
    tracers_new = tracers + wet[None] * tendency
    return (surface, tracers_new)


def solution(mesh):
    in_specs = (
        P(("member", "lon"), None),
        P(("member", "lon"), None),
        P("lon", None),
        P("lon", None),
        P("lon", None),
        P("lon", None),
        P("member", None, "lon", None),
        P("member", "lon", None),
        P("member", "lon", None),
    )
    out_specs = (P(("member", "lon"), None), P("member", None, "lon", None))
    return jax.shard_map(body, mesh=mesh, in_specs=in_specs, out_specs=out_specs, check_vma=False)
```
